32 devices in a mesh: dp: 8 (over y, x, core), mp: 4 (over z).
Axes of the slice: x: 2, y: 2, z: 4, core: 2. Of those that a mesh axis runs over, the one named last changes fastest.
Arguments:
- tokens: bfloat16 [32768, 768], P(('dp', 'mp')), may hold values from -6 to 6
- w_query: bfloat16 [768, 768], P(None, 'mp'), may hold values from -0.3125 to 0.3125
- b_query: float32 [768], P('mp'), may hold values from -3 to 3
- w_key: bfloat16 [768, 768], P(None, 'mp'), may hold values from -0.3125 to 0.3125
- w_value: bfloat16 [768, 768], P(None, 'mp'), may hold values from -0.21875 to 0.21875
- b_value: float32 [768], P('mp'), may hold values from -3 to 3
- w_out: bfloat16 [768, 768], P('mp'), may hold values from -0.875 to 0.875
- b_out: float32 [768], replicated, may hold values from -3 to 3
- norm1_gain: float32 [768], replicated, may hold values from 0.25 to 1.75
- norm1_bias: float32 [768], replicated, may hold values from -3 to 3
- w_up: bfloat16 [768, 3072], P(None, 'mp'), may hold values from -0.21875 to 0.21875
- b_up: bfloat16 [3072], P('mp'), may hold values from -3 to 3
- w_down: bfloat16 [3072, 768], P('mp'), may hold values from -0.109375 to 0.109375
- b_down: float32 [768], replicated, may hold values from -3 to 3
- norm2_gain: float32 [768], replicated, may hold values from 0.25 to 1.75
- norm2_bias: float32 [768], replicated, may hold values from -3 to 3
- key_mask: int32 [8, 4096], P('dp'), may hold values from 0 to 1
- cluster_order: int32 [8, 12, 4096], P('dp', 'mp'), may hold values from 0 to 4095, as said below
- cotangent: bfloat16 [32768, 768], P(('dp', 'mp')), may hold values from -6 to 6
Outputs:
- layer_out: bfloat16 [32768, 768], P(('dp', 'mp'))
- grad_tokens: bfloat16 [32768, 768], P(('dp', 'mp'))
- grad_w_query: float32 [768, 768], P(None, 'mp')
- grad_b_query: float32 [768], P('mp')
- grad_w_key: float32 [768, 768], P(None, 'mp')
- grad_w_value: float32 [768, 768], P(None, 'mp')
- grad_b_value: float32 [768], P('mp')
- grad_w_out: float32 [768, 768], P('mp')
- grad_b_out: float32 [768], replicated
- grad_norm1_gain: float32 [768], replicated
- grad_norm1_bias: float32 [768], replicated
- grad_w_up: float32 [768, 3072], P(None, 'mp')
- grad_b_up: float32 [3072], P('mp')
- grad_w_down: float32 [3072, 768], P('mp')
- grad_b_down: float32 [768], replicated
- grad_norm2_gain: float32 [768], replicated
- grad_norm2_bias: float32 [768], replicated
The draws below stay inside these ranges and needn't reach their ends.
Inputs may be any that keep to these rules, and one draw needn't show every extreme that they name: `cluster_order`: for each sequence and head a permutation of the 4096 positions; that head's cluster c holds the positions at entries c * 128 to (c + 1) * 128 - 1. The positions whose key_mask is 1 stand first, so that they fill the lowest clusters of every head and the remaining clusters hold masked keys only.
All inputs are finite; a program needn't handle non-finite values.
Results may differ from the reference program's by a relative error of at most 0.02.
The reference program's roundings to bfloat16 on the way count: a program that leaves them out, or rounds other values in their place, can miss the bound.
Values may be sent and summed in bfloat16 or wider, within the bound.
A program may use at most 192 MiB of HBM per device.

```python
import jax
import jax.numpy as jnp
from jax import lax

D = 768
H = 12
HD = 64
FF = 3072
C = 128
L = 4096
SEQS = 8
TOKENS = 32768


def shuffled(subkey):
    return jax.random.permutation(subkey, L).astype(jnp.int32)


def live_layout(key):
    count_key, place_key = jax.random.split(jax.random.fold_in(key, 11))
    live_counts = jax.random.randint(count_key, (SEQS, 1), L // 8, 3 * L // 8 + 1).astype(jnp.int32)
    position_rank = jax.vmap(shuffled)(jax.random.split(place_key, SEQS))
    return (position_rank < live_counts).astype(jnp.int32)


def draw_key_mask(key, part):
    return live_layout(key)


def draw_cluster_order(key, part):
    live_flags = live_layout(key)
    key = jax.random.fold_in(key, 5)
    shuffles = jax.vmap(shuffled)(jax.random.split(key, SEQS * H)).reshape(SEQS, H, L)
    sort_keys = jnp.where(live_flags[:, None, :] == 1, shuffles, shuffles + L)
    return jnp.argsort(sort_keys, axis=-1).astype(jnp.int32)


def block_levels(rng, dims, pieces, low, high):
    gain = 1.0
    for dim, parts in pieces:
        heights = jax.random.uniform(jax.random.fold_in(jax.random.fold_in(rng, 6), dim), (parts,), jnp.float32, low / len(pieces), high / len(pieces))
        gain = gain * jnp.repeat(jnp.exp(heights), dims[dim] // parts).reshape((-1,) + (1,) * (len(dims) - 1 - dim))
    return gain


def scatter_about(rng, dims, spread, reach, shards=(), dtype=jnp.bfloat16):
    level = block_levels(rng, dims, shards, -0.22, 0.18) if shards else 1.0
    drawn = jax.random.normal(rng, dims, jnp.float32) * spread * level
    return jnp.minimum(jnp.maximum(drawn, -reach), reach).astype(dtype)


def setup_inputs(seed: int = 0) -> dict:
    key_list = jax.random.split(jax.random.key(seed), 20)
    return {
        "tokens": scatter_about(key_list[0], (TOKENS, D), 1.0, 6.0, ((0, 32),)),
        "w_query": scatter_about(key_list[1], (D, H * HD), (D // 2) ** -0.5, 0.3125, ((1, 4),)),
        "b_query": scatter_about(key_list[2], (H * HD,), 0.5, 3.0, ((0, 4),), jnp.float32),
        "w_key": scatter_about(key_list[3], (D, H * HD), (D // 2) ** -0.5, 0.3125, ((1, 4),)),
        "w_value": scatter_about(key_list[4], (D, H * HD), D ** -0.5, 0.21875, ((1, 4),)),
        "b_value": scatter_about(key_list[5], (H * HD,), 0.5, 3.0, ((0, 4),), jnp.float32),
        "w_out": scatter_about(key_list[6], (H * HD, D), (H * HD // 16) ** -0.5, 0.875, ((0, 4),)),
        "b_out": scatter_about(key_list[7], (D,), 0.5, 3.0, (), jnp.float32),
        "norm1_gain": jnp.clip(1.0 + 0.15 * jax.random.normal(key_list[8], (D,), jnp.float32), 0.25, 1.75),
        "norm1_bias": scatter_about(key_list[9], (D,), 0.5, 3.0, (), jnp.float32),
        "w_up": scatter_about(key_list[10], (D, FF), D ** -0.5, 0.21875, ((1, 4),)),
        "b_up": scatter_about(key_list[11], (FF,), 0.5, 3.0, ((0, 4),)),
        "w_down": scatter_about(key_list[12], (FF, D), FF ** -0.5, 0.109375, ((0, 4),)),
        "b_down": scatter_about(key_list[13], (D,), 0.5, 3.0, (), jnp.float32),
        "norm2_gain": jnp.clip(1.0 + 0.15 * jax.random.normal(key_list[14], (D,), jnp.float32), 0.25, 1.75),
        "norm2_bias": scatter_about(key_list[15], (D,), 0.5, 3.0, (), jnp.float32),
        "key_mask": draw_key_mask(jax.random.fold_in(key_list[19], 71), 0),
        "cluster_order": draw_cluster_order(jax.random.fold_in(key_list[19], 71), 0),
        "cotangent": scatter_about(key_list[18], (TOKENS, D), 1.0, 6.0, ((0, 32),)),
    }


EPS = 1e-12

@jax.custom_vjp
def low(v):
    return lax.optimization_barrier(v.astype(jnp.bfloat16)).astype(jnp.float32)

@jax.custom_vjp
def low_back(v):
    return v

def low_keep(v):
    return (low(v), None)

def low_pass(kept, grad):
    return (grad,)

def back_keep(v):
    return (v, None)

def back_low(kept, grad):
    return (low(grad),)
low.defvjp(low_keep, low_pass)
low_back.defvjp(back_keep, back_low)

def matmul(left, right):
    return jnp.dot(left, right, precision=lax.Precision.HIGHEST, preferred_element_type=jnp.float32)

def layer_norm(hidden, norm_gain, norm_bias):
    average = lax.optimization_barrier(jnp.mean(hidden, axis=-1, keepdims=True))
    centred = hidden - average
    variance = lax.optimization_barrier(jnp.mean(centred * centred, axis=-1, keepdims=True))
    return centred * lax.rsqrt(variance + EPS) * norm_gain + norm_bias

def rounded(value):
    return low(low_back(value))

def sequence(params, inputs, key_mask, cluster_order):
    w_query, b_query, w_key, w_value, b_value, w_out, b_out, norm1_gain, norm1_bias, w_up, b_up, w_down, b_down, norm2_gain, norm2_bias = params
    queries = rounded(matmul(inputs, w_query) + b_query)
    key_rows = rounded(matmul(inputs, w_key))
    value_rows = rounded(matmul(inputs, w_value) + b_value)
    positions = cluster_order.astype(jnp.int32)
    inverse = jnp.argsort(positions, axis=-1).astype(jnp.int32)

    def sorted_blocks(matrix):
        per_head = matrix.reshape(L, H, HD).transpose(1, 0, 2)
        return jnp.take_along_axis(per_head, positions[:, :, None], axis=1).reshape(H, L // C, C, HD)
    key_keep = jnp.take_along_axis(jnp.broadcast_to(key_mask[None, :], (H, L)), positions, axis=1)
    penalty = (key_keep.astype(jnp.float32) - 1.0).reshape(H, L // C, 1, C) * 10000.0
    scores = jnp.einsum('hncd,hnkd->hnck', sorted_blocks(queries), sorted_blocks(key_rows), precision=lax.Precision.HIGHEST) * 0.125 + penalty
    scores = low_back(scores)
    attn_probs = low(jax.nn.softmax(scores, axis=-1))
    blocks = jnp.einsum('hnck,hnkd->hncd', attn_probs, sorted_blocks(value_rows), precision=lax.Precision.HIGHEST).reshape(H, L, HD)
    context = jnp.take_along_axis(blocks, inverse[:, :, None], axis=1).transpose(1, 0, 2).reshape(L, H * HD)
    context = rounded(context)
    attended = low_back(matmul(context, w_out))
    first_norm = layer_norm(inputs + attended + b_out, norm1_gain, norm1_bias)
    pre_act = low_back(matmul(low(first_norm), w_up) + b_up)
    ffn_out = low_back(matmul(low(jax.nn.gelu(pre_act, approximate=False)), w_down))
    return layer_norm(first_norm + ffn_out + b_down, norm2_gain, norm2_bias)

def reference(tokens, w_query, b_query, w_key, w_value, b_value, w_out, b_out, norm1_gain, norm1_bias, w_up, b_up, w_down, b_down, norm2_gain, norm2_bias, key_mask, cluster_order, cotangent):
    params = tuple((array.astype(jnp.float32) for array in (w_query, b_query, w_key, w_value, b_value, w_out, b_out, norm1_gain, norm1_bias, w_up, b_up, w_down, b_down, norm2_gain, norm2_bias)))
    inputs = tokens.astype(jnp.float32).reshape(SEQS, L, D)

    def entire(params, inputs):

        def one_record(record):
            return jax.checkpoint(sequence)(params, record[0], record[1], record[2])
        return lax.map(one_record, (inputs, key_mask, cluster_order))
    outputs, pull = jax.vjp(entire, params, inputs)
    grads, grad_in = pull(cotangent.astype(jnp.float32).reshape(SEQS, L, D))
    return (outputs.reshape(TOKENS, D).astype(jnp.bfloat16), grad_in.reshape(TOKENS, D).astype(jnp.bfloat16), grads[0], grads[1], grads[2], grads[3], grads[4], grads[5], grads[6], grads[7], grads[8], grads[9], grads[10], grads[11], grads[12], grads[13], grads[14])
```

```python
import functools
import jax
import jax.numpy as jnp
from jax import lax
from jax.experimental import pallas as pl
from jax.experimental.pallas import tpu as pltpu
from jax.sharding import PartitionSpec as P

L = 4096
C = 128
HD = 64
F32 = jnp.float32
BF16 = jnp.bfloat16
VMEM = pltpu.VMEM


def dot(a, b, da, db):
    return lax.dot_general(a, b, (((da,), (db,)), ((), ())), preferred_element_type=F32)


def attend_kernel(first, ord_ref, qkv_ref, c_ref, ts_ref, pr_ref, src, ctx, buf_a, buf_b, out_a, out_b):
    head = pl.program_id(0) + first
    live = ord_ref[3 * L]
    base = head * L

    src[:, 0, :] = qkv_ref[0, :, :C].astype(F32)
    src[:, 1, :] = qkv_ref[0, :, C:].astype(F32)

    def gather(cluster, buf):
        start = base + cluster * C
        for u in range(C):
            buf[u] = src[ord_ref[start + u]]

    def compute(cluster, buf, out):
        rows = pl.ds(pl.multiple_of(cluster * C, C), C)
        t0 = buf[:, 0, :].astype(BF16)
        t1 = buf[:, 1, :].astype(BF16)
        ts_ref[0, rows, :C] = t0
        ts_ref[0, rows, C:] = t1
        slot = cluster * C + lax.broadcasted_iota(jnp.int32, (1, C), 1)
        penalty = jnp.where(slot < live, 0.0, -10000.0)
        scores = dot(t0, t1, 1, 1) * 0.125 + penalty
        peak = jnp.max(scores, axis=-1, keepdims=True)
        e = jnp.exp(scores - peak)
        probs = e * (1.0 / jnp.sum(e, axis=-1, keepdims=True))
        pr_ref[0, rows, :] = probs
        out[...] = jnp.dot(probs.astype(BF16), t0, preferred_element_type=F32)

    def scatter(cluster, out):
        start = base + cluster * C
        for u in range(C):
            ctx[pl.ds(ord_ref[start + u], 1), :] = out[pl.ds(u, 1), :]

    last = L // C - 1
    gather(0, buf_a)

    def pair(i, _):
        gather(2 * i + 1, buf_b)
        compute(2 * i, buf_a, out_a)
        scatter(jnp.maximum(2 * i - 1, 0), out_b)
        gather(jnp.minimum(2 * i + 2, last), buf_a)
        compute(2 * i + 1, buf_b, out_b)
        scatter(2 * i, out_a)
        return 0

    lax.fori_loop(0, L // C // 2, pair, 0)
    scatter(last, out_b)

    lane = lax.broadcasted_iota(jnp.int32, (1, C), 1)
    if first == 2:
        for k in range(4):
            low = ctx[pl.ds(k * 1024, 512), :]
            high = pltpu.roll(ctx[pl.ds(k * 1024 + 512, 512), :], HD, 1)
            c_ref[pl.ds(k * 512, 512), :] = jnp.where(lane < HD, low, high).astype(BF16)
    else:

        @pl.when(head == 0)
        def _():
            c_ref[...] = ctx[...].astype(BF16)

        @pl.when(head == 1)
        def _():
            c_ref[...] = jnp.where(lane < HD, c_ref[...], ctx[...].astype(BF16))


def attend(first, order, qkv):
    heads = 2 if first == 0 else 1
    whole = lambda shape: pl.BlockSpec(shape, lambda h: (0,) * len(shape), pipeline_mode=pl.Buffered(1))
    in_head = lambda shape: pl.BlockSpec((1,) + shape, lambda h: (h + first, 0, 0))
    per_head = lambda shape: pl.BlockSpec((1,) + shape, lambda h: (h, 0, 0))
    out_rows = L if first == 0 else L // 2
    return pl.pallas_call(
        functools.partial(attend_kernel, first),
        grid=(heads,),
        in_specs=[pl.BlockSpec(memory_space=pltpu.SMEM), in_head((L, 2 * C))],
        out_specs=[whole((out_rows, C)), per_head((L, 2 * C)), per_head((L, C))],
        out_shape=[
            jax.ShapeDtypeStruct((out_rows, C), BF16),
            jax.ShapeDtypeStruct((heads, L, 2 * C), BF16),
            jax.ShapeDtypeStruct((heads, L, C), F32),
        ],
        scratch_shapes=[
            VMEM((L, 2, C), F32), VMEM((L, C), F32),
            VMEM((C, 2, C), F32), VMEM((C, 2, C), F32), VMEM((C, C), F32), VMEM((C, C), F32),
        ],
        compiler_params=pltpu.CompilerParams(vmem_limit_bytes=56 << 20),
        cost_estimate=pl.CostEstimate(flops=heads * 18 * 10**9, bytes_accessed=10 << 20, transcendentals=0),
        name="attend",
    )(order, qkv)


def attend_back_kernel(head, ord_ref, g_ref, ts_ref, pr_ref, d_ref, gsrc, dst, buf_a, buf_b, out_a, out_b):
    base = head * L
    lane = lax.broadcasted_iota(jnp.int32, (1, C), 1)
    if head == 2:
        for k in range(4):
            both = g_ref[pl.ds(k * 512, 512), :].astype(F32)
            gsrc[pl.ds(k * 1024, 512), :] = both
            gsrc[pl.ds(k * 1024 + 512, 512), :] = pltpu.roll(both, HD, 1)
    else:
        gsrc[...] = g_ref[...].astype(F32)

    keep = (lane >= HD) if head == 1 else (lane < HD)

    def gather(cluster, buf):
        start = base + cluster * C
        for u in range(C):
            buf[pl.ds(u, 1), :] = gsrc[pl.ds(ord_ref[start + u], 1), :]

    def compute(cluster, buf, out):
        rows = pl.ds(pl.multiple_of(cluster * C, C), C)
        t0 = ts_ref[0, rows, :C]
        t1 = ts_ref[0, rows, C:]
        probs = pr_ref[0, rows, :]
        g = jnp.where(keep, buf[...], 0.0).astype(BF16)
        dp = dot(g, t0, 1, 1)
        row = jnp.sum(probs * dp, axis=-1, keepdims=True)
        ds = (probs * (dp - row)).astype(BF16)
        out[:, 0, :] = jnp.dot(ds, t1, preferred_element_type=F32) * 0.125 + dot(probs.astype(BF16), g, 0, 0)
        out[:, 1, :] = dot(ds, t0, 0, 0) * 0.125

    def scatter(cluster, out):
        start = base + cluster * C
        for u in range(C):
            dst[ord_ref[start + u]] = out[u]

    last = L // C - 1
    gather(0, buf_a)

    def pair(i, _):
        gather(2 * i + 1, buf_b)
        compute(2 * i, buf_a, out_a)
        scatter(jnp.maximum(2 * i - 1, 0), out_b)
        gather(jnp.minimum(2 * i + 2, last), buf_a)
        compute(2 * i + 1, buf_b, out_b)
        scatter(2 * i, out_a)
        return 0

    lax.fori_loop(0, L // C // 2, pair, 0)
    scatter(last, out_b)

    d_ref[:, :C] = dst[:, 0, :].astype(BF16)
    d_ref[:, C:] = dst[:, 1, :].astype(BF16)


def attend_back(head, order, g, ts, probs):
    i = head % 2
    vm = pl.BlockSpec(memory_space=pltpu.VMEM)
    one = lambda shape: pl.BlockSpec((1,) + shape, lambda h: (i, 0, 0), pipeline_mode=pl.Buffered(1))
    return pl.pallas_call(
        functools.partial(attend_back_kernel, head),
        grid=(1,),
        in_specs=[pl.BlockSpec(memory_space=pltpu.SMEM), vm, one((L, 2 * C)), one((L, C))],
        out_specs=vm,
        out_shape=jax.ShapeDtypeStruct((L, 2 * C), BF16),
        scratch_shapes=[
            VMEM((L, C), F32), VMEM((L, 2, C), F32),
            VMEM((C, C), F32), VMEM((C, C), F32), VMEM((C, 2, C), F32), VMEM((C, 2, C), F32),
        ],
        compiler_params=pltpu.CompilerParams(vmem_limit_bytes=40 << 20),
        cost_estimate=pl.CostEstimate(flops=24 * 10**9, bytes_accessed=10 << 20, transcendentals=0),
        name="attend_back",
    )(order, g, ts, probs)


MESH = pl.DeviceIdType.MESH
WIDTH = 768
ROWS = 1024
SUB = 512
SUBS = ROWS // SUB
SHARE = 224
PACK = 8 * SHARE
OUT_ROW = 1536
BIAS_ROW = 1728
QUARTER = 192
ORDER = 3 * L + 128
DMA = pltpu.SemaphoreType.DMA
ANY = pl.BlockSpec(memory_space=pl.ANY)
VM = pl.BlockSpec(memory_space=pltpu.VMEM)
sds = jax.ShapeDtypeStruct


def place():
    dp, mp = lax.axis_index("dp"), lax.axis_index("mp")
    core = lax.rem(dp, 2)
    return dp, mp, core, jnp.where(core == 0, mp, 3 - mp)


def at(dp, mp):
    return {"dp": dp, "mp": mp}


def signal(barrier, device):
    pl.semaphore_signal(barrier, inc=1, device_id=device, device_id_type=MESH)


def send(src, dst, send_sem, recv_sem, device):
    copy = pltpu.make_async_remote_copy(
        src_ref=src, dst_ref=dst, send_sem=send_sem, recv_sem=recv_sem, device_id=device, device_id_type=MESH
    )
    copy.start()
    return copy


def wait(ref, sem):
    pltpu.make_async_copy(ref, ref, sem).wait()


def mate(dp, rel):
    return dp + 2 * ((lax.rem(dp, 8) // 2 ^ rel) - lax.rem(dp, 8) // 2)


def greet(barrier, both_cores):
    dp, mp, core, t = place()
    step = 1 - 2 * core
    for k in range(4):
        if k:
            signal(barrier, at(dp, lax.rem(mp + k, 4)))
        signal(barrier, at(dp + step, lax.rem(mp + k, 4)))
    for rel in (1, 2, 3):
        signal(barrier, at(mate(dp, rel), mp))
        if both_cores:
            signal(barrier, at(mate(dp, rel) + step, mp))
    pl.semaphore_wait(barrier, 13 if both_cores else 10)


def worker(group, half, dp_base):
    return at(dp_base + group % 2, 2 * half + group // 2)


def chain_device(u, half, dp_base):
    return at(dp_base + half, jnp.where(half == 0, u, 3 - u))


def collect_kernel(x_ref, wsrc_ref, bsrc_ref, osrc_ref, up_ref, down_ref, wout_ref, extra_ref, xs_ref, qkv_ref, w_ref, ord_ref, share_ref,
                   xs, qkv, w, bias, relay,
                   chain_recv, relay_recv, pair_recv, chain_send, relay_send, pair_send, own_sem,
                   wz_recv, wz_send, wp_recv, wp_send, b_recv, b_send, o_recv, o_send, xs_out, qkv_out, w_out, share_sem):
    dp, mp, core, t = place()
    base, half, spot = dp - core, mp // 2, lax.rem(dp, 8) // 2
    step = 1 - 2 * core
    partner, lower, upper = at(dp + step, mp), at(dp, mp - step), at(dp, mp + step)
    group = lax.rem(mp, 2) * 2 + core
    gives = core == lax.rem(mp, 2)
    order_self = worker(mp, core, base)
    order_here = (order_self["dp"] == dp) & (order_self["mp"] == mp)
    cut = lambda s: pl.ds(s * SUB, SUB)
    home = lambda u, s: xs.at[pl.ds(pl.multiple_of(u * ROWS + s * SUB, SUB), SUB)]
    quarter = lambda q: pl.ds(pl.multiple_of(q * QUARTER, QUARTER), QUARTER)

    own = pltpu.make_async_copy(x_ref, xs.at[pl.ds(pl.multiple_of(jnp.minimum(t, 1) * ROWS, ROWS), ROWS)], own_sem)

    @pl.when(t <= 1)
    def _():
        own.start()

    greet(pltpu.get_barrier_semaphore(), False)

    for far in (0, 1):
        target = mp // 2 + 2 * far

        @pl.when(gives & (target != mp))
        def _():
            send(wsrc_ref.at[quarter(spot)], w.at[quarter(spot)], wz_send.at[far], wz_recv, at(dp, target))
            send(bsrc_ref, bias, b_send.at[far], b_recv, at(dp, target))

        @pl.when(gives & (target == mp))
        def _():
            pltpu.make_async_copy(wsrc_ref.at[quarter(spot)], w.at[quarter(spot)], wz_recv).start()
            pltpu.make_async_copy(bsrc_ref, bias, b_recv).start()

    @pl.when(order_here)
    def _():
        pltpu.make_async_copy(osrc_ref, ord_ref, o_recv).start()

    @pl.when(jnp.logical_not(order_here))
    def _():
        send(osrc_ref, ord_ref, o_send, o_recv, order_self)

    @pl.when(t == 3)
    def _():
        for s in range(SUBS):
            send(x_ref.at[cut(s)], relay.at[cut(s)], chain_send.at[0, s], relay_recv.at[s], lower)

    @pl.when((t == 1) | (t == 2))
    def _():
        for s in range(SUBS):
            send(x_ref.at[cut(s)], home(t, s), chain_send.at[0, s], chain_recv.at[t, s], lower)

    @pl.when(t == 0)
    def _():
        for s in range(SUBS):
            send(x_ref.at[cut(s)], home(0, s), chain_send.at[0, s], chain_recv.at[0, s], upper)

    pack = ((0, up_ref), (768, down_ref), (OUT_ROW, wout_ref), (BIAS_ROW, extra_ref))
    for i in range(8):
        @pl.when(lax.rem(dp, 8) == i)
        def _():
            for first, part in pack:
                low, high = max(first, i * SHARE), min(first + part.shape[0], (i + 1) * SHARE)
                if low < high:
                    src = part.at[pl.ds(low - first, high - low)]
                    pltpu.make_async_copy(src, share_ref.at[pl.ds(low - i * SHARE, high - low)], share_sem).start()

    wait(w.at[quarter(spot)], wz_recv)
    for rel in (1, 2, 3):
        send(w.at[quarter(spot)], w.at[quarter(spot)], wp_send.at[rel], wp_recv.at[rel], at(mate(dp, rel), mp))

    @pl.when(t <= 1)
    def _():
        own.wait()
        for s in range(SUBS):
            send(home(t, s), home(t, s), pair_send.at[t, s], pair_recv.at[t, s], partner)

    tt = jnp.minimum(t, 3 - t)

    def rows_of(i, s):
        return pl.ds(pl.multiple_of(lax.rem(tt + i, 4) * ROWS + s * SUB, SUB), SUB)

    def receive(i, s):
        u = lax.rem(tt + i, 4)
        if i == 1:
            @pl.when(t == 2)
            def _():
                wait(relay.at[cut(s)], relay_recv.at[s])
                send(relay.at[cut(s)], home(3, s), relay_send.at[s], chain_recv.at[3, s], lower)

        if i > 0:
            @pl.when(t <= 1)
            def _():
                wait(home(u, s), chain_recv.at[u, s])
                if i < 3:
                    @pl.when(t == 1)
                    def _():
                        send(home(u, s), home(u, s), chain_send.at[i, s], chain_recv.at[u, s], lower)
                send(home(u, s), home(u, s), pair_send.at[u, s], pair_recv.at[u, s], partner)

        @pl.when(t >= 2)
        def _():
            wait(home(u, s), pair_recv.at[u, s])

        rows = rows_of(i, s)
        pltpu.make_async_copy(xs.at[rows], xs_ref.at[rows], xs_out.at[i, s]).start()

    def project(i, s):
        rows = rows_of(i, s)
        row = jnp.concatenate([bias[pl.ds(h, 1), :] for h in range(3)], axis=1)
        qkv[rows, :] = (dot(xs[rows, :], w[...], 1, 1) + row).astype(BF16)
        for h in range(3):
            pltpu.make_async_copy(qkv.at[rows, pl.ds(h * 256, 256)], qkv_ref.at[h, rows], qkv_out.at[i, s, h]).start()

    pieces = [(i, s) for i in range(4) for s in range(SUBS)]
    for i, s in pieces[:4]:
        receive(i, s)
    for rel in (1, 2, 3):
        wait(w.at[quarter(spot ^ rel)], wp_recv.at[rel])
    wait(bias, b_recv)
    pltpu.make_async_copy(w, w_ref, w_out).start()
    for i, s in pieces[:3]:
        project(i, s)
    for k in range(4, len(pieces)):
        receive(*pieces[k])
        project(*pieces[k - 1])
    project(*pieces[-1])

    for i in range(4):
        u = lax.rem(tt + i, 4)
        for s in range(SUBS):
            rows = pl.ds(pl.multiple_of(u * ROWS + s * SUB, SUB), SUB)
            wait(xs.at[rows], xs_out.at[i, s])
            for h in range(3):
                wait(qkv_ref.at[h, rows], qkv_out.at[i, s, h])

            @pl.when(t <= 1)
            def _():
                wait(home(u, s), pair_send.at[u, s])
    for s in range(SUBS):
        wait(x_ref.at[cut(s)], chain_send.at[0, s])

        @pl.when(t == 1)
        def _():
            wait(x_ref.at[cut(s)], chain_send.at[1, s])
            wait(x_ref.at[cut(s)], chain_send.at[2, s])

        @pl.when(t == 2)
        def _():
            wait(relay.at[cut(s)], relay_send.at[s])
    for rel in (1, 2, 3):
        wait(w.at[quarter(spot)], wp_send.at[rel])
    for far in (0, 1):
        @pl.when(gives & (mp // 2 + 2 * far != mp))
        def _():
            wait(wsrc_ref.at[quarter(spot)], wz_send.at[far])
            wait(bsrc_ref, b_send.at[far])
    wait(ord_ref, o_recv)

    @pl.when(jnp.logical_not(order_here))
    def _():
        wait(osrc_ref, o_send)

    wait(w, w_out)
    wait(share_ref, share_sem)


def collect(x, w, b, order, up, down, out, extra):
    return pl.pallas_call(
        collect_kernel,
        out_shape=[sds((4 * ROWS, WIDTH), BF16), sds((3, 4 * ROWS, 256), BF16), sds((WIDTH, WIDTH), BF16), sds((ORDER,), jnp.int32), sds((SHARE, WIDTH), BF16)],
        in_specs=[ANY] * 8,
        out_specs=[ANY] * 5,
        scratch_shapes=[
            VMEM((4 * ROWS, WIDTH), BF16), VMEM((4 * ROWS, WIDTH), BF16), VMEM((WIDTH, WIDTH), BF16), VMEM((8, 256), F32),
            VMEM((ROWS, WIDTH), BF16),
            DMA((4, SUBS)), DMA((SUBS,)), DMA((4, SUBS)), DMA((3, SUBS)), DMA((SUBS,)), DMA((4, SUBS)), DMA,
            DMA, DMA((2,)), DMA((4,)), DMA((4,)), DMA, DMA((2,)), DMA, DMA, DMA((4, SUBS)), DMA((4, SUBS, 3)), DMA, DMA,
        ],
        compiler_params=pltpu.CompilerParams(collective_id=0, has_side_effects=True, vmem_limit_bytes=40 << 20),
        name="collect",
    )(x, w, b, order, up, down, out, extra)


def greet_exchange(barrier):
    dp, mp, core, t = place()
    half, base = mp // 2, dp - core
    mine = lax.rem(mp, 2) * 2 + core
    for u in range(4):
        @pl.when((half != core) | (t != u))
        def _():
            pl.semaphore_signal(barrier, inc=1, device_id=chain_device(u, half, base), device_id_type=MESH)
    for g in range(4):
        @pl.when((half != core) | (mine != g))
        def _():
            pl.semaphore_signal(barrier, inc=1, device_id=worker(g, core, base), device_id_type=MESH)

    @pl.when(half == core)
    def _():
        pl.semaphore_wait(barrier, 6)

    @pl.when(half != core)
    def _():
        pl.semaphore_wait(barrier, 8)


def spread_kernel(a_ref, b_ref, oa_ref, ob_ref, send_sem, recv_sem, local_sem):
    dp, mp, core, t = place()
    half, base = mp // 2, dp - core
    mine = lax.rem(mp, 2) * 2 + core
    greet_exchange(pltpu.get_barrier_semaphore())
    for u in (3, 2, 1, 0):
        pair = ((a_ref.at[pl.ds(u * 1024, 1024)], oa_ref.at[mine]), (b_ref.at[pl.ds(u * 512, 512)], ob_ref.at[mine]))
        for k, (src, dst) in enumerate(pair):
            @pl.when((half != core) | (t != u))
            def _():
                send(src, dst, send_sem.at[u, k], recv_sem.at[mine, k], chain_device(u, half, base))

            @pl.when((half == core) & (t == u))
            def _():
                pltpu.make_async_copy(src, dst, local_sem.at[k]).start()
    for u in range(4):
        for k, src in enumerate((a_ref.at[pl.ds(u * 1024, 1024)], b_ref.at[pl.ds(u * 512, 512)])):
            @pl.when((half != core) | (t != u))
            def _():
                pltpu.make_async_copy(src, src, send_sem.at[u, k]).wait()
    for g in range(4):
        for k, dst in enumerate((oa_ref.at[g], ob_ref.at[g])):
            @pl.when((half != core) | (mine != g))
            def _():
                pltpu.make_async_copy(dst, dst, recv_sem.at[g, k]).wait()

            @pl.when((half == core) & (mine == g))
            def _():
                pltpu.make_async_copy(dst, dst, local_sem.at[k]).wait()


def spread(a, b):
    return pl.pallas_call(
        spread_kernel,
        out_shape=[jax.ShapeDtypeStruct((4, 1024, C), BF16), jax.ShapeDtypeStruct((4, 512, C), BF16)],
        in_specs=[ANY, ANY],
        out_specs=[ANY, ANY],
        scratch_shapes=[DMA((4, 2)), DMA((4, 2)), DMA((2,))],
        compiler_params=pltpu.CompilerParams(collective_id=1, has_side_effects=True),
        name="spread",
    )(a, b)


def regroup_kernel(a_ref, b_ref, oa_ref, ob_ref, send_sem, recv_sem, local_sem):
    dp, mp, core, t = place()
    half, base = mp // 2, dp - core
    mine = lax.rem(mp, 2) * 2 + core
    greet_exchange(pltpu.get_barrier_semaphore())
    big = lambda u: oa_ref.at[pl.ds(u * 1024, 1024)]
    small = lambda u: ob_ref.at[pl.ds(u * 512, 512)]
    for g in (0, 1, 2, 3):
        for k, (src, dst) in enumerate(((a_ref.at[g], big(t)), (b_ref.at[g], small(t)))):
            @pl.when((half != core) | (mine != g))
            def _():
                send(src, dst, send_sem.at[g, k], recv_sem.at[t, k], worker(g, core, base))

            @pl.when((half == core) & (mine == g))
            def _():
                pltpu.make_async_copy(src, dst, local_sem.at[k]).start()
    for g in range(4):
        for k, src in enumerate((a_ref.at[g], b_ref.at[g])):
            @pl.when((half != core) | (mine != g))
            def _():
                pltpu.make_async_copy(src, src, send_sem.at[g, k]).wait()
    for u in range(4):
        for k, dst in enumerate((big(u), small(u))):
            @pl.when((half != core) | (t != u))
            def _():
                pltpu.make_async_copy(dst, dst, recv_sem.at[u, k]).wait()

            @pl.when((half == core) & (t == u))
            def _():
                pltpu.make_async_copy(dst, dst, local_sem.at[k]).wait()


def regroup(a, b):
    return pl.pallas_call(
        regroup_kernel,
        out_shape=[jax.ShapeDtypeStruct((4096, C), BF16), jax.ShapeDtypeStruct((2048, C), BF16)],
        in_specs=[ANY, ANY],
        out_specs=[ANY, ANY],
        scratch_shapes=[DMA((4, 2)), DMA((4, 2)), DMA((2,))],
        compiler_params=pltpu.CompilerParams(collective_id=2, has_side_effects=True),
        name="regroup",
    )(a, b)


def settle_kernel(d0_ref, d1_ref, d2_ref, xs_ref, w_ref, extra_ref, mine_ref, out_ref, heads_ref, grads_ref,
                  stage, pair_in, chain_in, gw, gwl, h_in, z_in, z_out,
                  pair_recv, pair_send, chain_recv, chain_send, relay_send,
                  s_recv, s_send, c_recv, c_send, h_recv, h_send, z_recv, z_send, q_recv, q_send):
    dp, mp, core, t = place()
    base, spot = dp - core, lax.rem(dp, 8) // 2
    step = 1 - 2 * core
    partner, lower, upper = at(dp + step, mp), at(dp, mp - step), at(dp, mp + step)
    group = lax.rem(mp, 2) * 2 + core
    gives = core == lax.rem(mp, 2)
    quarter = lambda q: pl.ds(pl.multiple_of(q * QUARTER, QUARTER), QUARTER)
    share = lambda j, parity: grads_ref.at[pl.ds(pl.multiple_of((2 * j + parity) * SHARE, SHARE), SHARE)]

    greet(pltpu.get_barrier_semaphore(), True)

    grads_ref[pl.ds(pl.multiple_of((2 * spot + core) * SHARE, SHARE), SHARE), :] = mine_ref[...]
    for rel in (1, 2, 3):
        send(mine_ref, share(spot, core), s_send.at[rel], s_recv.at[rel], at(mate(dp, rel), mp))

    def weight_gradients():
        gw[...] = jnp.zeros_like(gw)

        def part(i, sums):
            rows = pl.ds(pl.multiple_of(i * SUB, SUB), SUB)
            x = xs_ref[rows, :]
            new = []
            for h, d_ref in enumerate((d0_ref, d1_ref, d2_ref)):
                d = d_ref[rows, :]
                gw[pl.ds(h * 256, 256), :] += dot(d, x, 0, 0)
                new.append(sums[h] + jnp.sum(d.astype(F32), axis=0, keepdims=True))
            return tuple(new)

        sums = lax.fori_loop(0, 4 * ROWS // SUB, part, tuple(jnp.zeros((1, 256), F32) for _ in range(3)))
        gwl[...] = gw[...].astype(BF16)
        for h in range(3):
            line = jnp.concatenate([sums[h], jnp.zeros((1, WIDTH - 256), F32)], axis=1)
            spare = h * 256 + (192 if h == 1 else 128)
            gwl[pl.ds(spare, 16), :] = jnp.concatenate([line, jnp.zeros((15, WIDTH), F32)], axis=0).astype(BF16)
        for rel in (1, 2, 3):
            send(gwl.at[quarter(spot ^ rel)], h_in.at[rel], h_send.at[rel], h_recv.at[rel], at(mate(dp, rel), mp))

    def plane_sum():
        for rel in (1, 2, 3):
            wait(h_in.at[rel], h_recv.at[rel])
        half_sum = gwl[quarter(spot), :].astype(F32)
        for rel in (1, 2, 3):
            half_sum += h_in[rel].astype(F32)
        z_out[...] = half_sum.astype(BF16)

        @pl.when(mp != group)
        def _():
            send(z_out, z_in.at[mp // 2], z_send, z_recv.at[mp // 2], at(dp, group))

    tt = jnp.minimum(t, 3 - t)
    for i in range(3):
        u = lax.rem(3 - i + tt, 4)
        for s in range(SUBS):
            rows = pl.ds(pl.multiple_of(u * ROWS + s * SUB, SUB), SUB)
            value = jnp.zeros((SUB, WIDTH), F32)
            for h, d_ref in enumerate((d0_ref, d1_ref, d2_ref)):
                value += jnp.dot(d_ref[rows, :], w_ref[pl.ds(h * 256, 256), :], preferred_element_type=F32)

            @pl.when(t >= 2)
            def _():
                stage[rows, :] = value.astype(BF16)
                send(stage.at[rows], pair_in.at[rows], pair_send.at[i, s], pair_recv.at[i, s], partner)

            @pl.when(t <= 1)
            def _():
                wait(pair_in.at[rows], pair_recv.at[i, s])
                here = value + pair_in[rows, :].astype(F32)
                if i == 0:
                    stage[rows, :] = here.astype(BF16)
                else:
                    @pl.when(t == 1)
                    def _():
                        wait(chain_in.at[rows], chain_recv.at[u, s])
                        stage[rows, :] = (here + chain_in[rows, :].astype(F32)).astype(BF16)

                    @pl.when(t == 0)
                    def _():
                        stage[rows, :] = here.astype(BF16)

                @pl.when((t == 0) | (i > 0))
                def _():
                    send(stage.at[rows], chain_in.at[rows], chain_send.at[i, s], chain_recv.at[u, s], upper)

                if i == 0:
                    @pl.when(t == 1)
                    def _():
                        send(stage.at[rows], chain_in.at[rows], chain_send.at[i, s], chain_recv.at[u, s], lower)

        if i < 2:
            @pl.when(t == 1)
            def _():
                (weight_gradients, plane_sum)[i]()

    @pl.when(t != 1)
    def _():
        weight_gradients()

    for rel in (1, 2, 3):
        wait(share(spot ^ rel, core), s_recv.at[rel])
    for j in range(4):
        send(share(j, core), share(j, core), c_send.at[j], c_recv.at[j], partner)

    @pl.when(t == 2)
    def _():
        for s in range(SUBS):
            rows = pl.ds(3 * ROWS + s * SUB, SUB)
            wait(chain_in.at[rows], chain_recv.at[3, s])
            send(chain_in.at[rows], chain_in.at[rows], relay_send.at[s], chain_recv.at[3, s], upper)
            if s == 0:
                plane_sum()

    @pl.when((t == 0) | (t == 3))
    def _():
        plane_sum()

    for s in range(SUBS):
        rows = pl.ds(pl.multiple_of(tt * ROWS + s * SUB, SUB), SUB)
        cut = pl.ds(s * SUB, SUB)
        value = jnp.zeros((SUB, WIDTH), F32)
        for h, d_ref in enumerate((d0_ref, d1_ref, d2_ref)):
            value += jnp.dot(d_ref[rows, :], w_ref[pl.ds(h * 256, 256), :], preferred_element_type=F32)

        @pl.when(t >= 2)
        def _():
            stage[rows, :] = value.astype(BF16)
            send(stage.at[rows], pair_in.at[rows], pair_send.at[3, s], pair_recv.at[3, s], partner)

        @pl.when(t <= 1)
        def _():
            stage[rows, :] = value.astype(BF16)

    @pl.when(gives)
    def _():
        both = jnp.zeros((QUARTER, WIDTH), F32)
        for far in (0, 1):
            source = mp // 2 + 2 * far

            @pl.when(source == mp)
            def _():
                z_in[far] = z_out[...]

            @pl.when(source != mp)
            def _():
                wait(z_in.at[far], z_recv.at[far])

            both += z_in[far].astype(F32)
        heads_ref[quarter(spot), :] = both.astype(BF16)
        mine = heads_ref.at[quarter(spot)]
        send(mine, mine, q_send.at[0], q_recv.at[spot], partner)
        for rel in (1, 2, 3):
            send(mine, mine, q_send.at[rel], q_recv.at[spot], at(mate(dp, rel), mp))
            send(mine, mine, q_send.at[rel + 3], q_recv.at[spot], at(mate(dp, rel) + step, mp))

    for s in range(SUBS):
        cut = pl.ds(s * SUB, SUB)
        rows = pl.ds(pl.multiple_of(t * ROWS + s * SUB, SUB), SUB)
        wait(chain_in.at[rows], chain_recv.at[t, s])
        value = extra_ref[cut, :] + chain_in[rows, :].astype(F32)

        @pl.when(t <= 1)
        def _():
            wait(pair_in.at[rows], pair_recv.at[3, s])
            out_ref[cut, :] = (value + stage[rows, :].astype(F32) + pair_in[rows, :].astype(F32)).astype(BF16)

        @pl.when(t >= 2)
        def _():
            out_ref[cut, :] = value.astype(BF16)

    for q in range(4):
        @pl.when(jnp.logical_not(gives) | (spot != q))
        def _():
            wait(heads_ref.at[quarter(q)], q_recv.at[q])
    for j in range(4):
        wait(share(j, 1 - core), c_recv.at[j])

    for s in range(SUBS):
        piece = stage.at[pl.ds(s * SUB, SUB)]

        @pl.when(t >= 2)
        def _():
            for i in range(4):
                wait(piece, pair_send.at[i, s])

        @pl.when(t <= 1)
        def _():
            for i in range(3):
                wait(piece, chain_send.at[i, s])

        @pl.when(t == 2)
        def _():
            wait(piece, relay_send.at[s])
    for rel in (1, 2, 3):
        wait(mine_ref, s_send.at[rel])
        wait(z_out, h_send.at[rel])
    for j in range(4):
        wait(mine_ref, c_send.at[j])

    @pl.when(mp != group)
    def _():
        wait(z_out, z_send)

    @pl.when(gives)
    def _():
        for k in range(7):
            wait(z_out, q_send.at[k])


def settle(d0, d1, d2, xs, w, extra, mine):
    return pl.pallas_call(
        settle_kernel,
        out_shape=[sds((ROWS, WIDTH), BF16), sds((WIDTH, WIDTH), BF16), sds((PACK, WIDTH), BF16)],
        in_specs=[VM] * 7,
        out_specs=[VM] * 3,
        scratch_shapes=[VMEM((4 * ROWS, WIDTH), BF16)] * 3 + [
            VMEM((WIDTH, WIDTH), F32), VMEM((WIDTH, WIDTH), BF16), VMEM((4, QUARTER, WIDTH), BF16), VMEM((2, QUARTER, WIDTH), BF16),
            VMEM((QUARTER, WIDTH), BF16),
            DMA((4, SUBS)), DMA((4, SUBS)), DMA((4, SUBS)), DMA((3, SUBS)), DMA((SUBS,)),
            DMA((4,)), DMA((4,)), DMA((4,)), DMA((4,)), DMA((4,)), DMA((4,)), DMA((2,)), DMA, DMA((4,)), DMA((7,)),
        ],
        compiler_params=pltpu.CompilerParams(collective_id=3, has_side_effects=True, vmem_limit_bytes=60 << 20),
        name="settle",
    )(d0, d1, d2, xs, w, extra, mine)


EPS = 1e-12
CHUNK = 256
FF_MODEL = 768


def gelu_and_slope(v):
    size = jnp.abs(v)
    u = 1.0 / (1.0 + (0.3275911 * 0.7071067811865476) * size)
    bell = jnp.exp(-0.5 * v * v)
    poly = u * (0.127414796 + u * (-0.142248368 + u * (0.7107068705 + u * (-0.7265760135 + u * 0.5307027145))))
    tail = poly * bell
    cdf = jnp.where(v < 0, tail, 1.0 - tail)
    return v * cdf, cdf + v * (bell * 0.3989422804014327)


def row_mean(v):
    return jnp.sum(v, axis=-1, keepdims=True) * (1.0 / FF_MODEL)


def ffn_kernel(c01_ref, c2_ref, tok_ref, cot_ref, vec_ref, *rest):
    pieces, rest = rest[:4], rest[4:]
    (out_ref, res_ref, g01_ref, g2_ref, sum_ref,
     w, wout, ctx, x, x_t, gf, gf_t, act, slope, zhat, acc, rstd, cols, recv,
     w_local, w_send, w_recv, g_send, g_recv, out_sem) = rest
    dp, mp, core, t = place()
    partner = at(dp + 1 - 2 * core, mp)
    spot = lax.rem(dp, 8) // 2
    barrier = pltpu.get_barrier_semaphore()
    pl.semaphore_signal(barrier, inc=1, device_id=partner, device_id_type=MESH)
    pl.semaphore_wait(barrier, 1)

    def rows_of(shard, j, parity):
        return w.at[shard, pl.ds(pl.multiple_of((2 * j + parity) * SHARE, SHARE), SHARE)]

    first, second = jnp.where(core == 0, 1, 2), jnp.where(core == 0, 2, 1)
    for piece, rel in ((3, 3), (2, second), (1, first), (0, 0)):
        for k in range(4):
            src = pieces[piece].at[k]
            shard = lax.rem(mp - k + 4, 4)
            j = spot ^ rel
            pltpu.make_async_copy(src, rows_of(shard, j, core), w_local.at[j, shard]).start()
            send(src, rows_of(shard, j, core), w_send.at[j, shard], w_recv.at[j, shard], partner)

    lane = lax.broadcasted_iota(jnp.int32, (1, C), 1)
    for g in range(4):
        ctx[:, pl.ds(g * C, C)] = c01_ref[g]
    for g in (0, 2):
        a, b = c2_ref[g].astype(F32), c2_ref[g + 1].astype(F32)
        col = pl.ds(4 * C + g * HD, C)
        ctx[pl.ds(0, 512), col] = jnp.where(lane < HD, a, pltpu.roll(b, HD, 1)).astype(BF16)
        ctx[pl.ds(512, 512), col] = jnp.where(lane < HD, pltpu.roll(a, HD, 1), b).astype(BF16)

    def wait_weights(j):
        for shard in range(4):
            ref = w.at[shard, pl.ds(0, SHARE)]
            pltpu.make_async_copy(ref, ref, w_local.at[j, shard]).wait()
            pltpu.make_async_copy(ref, ref, w_recv.at[j, shard]).wait()

    for j in (3, 0, 1, 2):
        wait_weights(j)

    for m in range(4):
        wout[pl.ds(m * C, C), :] = w[m, pl.ds(OUT_ROW, C), :]
        wout[pl.ds(4 * C + m * HD, HD), :] = w[m, pl.ds(OUT_ROW + C, HD), :]

    cols[...] = jnp.zeros_like(cols)
    b_out, gain1, bias1, b_down, gain2, bias2 = (vec_ref[pl.ds(i, 1), :] for i in range(6))

    def forward(r, _):
        rows = pl.ds(pl.multiple_of(r * CHUNK, CHUNK), CHUNK)
        h = jnp.dot(ctx[rows, :], wout[...], preferred_element_type=F32) + tok_ref[rows, :].astype(F32) + b_out
        h = h - row_mean(h)
        scale = lax.rsqrt(row_mean(h * h) + EPS)
        rstd[rows, :] = scale
        h = h * scale
        zhat[rows, :] = h
        first = h * gain1 + bias1
        acc[rows, :] = first + b_down
        x[rows, :] = first.astype(BF16)
        x_t[:, rows] = first.T.astype(BF16)

        def hidden(m, _):
            total = acc[rows, :]
            up_bias = w[m, pl.ds(BIAS_ROW, 16), :].astype(F32)[0:1, :]
            for f in range(3):
                cut = pl.ds(f * 256, 256)
                pre = jnp.dot(x[rows, :], w[m, pl.ds(0, 768), cut], preferred_element_type=F32) + up_bias[:, f * 256 : f * 256 + 256]
                value, grad = gelu_and_slope(pre)
                value = value.astype(BF16)
                act[m, rows, cut] = value
                slope[m, rows, cut] = grad.astype(BF16)
                total += jnp.dot(value, w[m, pl.ds(768 + f * 256, 256), :], preferred_element_type=F32)
            acc[rows, :] = total
            return 0

        lax.fori_loop(0, 4, hidden, 0)

        z = acc[rows, :]
        z = z - row_mean(z)
        scale = lax.rsqrt(row_mean(z * z) + EPS)
        z = z * scale
        out_ref[rows, :] = (z * gain2 + bias2).astype(BF16)
        cot = cot_ref[rows, :].astype(F32)
        dz = cot * gain2
        gs = scale * (dz - row_mean(dz) - z * row_mean(dz * z))
        cols[pl.ds(2, 1), :] += jnp.sum(cot * z, axis=0, keepdims=True)
        cols[pl.ds(3, 1), :] += jnp.sum(cot, axis=0, keepdims=True)
        cols[pl.ds(5, 1), :] += jnp.sum(gs, axis=0, keepdims=True)
        acc[rows, :] = gs
        gf[rows, :] = gs.astype(BF16)
        gf_t[:, rows] = gs.T.astype(BF16)
        return 0

    lax.fori_loop(0, 1024 // CHUNK, forward, 0)

    def give(m, j):
        cut = pl.ds(pl.multiple_of((2 * j + 1 - core) * SHARE, SHARE), SHARE)
        send(w.at[m, cut], recv.at[m, j], g_send.at[m, j], g_recv.at[m, j], partner)

    for j in range(4):
        for shard in range(4):
            ref = w.at[shard, pl.ds(0, SHARE)]
            pltpu.make_async_copy(ref, ref, w_send.at[j, shard]).wait()

    def backward(m, _):
        def rows_back(r, _):
            rows = pl.ds(pl.multiple_of(r * CHUNK, CHUNK), CHUNK)
            total = acc[rows, :]
            for f in range(3):
                cut = pl.ds(f * 256, 256)
                ga = dot(gf[rows, :], w[m, pl.ds(768 + f * 256, 256), :], 1, 1)
                gp = (ga * slope[m, rows, cut].astype(F32)).astype(BF16)
                slope[m, rows, cut] = gp
                total += dot(gp, w[m, pl.ds(0, 768), cut], 1, 1)
            acc[rows, :] = total
            return 0

        lax.fori_loop(0, 1024 // CHUNK, rows_back, 0)
        bias = []
        for f in range(3):
            cut = pl.ds(f * 256, 256)
            gp = slope[m, :, cut]
            w[m, pl.ds(0, 768), cut] = jnp.dot(x_t[...], gp, preferred_element_type=F32).astype(BF16)
            w[m, pl.ds(768, 768), cut] = jnp.dot(gf_t[...], act[m, :, cut], preferred_element_type=F32).astype(BF16)
            bias.append(jnp.sum(gp.astype(F32), axis=0, keepdims=True))
        cols[pl.ds(8 + m, 1), :] = jnp.concatenate(bias, axis=1)
        for j in range(3):
            give(m, j)
        return 0

    lax.fori_loop(0, 4, backward, 0)

    def first_back(r, _):
        rows = pl.ds(pl.multiple_of(r * CHUNK, CHUNK), CHUNK)
        grad = acc[rows, :]
        z = zhat[rows, :]
        dz = grad * gain1
        gr = rstd[rows, :] * (dz - row_mean(dz) - z * row_mean(dz * z))
        cols[pl.ds(0, 1), :] += jnp.sum(grad * z, axis=0, keepdims=True)
        cols[pl.ds(1, 1), :] += jnp.sum(grad, axis=0, keepdims=True)
        cols[pl.ds(4, 1), :] += jnp.sum(gr, axis=0, keepdims=True)
        res_ref[rows, :] = gr
        low = gr.astype(BF16)
        gf[rows, :] = low
        gc = dot(low, wout[...], 1, 1).astype(BF16)
        for g in range(4):
            g01_ref[g, rows, :] = gc[:, g * C : g * C + C]
        ctx_grad[rows, :] = gc[:, 4 * C :]
        return 0

    ctx_grad = x
    ctx_grad = x.at[:, pl.ds(0, 2 * C)]
    lax.fori_loop(0, 1024 // CHUNK, first_back, 0)
    for g in (0, 2):
        top = ctx_grad[pl.ds(0, 512), pl.ds(g * HD, C)].astype(F32)
        low = ctx_grad[pl.ds(512, 512), pl.ds(g * HD, C)].astype(F32)
        g2_ref[g] = jnp.where(lane < HD, top, pltpu.roll(low, HD, 1)).astype(BF16)
        g2_ref[g + 1] = jnp.where(lane < HD, pltpu.roll(top, HD, 1), low).astype(BF16)

    for n in range(3):
        cut = pl.ds(n * 256, 256)
        part = dot(ctx[:, cut], gf[...], 0, 0).astype(BF16)
        if n < 2:
            for i in range(2):
                w[2 * n + i, pl.ds(OUT_ROW, C), :] = part[i * C : i * C + C, :]
        else:
            for i in range(4):
                w[i, pl.ds(OUT_ROW + C, HD), :] = part[i * HD : i * HD + HD, :]
    for m in range(4):
        w[m, pl.ds(BIAS_ROW, 16), :] = jnp.concatenate(
            [cols[pl.ds(8 + m, 1), :], cols[pl.ds(0, 6), :], jnp.zeros((9, FF_MODEL), F32)], axis=0
        ).astype(BF16)
        give(m, 3)

    for rel in (3, 2, 1, 0):
        j = spot ^ rel
        along = jnp.where(core == 0, rel % 2, rel // 2)
        across = jnp.where(core == 0, rel // 2, rel % 2)
        for m in range(4):
            wait(recv.at[m, j], g_recv.at[m, j])
            cut = pl.ds(pl.multiple_of((2 * j + core) * SHARE, SHARE), SHARE)
            recv[m, j] = (recv[m, j].astype(F32) + w[m, cut, :].astype(F32)).astype(BF16)
            pltpu.make_async_copy(recv.at[m, j], sum_ref.at[along, across, m], out_sem.at[m, rel]).start()
    for m in range(4):
        for j in range(4):
            wait(recv.at[m, j], out_sem.at[m, j])
            wait(recv.at[m, j], g_send.at[m, j])


def ffn(c01, c2, tokens, cot, vecs, pieces):
    dma = pltpu.SemaphoreType.DMA
    vm, any_ = pl.BlockSpec(memory_space=pltpu.VMEM), pl.BlockSpec(memory_space=pl.ANY)
    sds = jax.ShapeDtypeStruct
    return pl.pallas_call(
        ffn_kernel,
        out_shape=[sds((1024, 768), BF16), sds((1024, 768), F32), sds((4, 1024, C), BF16), sds((4, 512, C), BF16),
                   sds((2, 2, 4, SHARE, 768), BF16)],
        in_specs=[vm] * 5 + [any_] * 4,
        out_specs=[vm] * 4 + [any_],
        scratch_shapes=[
            VMEM((4, PACK, 768), BF16), VMEM((768, 768), BF16),
            VMEM((1024, 768), BF16), VMEM((1024, 768), BF16), VMEM((768, 1024), BF16), VMEM((1024, 768), BF16), VMEM((768, 1024), BF16),
            VMEM((4, 1024, 768), BF16), VMEM((4, 1024, 768), BF16),
            VMEM((1024, 768), F32), VMEM((1024, 768), F32), VMEM((1024, 1), F32), VMEM((16, 768), F32),
            VMEM((4, 4, SHARE, 768), BF16),
            dma((4, 4)), dma((4, 4)), dma((4, 4)), dma((4, 4)), dma((4, 4)), dma((4, 4)),
        ],
        compiler_params=pltpu.CompilerParams(collective_id=4, has_side_effects=True, vmem_limit_bytes=63 << 20),
        name="ffn",
    )(c01, c2, tokens, cot, vecs, *pieces)


def swap(value, even_bits, odd_bits, n_dp):
    return lax.ppermute(value, "dp", [(d, d ^ (odd_bits if d % 2 else even_bits)) for d in range(n_dp)])


def pick(value, index, axis):
    return lax.dynamic_index_in_dim(value, index, axis, keepdims=False)


def total(a, b):
    return (a.astype(F32) + b.astype(F32)).astype(BF16)


def tie(*values):
    return lax.optimization_barrier(values)


def body(n_dp, tokens, w_query, b_query, w_key, w_value, b_value, w_out, b_out, norm1_gain, norm1_bias, w_up, b_up, w_down,
         b_down, norm2_gain, norm2_bias, key_mask, cluster_order, cotangent):
    dp, mp, core, t = place()
    ring = lambda k: [(z, (z + k) % 4) for z in range(4)]

    live = jnp.sum(key_mask).astype(jnp.int32)
    order = jnp.where(core == 1, cluster_order ^ 3072, cluster_order).reshape(3 * L)
    order = jnp.concatenate([order, jnp.broadcast_to(live, (128,))])
    q, k, v = (w.T.reshape(3, HD, WIDTH) for w in (w_query, w_key, w_value))
    none = jnp.zeros((HD, WIDTH), BF16)
    w_heads = jnp.concatenate([part for h in range(3) for part in ([q[h], v[h], k[h], none] if h == 1 else [v[h], q[h], none, k[h]])])
    bq, bv, bz = b_query.reshape(3, HD), b_value.reshape(3, HD), jnp.zeros((C,), F32)
    b_heads = jnp.stack([jnp.concatenate([bq[h], bv[h], bz] if h == 1 else [bv[h], bq[h], bz]) for h in range(3)])
    b_heads = jnp.concatenate([b_heads, jnp.zeros((5, 256), F32)])
    extra = jnp.concatenate([b_up.reshape(1, WIDTH), jnp.zeros((PACK - BIAS_ROW - 1, WIDTH), BF16)])

    xs, qkv, w_heads, order, share = collect(tokens, w_heads, b_heads, order, w_up, w_down, w_out, extra)
    qkv, share = tie(qkv, share)
    shares = [share] + [lax.ppermute(share, "mp", ring(i)) for i in (1, 2, 3)]
    c01, ts01, probs01 = attend(0, order, qkv)
    c01, *shares = tie(c01, *shares)
    near = jnp.stack(shares)
    next_to = swap(near, 2, 4, n_dp)
    c2, ts2, probs2 = attend(2, order, qkv)
    c2, near, next_to = tie(c2, near, next_to)
    far = swap(jnp.stack([near, next_to]), 4, 2, n_dp)
    c01, c2 = spread(c01, c2)

    vecs = jnp.stack([b_out, norm1_gain, norm1_bias, b_down, norm2_gain, norm2_bias, b_out, b_out])
    layer_out, grad_residual, g01, g2, sums = ffn(c01, c2, tokens, cotangent, vecs, (near, next_to, far[0], far[1]))

    got = swap(sums[1], 2, 4, n_dp)
    g01, g2 = regroup(g01, g2)
    d0 = attend_back(0, order, g01, ts01, probs01)
    d0, sums, got = tie(d0, sums, got)
    sums = total(sums[0], got)
    got = swap(sums[1], 4, 2, n_dp)
    d1 = attend_back(1, order, g01, ts01, probs01)
    d1, sums, got = tie(d1, sums, got)
    sums = total(sums[0], got)
    for bit in range(3, n_dp.bit_length() - 1):
        sums = total(sums, swap(sums, 1 << bit, 1 << bit, n_dp))
    parts = [pick(sums, mp, 0)]
    for i in (1, 2, 3):
        parts.append(lax.ppermute(pick(sums, (mp + i) % 4, 0), "mp", ring(i)))
    d2 = attend_back(2, order, g2, ts2, probs2)
    d2, *parts = tie(d2, *parts)
    mine = sum(p.astype(F32) for p in parts).astype(BF16)
    grad_tokens, heads, grads = settle(d0, d1, d2, xs, w_heads, grad_residual, mine)
    for bit in range(3, n_dp.bit_length() - 1):
        heads = total(heads, swap(heads, 1 << bit, 1 << bit, n_dp))
    grads, heads = grads.astype(F32), heads.astype(F32).reshape(3, 256, WIDTH)
    at_q, at_v, at_k = (HD, 0, HD), (0, HD, 0), (3 * HD, 2 * HD, 3 * HD)
    spare = (2 * HD, 3 * HD, 2 * HD)
    cols = lambda where: jnp.concatenate([heads[h, where[h] : where[h] + HD] for h in range(3)]).T
    sums_of = lambda where: jnp.concatenate([heads[h, spare[h], where[h] : where[h] + HD] for h in range(3)])

    vec = lambda i: grads[1728 + i]
    return (
        layer_out,
        grad_tokens,
        cols(at_q),
        sums_of(at_q),
        cols(at_k),
        cols(at_v),
        sums_of(at_v),
        grads[1536:1728],
        vec(5),
        vec(1),
        vec(2),
        grads[:768],
        vec(0),
        grads[768:1536].T,
        vec(6),
        vec(3),
        vec(4),
    )


def solution(mesh):
    return jax.shard_map(
        functools.partial(body, mesh.shape["dp"]),
        mesh=mesh,
        in_specs=(
            P(("dp", "mp"), None), P(None, "mp"), P("mp"), P(None, "mp"), P(None, "mp"), P("mp"), P("mp", None), P(), P(), P(),
            P(None, "mp"), P("mp"), P("mp", None), P(), P(), P(), P("dp", None), P("dp", "mp", None), P(("dp", "mp"), None),
        ),
        out_specs=(
            P(("dp", "mp"), None), P(("dp", "mp"), None), P(None, "mp"), P("mp"), P(None, "mp"), P(None, "mp"), P("mp"),
            P("mp", None), P(), P(), P(), P(None, "mp"), P("mp"), P("mp", None), P(), P(), P(),
        ),
        check_vma=False,
    )
```

```python
import functools
import jax
import jax.numpy as jnp
from jax import lax
from jax.experimental import pallas as pl
from jax.experimental.pallas import tpu as pltpu
from jax.sharding import PartitionSpec as P

L = 4096
C = 128
HD = 64
GROUP = 2
STEP = 1024
GROUPS = STEP // (GROUP * C)
F32 = jnp.float32
BF16 = jnp.bfloat16
VMEM = pltpu.VMEM


def dot(a, b, da, db):
    return lax.dot_general(a, b, (((da,), (db,)), ((), ())), preferred_element_type=F32)


def in_turn(gather, compute, scatter, bufs, outs):
    gather(0, bufs[0])
    for group in range(GROUPS):
        if group + 1 < GROUPS:
            gather(group + 1, bufs[(group + 1) % 2])
        compute(group, bufs[group % 2], outs[group % 2])
        if group:
            scatter(group - 1, outs[(group - 1) % 2])
    scatter(GROUPS - 1, outs[(GROUPS - 1) % 2])


def attend_kernel(first, ord_ref, mask_ref, qkv_ref, c_ref, ts_ref, pr_ref, src, ctx, *slots):
    head, step = pl.program_id(0) + first, pl.program_id(1)
    live = jnp.sum(mask_ref[...].astype(F32), axis=1, keepdims=True).astype(jnp.int32)

    @pl.when(step == 0)
    def _():
        src[pl.ds(0, L, stride=2), :] = qkv_ref[0, :, :C].astype(F32)
        src[pl.ds(1, L, stride=2), :] = qkv_ref[0, :, C:].astype(F32)

    def gather(group, buf):
        for u in range(GROUP * C):
            buf[pl.ds(2 * u, 2), :] = src[pl.ds(pl.multiple_of(ord_ref[group * GROUP * C + u], 2), 2), :]

    def compute(group, buf, out):
        each = range(GROUP)
        rows = [pl.ds((group * GROUP + i) * C, C) for i in each]
        t0 = [buf[pl.ds(2 * i * C, C, stride=2), :].astype(BF16) for i in each]
        t1 = [buf[pl.ds(2 * i * C + 1, C, stride=2), :].astype(BF16) for i in each]
        for i in each:
            ts_ref[0, rows[i], :C] = t0[i]
            ts_ref[0, rows[i], C:] = t1[i]
        slot = [step * STEP + (group * GROUP + i) * C + lax.broadcasted_iota(jnp.int32, (C, C), 0) for i in each]
        scores = [dot(t1[i], t0[i], 1, 1) * 0.125 + jnp.where(slot[i] < live, 0.0, -10000.0) for i in each]
        e = [jnp.exp(scores[i] - jnp.max(scores[i], axis=0, keepdims=True)) for i in each]
        probs = [e[i] * (1.0 / jnp.sum(e[i], axis=0, keepdims=True)) for i in each]
        for i in each:
            pr_ref[0, rows[i], :] = probs[i]
        for i in each:
            out[pl.ds(i * C, C), :] = dot(probs[i].astype(BF16), t0[i], 0, 0)

    def scatter(group, out):
        for u in range(GROUP * C):
            ctx[pl.ds(ord_ref[group * GROUP * C + u], 1), :] = out[pl.ds(u, 1), :]

    in_turn(gather, compute, scatter, slots[:2], slots[2:])

    @pl.when(step == L // STEP - 1)
    def _():
        lane = lax.broadcasted_iota(jnp.int32, (1, C), 1)
        if first == 2:
            for k in range(4):
                low = ctx[pl.ds(k * 2048, 512, stride=2), :]
                high = pltpu.roll(ctx[pl.ds(k * 2048 + 1024, 512, stride=2), :], HD, 1)
                c_ref[pl.ds(k * 512, 512), :] = jnp.where(lane < HD, low, high).astype(BF16)
        else:
            rows = ctx[pl.ds(0, L, stride=2), :].astype(BF16)

            @pl.when(head == 0)
            def _():
                c_ref[...] = rows

            @pl.when(head == 1)
            def _():
                c_ref[...] = jnp.where(lane < HD, c_ref[...], rows)


def attend(first, order, mask, qkv):
    heads = 2 if first == 0 else 1
    whole = lambda shape: pl.BlockSpec(shape, lambda h, i: (0,) * len(shape), pipeline_mode=pl.Buffered(1))
    per_step = lambda width: pl.BlockSpec((1, STEP, width), lambda h, i: (h, i, 0))
    steps = L // STEP
    out_rows = L if first == 0 else L // 2
    return pl.pallas_call(
        functools.partial(attend_kernel, first),
        grid=(heads, steps),
        in_specs=[
            pl.BlockSpec((STEP,), lambda h, i: ((h + first) * steps + i,), memory_space=pltpu.SMEM),
            whole((1, L)),
            pl.BlockSpec((1, L, 2 * C), lambda h, i: (h + first, 0, 0)),
        ],
        out_specs=[whole((out_rows, C)), per_step(2 * C), per_step(C)],
        out_shape=[
            jax.ShapeDtypeStruct((out_rows, C), BF16),
            jax.ShapeDtypeStruct((heads, L, 2 * C), BF16),
            jax.ShapeDtypeStruct((heads, L, C), F32),
        ],
        scratch_shapes=[VMEM((2 * L, C), F32), VMEM((2 * L, C), F32)]
        + [VMEM((2 * GROUP * C, C), F32)] * 2 + [VMEM((GROUP * C, C), F32)] * 2,
        compiler_params=pltpu.CompilerParams(vmem_limit_bytes=60 << 20),
        cost_estimate=pl.CostEstimate(flops=heads * 9 * 10**9, bytes_accessed=10 << 20, transcendentals=0),
        name="attend",
    )(order, mask, qkv)


def attend_back_kernel(head, ord_ref, g_ref, ts_ref, pr_ref, d_ref, gsrc, dst, *slots):
    step = pl.program_id(0)
    lane = lax.broadcasted_iota(jnp.int32, (1, C), 1)

    @pl.when(step == 0)
    def _():
        if head == 2:
            for k in range(4):
                both = g_ref[pl.ds(k * 512, 512), :].astype(F32)
                gsrc[pl.ds(k * 2048, 512, stride=2), :] = both
                gsrc[pl.ds(k * 2048 + 1024, 512, stride=2), :] = pltpu.roll(both, HD, 1)
        else:
            gsrc[pl.ds(0, L, stride=2), :] = g_ref[...].astype(F32)

    keep = (lane >= HD) if head == 1 else (lane < HD)

    def gather(group, buf):
        for u in range(GROUP * C):
            buf[pl.ds(u, 1), :] = gsrc[pl.ds(ord_ref[group * GROUP * C + u], 1), :]

    def compute(group, buf, out):
        each = range(GROUP)
        rows = [pl.ds((group * GROUP + i) * C, C) for i in each]
        t0 = [ts_ref[0, rows[i], :C] for i in each]
        t1 = [ts_ref[0, rows[i], C:] for i in each]
        probs = [pr_ref[0, rows[i], :] for i in each]
        g = [jnp.where(keep, buf[pl.ds(i * C, C), :], 0.0).astype(BF16) for i in each]
        dp = [dot(t0[i], g[i], 1, 1) for i in each]
        ds = [(probs[i] * (dp[i] - jnp.sum(probs[i] * dp[i], axis=0, keepdims=True))).astype(BF16) for i in each]
        for i in each:
            grad = dot(ds[i], t1[i], 0, 0) * 0.125 + jnp.dot(probs[i].astype(BF16), g[i], preferred_element_type=F32)
            out[pl.ds(2 * i * C, C, stride=2), :] = grad
        for i in each:
            out[pl.ds(2 * i * C + 1, C, stride=2), :] = jnp.dot(ds[i], t0[i], preferred_element_type=F32) * 0.125

    def scatter(group, out):
        for u in range(GROUP * C):
            dst[pl.ds(pl.multiple_of(ord_ref[group * GROUP * C + u], 2), 2), :] = out[pl.ds(2 * u, 2), :]

    in_turn(gather, compute, scatter, slots[:2], slots[2:])

    @pl.when(step == L // STEP - 1)
    def _():
        d_ref[:, :C] = dst[pl.ds(0, L, stride=2), :].astype(BF16)
        d_ref[:, C:] = dst[pl.ds(1, L, stride=2), :].astype(BF16)


def attend_back(head, order, g, ts, probs):
    steps = L // STEP
    whole = lambda shape: pl.BlockSpec(shape, lambda i: (0,) * len(shape), pipeline_mode=pl.Buffered(1))
    per_step = lambda width: pl.BlockSpec((1, STEP, width), lambda i: (head % 2, i, 0))
    return pl.pallas_call(
        functools.partial(attend_back_kernel, head),
        grid=(steps,),
        in_specs=[
            pl.BlockSpec((STEP,), lambda i: (head * steps + i,), memory_space=pltpu.SMEM),
            whole(g.shape), per_step(2 * C), per_step(C),
        ],
        out_specs=whole((L, 2 * C)),
        out_shape=jax.ShapeDtypeStruct((L, 2 * C), BF16),
        scratch_shapes=[VMEM((2 * L, C), F32), VMEM((2 * L, C), F32)]
        + [VMEM((GROUP * C, C), F32)] * 2 + [VMEM((2 * GROUP * C, C), F32)] * 2,
        compiler_params=pltpu.CompilerParams(vmem_limit_bytes=60 << 20),
        cost_estimate=pl.CostEstimate(flops=9 * 10**9, bytes_accessed=10 << 20, transcendentals=0),
        name="attend_back",
    )(order, g, ts, probs)


MESH = pl.DeviceIdType.MESH
WIDTH = 768
ROWS = 1024
SUB = 512
SUBS = ROWS // SUB
SHARE = 224
PACK = 8 * SHARE
OUT_ROW = 1536
BIAS_ROW = 1728
QUARTER = 192
DMA = pltpu.SemaphoreType.DMA
ANY = pl.BlockSpec(memory_space=pl.ANY)
VM = pl.BlockSpec(memory_space=pltpu.VMEM)
sds = jax.ShapeDtypeStruct


def place():
    dp, mp = lax.axis_index("dp"), lax.axis_index("mp")
    core = lax.rem(dp, 2)
    return dp, mp, core, jnp.where(core == 0, mp, 3 - mp)


def at(dp, mp):
    return {"dp": dp, "mp": mp}


def signal(barrier, device):
    pl.semaphore_signal(barrier, inc=1, device_id=device, device_id_type=MESH)


def send(src, dst, send_sem, recv_sem, device):
    copy = pltpu.make_async_remote_copy(
        src_ref=src, dst_ref=dst, send_sem=send_sem, recv_sem=recv_sem, device_id=device, device_id_type=MESH
    )
    copy.start()
    return copy


def wait(ref, sem):
    pltpu.make_async_copy(ref, ref, sem).wait()


def mate(dp, rel):
    return dp + 2 * ((lax.rem(dp, 8) // 2 ^ rel) - lax.rem(dp, 8) // 2)


def greet(barrier, both_cores):
    dp, mp, core, t = place()
    step = 1 - 2 * core
    for k in range(4):
        if k:
            signal(barrier, at(dp, lax.rem(mp + k, 4)))
        signal(barrier, at(dp + step, lax.rem(mp + k, 4)))
    for rel in (1, 2, 3):
        signal(barrier, at(mate(dp, rel), mp))
        if both_cores:
            signal(barrier, at(mate(dp, rel) + step, mp))
    pl.semaphore_wait(barrier, 13 if both_cores else 10)


def worker(group, half, dp_base):
    return at(dp_base + group % 2, 2 * half + group // 2)


def chain_device(u, half, dp_base):
    return at(dp_base + half, jnp.where(half == 0, u, 3 - u))


def collect_kernel(x_ref, wq_ref, wk_ref, wv_ref, bsrc_ref, osrc_ref, msrc_ref, up_ref, down_ref, wout_ref, extra_ref,
                   xs_ref, qkv_ref, w_ref, ord_ref, mask_ref, share_ref,
                   xs, qkv, w, wsrc, bias, relay,
                   chain_recv, relay_recv, pair_recv, chain_send, relay_send, pair_send, own_sem,
                   wz_recv, wz_send, wp_recv, wp_send, b_recv, b_send, o_recv, o_send, m_recv, m_send, xs_out, qkv_out, w_out, share_sem, build_sem):
    dp, mp, core, t = place()
    base, half, spot = dp - core, mp // 2, lax.rem(dp, 8) // 2
    step = 1 - 2 * core
    partner, lower, upper = at(dp + step, mp), at(dp, mp - step), at(dp, mp + step)
    group = lax.rem(mp, 2) * 2 + core
    gives = core == lax.rem(mp, 2)
    order_self = worker(mp, core, base)
    order_here = (order_self["dp"] == dp) & (order_self["mp"] == mp)
    cut = lambda s: pl.ds(s * SUB, SUB)
    home = lambda u, s: xs.at[pl.ds(pl.multiple_of(u * ROWS + s * SUB, SUB), SUB)]
    quarter = lambda q: pl.ds(pl.multiple_of(q * QUARTER, QUARTER), QUARTER)

    own = pltpu.make_async_copy(x_ref, xs.at[pl.ds(pl.multiple_of(jnp.minimum(t, 1) * ROWS, ROWS), ROWS)], own_sem)

    @pl.when(t <= 1)
    def _():
        own.start()

    parts = []
    for h in range(3):
        for n, part in enumerate((wq_ref, wv_ref, wk_ref, None) if h == 1 else (wv_ref, wq_ref, None, wk_ref)):
            rows = pl.ds((4 * h + n) * HD, HD)
            if part is None:
                wsrc[rows, :] = jnp.zeros((HD, WIDTH), BF16)
            else:
                copy = pltpu.make_async_copy(part.at[pl.ds(h * HD, HD)], wsrc.at[rows], build_sem.at[4 * h + n])
                copy.start()
                parts.append(copy)
    for copy in parts:
        copy.wait()

    greet(pltpu.get_barrier_semaphore(), False)

    for far in (0, 1):
        target = mp // 2 + 2 * far

        @pl.when(gives & (target != mp))
        def _():
            send(wsrc.at[quarter(spot)], w.at[quarter(spot)], wz_send.at[far], wz_recv, at(dp, target))
            send(bsrc_ref, bias, b_send.at[far], b_recv, at(dp, target))

        @pl.when(gives & (target == mp))
        def _():
            pltpu.make_async_copy(wsrc.at[quarter(spot)], w.at[quarter(spot)], wz_recv).start()
            pltpu.make_async_copy(bsrc_ref, bias, b_recv).start()

    @pl.when(order_here)
    def _():
        pltpu.make_async_copy(osrc_ref, ord_ref, o_recv).start()
        pltpu.make_async_copy(msrc_ref, mask_ref, m_recv).start()

    @pl.when(jnp.logical_not(order_here))
    def _():
        send(osrc_ref, ord_ref, o_send, o_recv, order_self)
        send(msrc_ref, mask_ref, m_send, m_recv, order_self)

    @pl.when(t == 3)
    def _():
        for s in range(SUBS):
            send(x_ref.at[cut(s)], relay.at[cut(s)], chain_send.at[0, s], relay_recv.at[s], lower)

    @pl.when((t == 1) | (t == 2))
    def _():
        for s in range(SUBS):
            send(x_ref.at[cut(s)], home(t, s), chain_send.at[0, s], chain_recv.at[t, s], lower)

    @pl.when(t == 0)
    def _():
        for s in range(SUBS):
            send(x_ref.at[cut(s)], home(0, s), chain_send.at[0, s], chain_recv.at[0, s], upper)

    pack = ((0, up_ref), (768, down_ref), (OUT_ROW, wout_ref), (BIAS_ROW, extra_ref))
    for i in range(8):
        @pl.when(lax.rem(dp, 8) == i)
        def _():
            for first, part in pack:
                low, high = max(first, i * SHARE), min(first + part.shape[0], (i + 1) * SHARE)
                if low < high:
                    src = part.at[pl.ds(low - first, high - low)]
                    pltpu.make_async_copy(src, share_ref.at[pl.ds(low - i * SHARE, high - low)], share_sem).start()

    wait(w.at[quarter(spot)], wz_recv)
    for rel in (1, 2, 3):
        send(w.at[quarter(spot)], w.at[quarter(spot)], wp_send.at[rel], wp_recv.at[rel], at(mate(dp, rel), mp))

    @pl.when(t <= 1)
    def _():
        own.wait()
        for s in range(SUBS):
            send(home(t, s), home(t, s), pair_send.at[t, s], pair_recv.at[t, s], partner)

    tt = jnp.minimum(t, 3 - t)

    def rows_of(i, s):
        return pl.ds(pl.multiple_of(lax.rem(tt + i, 4) * ROWS + s * SUB, SUB), SUB)

    def receive(i, s):
        u = lax.rem(tt + i, 4)
        if i == 1:
            @pl.when(t == 2)
            def _():
                wait(relay.at[cut(s)], relay_recv.at[s])
                send(relay.at[cut(s)], home(3, s), relay_send.at[s], chain_recv.at[3, s], lower)

        if i > 0:
            @pl.when(t <= 1)
            def _():
                wait(home(u, s), chain_recv.at[u, s])
                if i < 3:
                    @pl.when(t == 1)
                    def _():
                        send(home(u, s), home(u, s), chain_send.at[i, s], chain_recv.at[u, s], lower)
                send(home(u, s), home(u, s), pair_send.at[u, s], pair_recv.at[u, s], partner)

        @pl.when(t >= 2)
        def _():
            wait(home(u, s), pair_recv.at[u, s])

        rows = rows_of(i, s)
        pltpu.make_async_copy(xs.at[rows], xs_ref.at[rows], xs_out.at[i, s]).start()

    def project(i, s):
        rows = rows_of(i, s)
        row = jnp.concatenate([bias[pl.ds(h, 1), :] for h in range(3)], axis=1)
        qkv[rows, :] = (dot(xs[rows, :], w[...], 1, 1) + row).astype(BF16)
        for h in range(3):
            pltpu.make_async_copy(qkv.at[rows, pl.ds(h * 256, 256)], qkv_ref.at[h, rows], qkv_out.at[i, s, h]).start()

    pieces = [(i, s) for i in range(4) for s in range(SUBS)]
    for i, s in pieces[:4]:
        receive(i, s)
    for rel in (1, 2, 3):
        wait(w.at[quarter(spot ^ rel)], wp_recv.at[rel])
    wait(bias, b_recv)
    pltpu.make_async_copy(w, w_ref, w_out).start()
    for i, s in pieces[:3]:
        project(i, s)
    for k in range(4, len(pieces)):
        receive(*pieces[k])
        project(*pieces[k - 1])
    project(*pieces[-1])

    for i in range(4):
        u = lax.rem(tt + i, 4)
        for s in range(SUBS):
            rows = pl.ds(pl.multiple_of(u * ROWS + s * SUB, SUB), SUB)
            wait(xs.at[rows], xs_out.at[i, s])
            for h in range(3):
                wait(qkv_ref.at[h, rows], qkv_out.at[i, s, h])

            @pl.when(t <= 1)
            def _():
                wait(home(u, s), pair_send.at[u, s])
    for s in range(SUBS):
        wait(x_ref.at[cut(s)], chain_send.at[0, s])

        @pl.when(t == 1)
        def _():
            wait(x_ref.at[cut(s)], chain_send.at[1, s])
            wait(x_ref.at[cut(s)], chain_send.at[2, s])

        @pl.when(t == 2)
        def _():
            wait(relay.at[cut(s)], relay_send.at[s])
    for rel in (1, 2, 3):
        wait(w.at[quarter(spot)], wp_send.at[rel])
    for far in (0, 1):
        @pl.when(gives & (mp // 2 + 2 * far != mp))
        def _():
            wait(wsrc.at[quarter(spot)], wz_send.at[far])
            wait(bsrc_ref, b_send.at[far])
    wait(ord_ref, o_recv)
    wait(mask_ref, m_recv)

    @pl.when(jnp.logical_not(order_here))
    def _():
        wait(osrc_ref, o_send)
        wait(msrc_ref, m_send)

    wait(w, w_out)
    wait(share_ref, share_sem)


def collect(x, wq, wk, wv, b, order, mask, up, down, out, extra):
    return pl.pallas_call(
        collect_kernel,
        out_shape=[sds((4 * ROWS, WIDTH), BF16), sds((3, 4 * ROWS, 256), BF16), sds((WIDTH, WIDTH), BF16), sds((3 * L,), jnp.int32),
                   sds((1, L), jnp.int32), sds((SHARE, WIDTH), BF16)],
        in_specs=[ANY] * 11,
        out_specs=[ANY] * 6,
        scratch_shapes=[
            VMEM((4 * ROWS, WIDTH), BF16), VMEM((4 * ROWS, WIDTH), BF16), VMEM((WIDTH, WIDTH), BF16), VMEM((WIDTH, WIDTH), BF16),
            VMEM((8, 256), F32), VMEM((ROWS, WIDTH), BF16),
            DMA((4, SUBS)), DMA((SUBS,)), DMA((4, SUBS)), DMA((3, SUBS)), DMA((SUBS,)), DMA((4, SUBS)), DMA,
            DMA, DMA((2,)), DMA((4,)), DMA((4,)), DMA, DMA((2,)), DMA, DMA, DMA, DMA,
            DMA((4, SUBS)), DMA((4, SUBS, 3)), DMA, DMA, DMA((12,)),
        ],
        compiler_params=pltpu.CompilerParams(collective_id=0, has_side_effects=True, vmem_limit_bytes=60 << 20),
        name="collect",
    )(x, wq, wk, wv, b, order, mask, up, down, out, extra)


def greet_exchange(barrier):
    dp, mp, core, t = place()
    half, base = mp // 2, dp - core
    mine = lax.rem(mp, 2) * 2 + core
    for u in range(4):
        @pl.when((half != core) | (t != u))
        def _():
            pl.semaphore_signal(barrier, inc=1, device_id=chain_device(u, half, base), device_id_type=MESH)
    for g in range(4):
        @pl.when((half != core) | (mine != g))
        def _():
            pl.semaphore_signal(barrier, inc=1, device_id=worker(g, core, base), device_id_type=MESH)

    @pl.when(half == core)
    def _():
        pl.semaphore_wait(barrier, 6)

    @pl.when(half != core)
    def _():
        pl.semaphore_wait(barrier, 8)


def spread_kernel(a_ref, b_ref, oa_ref, ob_ref, send_sem, recv_sem, local_sem):
    dp, mp, core, t = place()
    half, base = mp // 2, dp - core
    mine = lax.rem(mp, 2) * 2 + core
    greet_exchange(pltpu.get_barrier_semaphore())
    for u in (3, 2, 1, 0):
        pair = ((a_ref.at[pl.ds(u * 1024, 1024)], oa_ref.at[mine]), (b_ref.at[pl.ds(u * 512, 512)], ob_ref.at[mine]))
        for k, (src, dst) in enumerate(pair):
            @pl.when((half != core) | (t != u))
            def _():
                send(src, dst, send_sem.at[u, k], recv_sem.at[mine, k], chain_device(u, half, base))

            @pl.when((half == core) & (t == u))
            def _():
                pltpu.make_async_copy(src, dst, local_sem.at[k]).start()
    for u in range(4):
        for k, src in enumerate((a_ref.at[pl.ds(u * 1024, 1024)], b_ref.at[pl.ds(u * 512, 512)])):
            @pl.when((half != core) | (t != u))
            def _():
                pltpu.make_async_copy(src, src, send_sem.at[u, k]).wait()
    for g in range(4):
        for k, dst in enumerate((oa_ref.at[g], ob_ref.at[g])):
            @pl.when((half != core) | (mine != g))
            def _():
                pltpu.make_async_copy(dst, dst, recv_sem.at[g, k]).wait()

            @pl.when((half == core) & (mine == g))
            def _():
                pltpu.make_async_copy(dst, dst, local_sem.at[k]).wait()


def spread(a, b):
    return pl.pallas_call(
        spread_kernel,
        out_shape=[jax.ShapeDtypeStruct((4, 1024, C), BF16), jax.ShapeDtypeStruct((4, 512, C), BF16)],
        in_specs=[ANY, ANY],
        out_specs=[ANY, ANY],
        scratch_shapes=[DMA((4, 2)), DMA((4, 2)), DMA((2,))],
        compiler_params=pltpu.CompilerParams(collective_id=1, has_side_effects=True),
        name="spread",
    )(a, b)


def regroup_kernel(a_ref, b_ref, oa_ref, ob_ref, send_sem, recv_sem, local_sem):
    dp, mp, core, t = place()
    half, base = mp // 2, dp - core
    mine = lax.rem(mp, 2) * 2 + core
    greet_exchange(pltpu.get_barrier_semaphore())
    big = lambda u: oa_ref.at[pl.ds(u * 1024, 1024)]
    small = lambda u: ob_ref.at[pl.ds(u * 512, 512)]
    for g in (0, 1, 2, 3):
        for k, (src, dst) in enumerate(((a_ref.at[g], big(t)), (b_ref.at[g], small(t)))):
            @pl.when((half != core) | (mine != g))
            def _():
                send(src, dst, send_sem.at[g, k], recv_sem.at[t, k], worker(g, core, base))

            @pl.when((half == core) & (mine == g))
            def _():
                pltpu.make_async_copy(src, dst, local_sem.at[k]).start()
    for g in range(4):
        for k, src in enumerate((a_ref.at[g], b_ref.at[g])):
            @pl.when((half != core) | (mine != g))
            def _():
                pltpu.make_async_copy(src, src, send_sem.at[g, k]).wait()
    for u in range(4):
        for k, dst in enumerate((big(u), small(u))):
            @pl.when((half != core) | (t != u))
            def _():
                pltpu.make_async_copy(dst, dst, recv_sem.at[u, k]).wait()

            @pl.when((half == core) & (t == u))
            def _():
                pltpu.make_async_copy(dst, dst, local_sem.at[k]).wait()


def regroup(a, b):
    return pl.pallas_call(
        regroup_kernel,
        out_shape=[jax.ShapeDtypeStruct((4096, C), BF16), jax.ShapeDtypeStruct((2048, C), BF16)],
        in_specs=[ANY, ANY],
        out_specs=[ANY, ANY],
        scratch_shapes=[DMA((4, 2)), DMA((4, 2)), DMA((2,))],
        compiler_params=pltpu.CompilerParams(collective_id=2, has_side_effects=True),
        name="regroup",
    )(a, b)


def settle_kernel(d0_ref, d1_ref, d2_ref, xs_ref, w_ref, extra_ref, mine_ref, out_ref, *rest):
    pieces_out, rest = rest[:8], rest[8:]
    (heads_ref, grads_ref, stage, pair_in, chain_in, gw, gwl, h_in, z_in, z_out,
                  pair_recv, pair_send, chain_recv, chain_send, relay_send,
                  s_recv, s_send, c_recv, c_send, h_recv, h_send, z_recv, z_send, q_recv, q_send, out_sem) = rest
    dp, mp, core, t = place()
    base, spot = dp - core, lax.rem(dp, 8) // 2
    step = 1 - 2 * core
    partner, lower, upper = at(dp + step, mp), at(dp, mp - step), at(dp, mp + step)
    group = lax.rem(mp, 2) * 2 + core
    gives = core == lax.rem(mp, 2)
    quarter = lambda q: pl.ds(pl.multiple_of(q * QUARTER, QUARTER), QUARTER)
    share = lambda j, parity: grads_ref.at[pl.ds(pl.multiple_of((2 * j + parity) * SHARE, SHARE), SHARE)]

    greet(pltpu.get_barrier_semaphore(), True)

    grads_ref[pl.ds(pl.multiple_of((2 * spot + core) * SHARE, SHARE), SHARE), :] = mine_ref[...]
    for rel in (1, 2, 3):
        send(mine_ref, share(spot, core), s_send.at[rel], s_recv.at[rel], at(mate(dp, rel), mp))

    def weight_gradients():
        gw[...] = jnp.zeros_like(gw)

        def part(i, sums):
            rows = pl.ds(pl.multiple_of(i * SUB, SUB), SUB)
            x = xs_ref[rows, :]
            new = []
            for h, d_ref in enumerate((d0_ref, d1_ref, d2_ref)):
                d = d_ref[rows, :]
                gw[pl.ds(h * 256, 256), :] += dot(d, x, 0, 0)
                new.append(sums[h] + jnp.sum(d.astype(F32), axis=0, keepdims=True))
            return tuple(new)

        sums = lax.fori_loop(0, 4 * ROWS // SUB, part, tuple(jnp.zeros((1, 256), F32) for _ in range(3)))
        gwl[...] = gw[...].astype(BF16)
        for h in range(3):
            line = jnp.concatenate([sums[h], jnp.zeros((1, WIDTH - 256), F32)], axis=1)
            spare = h * 256 + (192 if h == 1 else 128)
            gwl[pl.ds(spare, 16), :] = jnp.concatenate([line, jnp.zeros((15, WIDTH), F32)], axis=0).astype(BF16)
        for rel in (1, 2, 3):
            send(gwl.at[quarter(spot ^ rel)], h_in.at[rel], h_send.at[rel], h_recv.at[rel], at(mate(dp, rel), mp))

    def plane_sum():
        for rel in (1, 2, 3):
            wait(h_in.at[rel], h_recv.at[rel])
        half_sum = gwl[quarter(spot), :].astype(F32)
        for rel in (1, 2, 3):
            half_sum += h_in[rel].astype(F32)
        z_out[...] = half_sum.astype(BF16)

        @pl.when(mp != group)
        def _():
            send(z_out, z_in.at[mp // 2], z_send, z_recv.at[mp // 2], at(dp, group))

    tt = jnp.minimum(t, 3 - t)
    for i in range(3):
        u = lax.rem(3 - i + tt, 4)
        for s in range(SUBS):
            rows = pl.ds(pl.multiple_of(u * ROWS + s * SUB, SUB), SUB)
            value = jnp.zeros((SUB, WIDTH), F32)
            for h, d_ref in enumerate((d0_ref, d1_ref, d2_ref)):
                value += jnp.dot(d_ref[rows, :], w_ref[pl.ds(h * 256, 256), :], preferred_element_type=F32)

            @pl.when(t >= 2)
            def _():
                stage[rows, :] = value.astype(BF16)
                send(stage.at[rows], pair_in.at[rows], pair_send.at[i, s], pair_recv.at[i, s], partner)

            @pl.when(t <= 1)
            def _():
                wait(pair_in.at[rows], pair_recv.at[i, s])
                here = value + pair_in[rows, :].astype(F32)
                if i == 0:
                    stage[rows, :] = here.astype(BF16)
                else:
                    @pl.when(t == 1)
                    def _():
                        wait(chain_in.at[rows], chain_recv.at[u, s])
                        stage[rows, :] = (here + chain_in[rows, :].astype(F32)).astype(BF16)

                    @pl.when(t == 0)
                    def _():
                        stage[rows, :] = here.astype(BF16)

                @pl.when((t == 0) | (i > 0))
                def _():
                    send(stage.at[rows], chain_in.at[rows], chain_send.at[i, s], chain_recv.at[u, s], upper)

                if i == 0:
                    @pl.when(t == 1)
                    def _():
                        send(stage.at[rows], chain_in.at[rows], chain_send.at[i, s], chain_recv.at[u, s], lower)

        if i < 2:
            @pl.when(t == 1)
            def _():
                (weight_gradients, plane_sum)[i]()

    @pl.when(t != 1)
    def _():
        weight_gradients()

    for rel in (1, 2, 3):
        wait(share(spot ^ rel, core), s_recv.at[rel])
    for j in range(4):
        send(share(j, core), share(j, core), c_send.at[j], c_recv.at[j], partner)

    @pl.when(t == 2)
    def _():
        for s in range(SUBS):
            rows = pl.ds(3 * ROWS + s * SUB, SUB)
            wait(chain_in.at[rows], chain_recv.at[3, s])
            send(chain_in.at[rows], chain_in.at[rows], relay_send.at[s], chain_recv.at[3, s], upper)
            if s == 0:
                plane_sum()

    @pl.when((t == 0) | (t == 3))
    def _():
        plane_sum()

    for s in range(SUBS):
        rows = pl.ds(pl.multiple_of(tt * ROWS + s * SUB, SUB), SUB)
        cut = pl.ds(s * SUB, SUB)
        value = jnp.zeros((SUB, WIDTH), F32)
        for h, d_ref in enumerate((d0_ref, d1_ref, d2_ref)):
            value += jnp.dot(d_ref[rows, :], w_ref[pl.ds(h * 256, 256), :], preferred_element_type=F32)

        @pl.when(t >= 2)
        def _():
            stage[rows, :] = value.astype(BF16)
            send(stage.at[rows], pair_in.at[rows], pair_send.at[3, s], pair_recv.at[3, s], partner)

        @pl.when(t <= 1)
        def _():
            stage[rows, :] = value.astype(BF16)

    @pl.when(gives)
    def _():
        both = jnp.zeros((QUARTER, WIDTH), F32)
        for far in (0, 1):
            source = mp // 2 + 2 * far

            @pl.when(source == mp)
            def _():
                z_in[far] = z_out[...]

            @pl.when(source != mp)
            def _():
                wait(z_in.at[far], z_recv.at[far])

            both += z_in[far].astype(F32)
        heads_ref[quarter(spot), :] = both.astype(BF16)
        mine = heads_ref.at[quarter(spot)]
        send(mine, mine, q_send.at[0], q_recv.at[spot], partner)
        for rel in (1, 2, 3):
            send(mine, mine, q_send.at[rel], q_recv.at[spot], at(mate(dp, rel), mp))
            send(mine, mine, q_send.at[rel + 3], q_recv.at[spot], at(mate(dp, rel) + step, mp))

    for s in range(SUBS):
        cut = pl.ds(s * SUB, SUB)
        rows = pl.ds(pl.multiple_of(t * ROWS + s * SUB, SUB), SUB)
        wait(chain_in.at[rows], chain_recv.at[t, s])
        value = extra_ref[cut, :] + chain_in[rows, :].astype(F32)

        @pl.when(t <= 1)
        def _():
            wait(pair_in.at[rows], pair_recv.at[3, s])
            out_ref[cut, :] = (value + stage[rows, :].astype(F32) + pair_in[rows, :].astype(F32)).astype(BF16)

        @pl.when(t >= 2)
        def _():
            out_ref[cut, :] = value.astype(BF16)

    for q in range(4):
        @pl.when(jnp.logical_not(gives) | (spot != q))
        def _():
            wait(heads_ref.at[quarter(q)], q_recv.at[q])
    for j in range(4):
        wait(share(j, 1 - core), c_recv.at[j])
    copies = []
    for first, rows, n in ((0, 768, 3), (768, 768, 4), (OUT_ROW, 192, 5), (BIAS_ROW, 64, 6)):
        copies.append(pltpu.make_async_copy(grads_ref.at[pl.ds(first, rows)], pieces_out[n], out_sem.at[n]))
    for h in range(3):
        for n, where in enumerate((0, 2, 1) if h == 1 else (1, 3, 0)):
            src = heads_ref.at[pl.ds((4 * h + where) * HD, HD)]
            copies.append(pltpu.make_async_copy(src, pieces_out[n].at[pl.ds(h * HD, HD)], out_sem.at[8 + 3 * h + n]))
        src = heads_ref.at[pl.ds(h * 256 + (192 if h == 1 else 128), 16)]
        copies.append(pltpu.make_async_copy(src, pieces_out[7].at[h], out_sem.at[17 + h]))
    for copy in copies:
        copy.start()

    for s in range(SUBS):
        piece = stage.at[pl.ds(s * SUB, SUB)]

        @pl.when(t >= 2)
        def _():
            for i in range(4):
                wait(piece, pair_send.at[i, s])

        @pl.when(t <= 1)
        def _():
            for i in range(3):
                wait(piece, chain_send.at[i, s])

        @pl.when(t == 2)
        def _():
            wait(piece, relay_send.at[s])
    for rel in (1, 2, 3):
        wait(mine_ref, s_send.at[rel])
        wait(z_out, h_send.at[rel])
    for j in range(4):
        wait(mine_ref, c_send.at[j])

    @pl.when(mp != group)
    def _():
        wait(z_out, z_send)

    @pl.when(gives)
    def _():
        for k in range(7):
            wait(z_out, q_send.at[k])

    for copy in copies:
        copy.wait()


def settle(d0, d1, d2, xs, w, extra, mine):
    return pl.pallas_call(
        settle_kernel,
        out_shape=[sds((ROWS, WIDTH), BF16)] + [sds((rows, WIDTH), BF16) for rows in (192, 192, 192, 768, 768, 192, 64)]
        + [sds((3, 16, WIDTH), BF16)],
        in_specs=[VM] * 7,
        out_specs=[VM] + [ANY] * 8,
        scratch_shapes=[VMEM((WIDTH, WIDTH), BF16), VMEM((PACK, WIDTH), BF16)] + [VMEM((4 * ROWS, WIDTH), BF16)] * 3 + [
            VMEM((WIDTH, WIDTH), F32), VMEM((WIDTH, WIDTH), BF16), VMEM((4, QUARTER, WIDTH), BF16), VMEM((2, QUARTER, WIDTH), BF16),
            VMEM((QUARTER, WIDTH), BF16),
            DMA((4, SUBS)), DMA((4, SUBS)), DMA((4, SUBS)), DMA((3, SUBS)), DMA((SUBS,)),
            DMA((4,)), DMA((4,)), DMA((4,)), DMA((4,)), DMA((4,)), DMA((4,)), DMA((2,)), DMA, DMA((4,)), DMA((7,)), DMA((20,)),
        ],
        compiler_params=pltpu.CompilerParams(collective_id=3, has_side_effects=True, vmem_limit_bytes=60 << 20),
        name="settle",
    )(d0, d1, d2, xs, w, extra, mine)


EPS = 1e-12
CHUNK = 512
FF_MODEL = 768


def gelu_and_slope(v):
    size = jnp.abs(v)
    u = 1.0 / (1.0 + (0.3275911 * 0.7071067811865476) * size)
    bell = jnp.exp(-0.5 * v * v)
    poly = u * (0.127414796 + u * (-0.142248368 + u * (0.7107068705 + u * (-0.7265760135 + u * 0.5307027145))))
    tail = poly * bell
    cdf = jnp.where(v < 0, tail, 1.0 - tail)
    return v * cdf, cdf + v * (bell * 0.3989422804014327)


def row_mean(v):
    return jnp.sum(v, axis=-1, keepdims=True) * (1.0 / FF_MODEL)


def ffn_kernel(c01_ref, c2_ref, tok_ref, cot_ref, vec_ref, *rest):
    pieces, rest = (rest[0], rest[1], rest[2].at[0], rest[2].at[1]), rest[3:]
    (out_ref, res_ref, g01_ref, g2_ref, keep_ref, give_ref,
     w, wout, ctx, x, x_t, gf, act, slope, zhat, acc, rstd, cols, recv,
     w_local, w_send, w_recv, g_send, g_recv, out_sem) = rest
    dp, mp, core, t = place()
    partner = at(dp + 1 - 2 * core, mp)
    spot = lax.rem(dp, 8) // 2
    barrier = pltpu.get_barrier_semaphore()
    pl.semaphore_signal(barrier, inc=1, device_id=partner, device_id_type=MESH)
    pl.semaphore_wait(barrier, 1)

    def rows_of(shard, j, parity):
        return w.at[shard, pl.ds(pl.multiple_of((2 * j + parity) * SHARE, SHARE), SHARE)]

    def bring(j, piece):
        for k in range(4):
            src = pieces[piece].at[k]
            shard = lax.rem(mp - k + 4, 4)
            pltpu.make_async_copy(src, rows_of(shard, j, core), w_local.at[j, shard]).start()
            send(src, rows_of(shard, j, core), w_send.at[j, shard], w_recv.at[j, shard], partner)

    for own in range(4):
        for c in range(2):
            @pl.when((spot == own) & (core == c))
            def _():
                for j in (3, 0, 1, 2):
                    rel = j ^ own
                    bring(j, rel if rel in (0, 3) or c == 0 else 3 - rel)

    lane = lax.broadcasted_iota(jnp.int32, (1, C), 1)
    for g in range(4):
        ctx[:, pl.ds(g * C, C)] = c01_ref[g]
    for g in (0, 2):
        a, b = c2_ref[g].astype(F32), c2_ref[g + 1].astype(F32)
        col = pl.ds(4 * C + g * HD, C)
        ctx[pl.ds(0, 512), col] = jnp.where(lane < HD, a, pltpu.roll(b, HD, 1)).astype(BF16)
        ctx[pl.ds(512, 512), col] = jnp.where(lane < HD, pltpu.roll(a, HD, 1), b).astype(BF16)

    def wait_weights(j):
        for shard in range(4):
            ref = w.at[shard, pl.ds(0, SHARE)]
            pltpu.make_async_copy(ref, ref, w_local.at[j, shard]).wait()
            pltpu.make_async_copy(ref, ref, w_recv.at[j, shard]).wait()

    wait_weights(3)
    for m in range(4):
        wout[pl.ds(m * C, C), :] = w[m, pl.ds(OUT_ROW, C), :]
        wout[pl.ds(4 * C + m * HD, HD), :] = w[m, pl.ds(OUT_ROW + C, HD), :]

    cols[...] = jnp.zeros_like(cols)
    b_out, gain1, bias1, b_down, gain2, bias2 = (vec_ref[pl.ds(i, 1), :] for i in range(6))

    def first_norm(r, _):
        rows = pl.ds(pl.multiple_of(r * CHUNK, CHUNK), CHUNK)
        h = jnp.dot(ctx[rows, :], wout[...], preferred_element_type=F32) + tok_ref[rows, :].astype(F32) + b_out
        h = h - row_mean(h)
        scale = lax.rsqrt(row_mean(h * h) + EPS)
        rstd[rows, :] = scale
        h = h * scale
        zhat[rows, :] = h
        first = h * gain1 + bias1
        acc[rows, :] = first + b_down
        x[rows, :] = first.astype(BF16)
        x_t[:, rows] = first.T.astype(BF16)

        return 0

    lax.fori_loop(0, 1024 // CHUNK, first_norm, 0)
    for j in range(3):
        wait_weights(j)

    def forward(r, _):
        rows = pl.ds(pl.multiple_of(r * CHUNK, CHUNK), CHUNK)

        def up(m, f):
            cut = pl.ds(f * 256, 256)
            bias = w[m, pl.ds(BIAS_ROW, 16), cut].astype(F32)[0:1, :]
            pre = jnp.dot(x[rows, :], w[m, pl.ds(0, 768), cut], preferred_element_type=F32) + bias
            value, grad = gelu_and_slope(pre)
            act[m, rows, cut] = value.astype(BF16)
            slope[m, rows, cut] = grad.astype(BF16)

        def down(m):
            acc[rows, :] += jnp.dot(act[m, rows, :], w[m, pl.ds(768, 768), :], preferred_element_type=F32)

        for m in range(4):
            for f in range(3):
                up(m, f)
                if m and f == 0:
                    down(m - 1)
        down(3)

        z = acc[rows, :]
        z = z - row_mean(z)
        scale = lax.rsqrt(row_mean(z * z) + EPS)
        z = z * scale
        out_ref[rows, :] = (z * gain2 + bias2).astype(BF16)
        cot = cot_ref[rows, :].astype(F32)
        dz = cot * gain2
        gs = scale * (dz - row_mean(dz) - z * row_mean(dz * z))
        cols[pl.ds(2, 1), :] += jnp.sum(cot * z, axis=0, keepdims=True)
        cols[pl.ds(3, 1), :] += jnp.sum(cot, axis=0, keepdims=True)
        cols[pl.ds(5, 1), :] += jnp.sum(gs, axis=0, keepdims=True)
        acc[rows, :] = gs
        gf[rows, :] = gs.astype(BF16)
        return 0

    lax.fori_loop(0, 1024 // CHUNK, forward, 0)

    def give(m, j):
        cut = pl.ds(pl.multiple_of((2 * j + 1 - core) * SHARE, SHARE), SHARE)
        send(w.at[m, cut], recv.at[m, j], g_send.at[m, j], g_recv.at[m, j], partner)

    for j in range(4):
        for shard in range(4):
            ref = w.at[shard, pl.ds(0, SHARE)]
            pltpu.make_async_copy(ref, ref, w_send.at[j, shard]).wait()

    def backward(m, _):
        def rows_back(r, _):
            rows = pl.ds(pl.multiple_of(r * CHUNK, CHUNK), CHUNK)
            for f in range(3):
                cut = pl.ds(f * 256, 256)
                ga = dot(gf[rows, :], w[m, pl.ds(768 + f * 256, 256), :], 1, 1)
                slope[m, rows, cut] = (ga * slope[m, rows, cut].astype(F32)).astype(BF16)
            acc[rows, :] += dot(slope[m, rows, :], w[m, pl.ds(0, 768), :], 1, 1)
            return 0

        lax.fori_loop(0, 1024 // CHUNK, rows_back, 0)
        bias = []
        for f in range(3):
            cut = pl.ds(f * 256, 256)
            gp = slope[m, :, cut]
            w[m, pl.ds(0, 768), cut] = jnp.dot(x_t[...], gp, preferred_element_type=F32).astype(BF16)
            w[m, pl.ds(768 + f * 256, 256), :] = dot(act[m, :, cut], gf[...], 0, 0).astype(BF16)
            bias.append(jnp.sum(gp.astype(F32), axis=0, keepdims=True))
        cols[pl.ds(8 + m, 1), :] = jnp.concatenate(bias, axis=1)
        for j in range(3):
            give(m, j)
        return 0

    lax.fori_loop(0, 4, backward, 0)

    def first_back(r, _):
        rows = pl.ds(pl.multiple_of(r * CHUNK, CHUNK), CHUNK)
        grad = acc[rows, :]
        z = zhat[rows, :]
        dz = grad * gain1
        gr = rstd[rows, :] * (dz - row_mean(dz) - z * row_mean(dz * z))
        cols[pl.ds(0, 1), :] += jnp.sum(grad * z, axis=0, keepdims=True)
        cols[pl.ds(1, 1), :] += jnp.sum(grad, axis=0, keepdims=True)
        cols[pl.ds(4, 1), :] += jnp.sum(gr, axis=0, keepdims=True)
        res_ref[rows, :] = gr
        low = gr.astype(BF16)
        gf[rows, :] = low
        gc = dot(low, wout[...], 1, 1).astype(BF16)
        for g in range(4):
            g01_ref[g, rows, :] = gc[:, g * C : g * C + C]
        ctx_grad[rows, :] = gc[:, 4 * C :]
        return 0

    ctx_grad = x
    ctx_grad = x.at[:, pl.ds(0, 2 * C)]
    lax.fori_loop(0, 1024 // CHUNK, first_back, 0)
    for g in (0, 2):
        top = ctx_grad[pl.ds(0, 512), pl.ds(g * HD, C)].astype(F32)
        low = ctx_grad[pl.ds(512, 512), pl.ds(g * HD, C)].astype(F32)
        g2_ref[g] = jnp.where(lane < HD, top, pltpu.roll(low, HD, 1)).astype(BF16)
        g2_ref[g + 1] = jnp.where(lane < HD, pltpu.roll(top, HD, 1), low).astype(BF16)

    for n in range(3):
        cut = pl.ds(n * 256, 256)
        part = dot(ctx[:, cut], gf[...], 0, 0).astype(BF16)
        if n < 2:
            for i in range(2):
                w[2 * n + i, pl.ds(OUT_ROW, C), :] = part[i * C : i * C + C, :]
        else:
            for i in range(4):
                w[i, pl.ds(OUT_ROW + C, HD), :] = part[i * HD : i * HD + HD, :]
    for m in range(4):
        w[m, pl.ds(BIAS_ROW, 16), :] = jnp.concatenate(
            [cols[pl.ds(8 + m, 1), :], cols[pl.ds(0, 6), :], jnp.zeros((9, FF_MODEL), F32)], axis=0
        ).astype(BF16)
        give(m, 3)

    for rel in (3, 2, 1, 0):
        j = spot ^ rel
        along = jnp.where(core == 0, rel % 2, rel // 2)
        across = jnp.where(core == 0, rel // 2, rel % 2)
        for m in range(4):
            wait(recv.at[m, j], g_recv.at[m, j])
            cut = pl.ds(pl.multiple_of((2 * j + core) * SHARE, SHARE), SHARE)
            recv[m, j] = (recv[m, j].astype(F32) + w[m, cut, :].astype(F32)).astype(BF16)
            for side, ref in enumerate((keep_ref, give_ref)):
                @pl.when(along == side)
                def _():
                    pltpu.make_async_copy(recv.at[m, j], ref.at[across, m], out_sem.at[m, rel]).start()
    for m in range(4):
        for j in range(4):
            wait(recv.at[m, j], out_sem.at[m, j])
            wait(recv.at[m, j], g_send.at[m, j])


def ffn(c01, c2, tokens, cot, vecs, pieces):
    dma = pltpu.SemaphoreType.DMA
    vm, any_ = pl.BlockSpec(memory_space=pltpu.VMEM), pl.BlockSpec(memory_space=pl.ANY)
    sds = jax.ShapeDtypeStruct
    return pl.pallas_call(
        ffn_kernel,
        out_shape=[sds((1024, 768), BF16), sds((1024, 768), F32), sds((4, 1024, C), BF16), sds((4, 512, C), BF16),
                   sds((2, 4, SHARE, 768), BF16), sds((2, 4, SHARE, 768), BF16)],
        in_specs=[vm] * 5 + [any_] * 3,
        out_specs=[vm] * 4 + [any_] * 2,
        scratch_shapes=[
            VMEM((4, PACK, 768), BF16), VMEM((768, 768), BF16),
            VMEM((1024, 768), BF16), VMEM((1024, 768), BF16), VMEM((768, 1024), BF16), VMEM((1024, 768), BF16),
            VMEM((4, 1024, 768), BF16), VMEM((4, 1024, 768), BF16),
            VMEM((1024, 768), F32), VMEM((1024, 768), F32), VMEM((1024, 1), F32), VMEM((16, 768), F32),
            VMEM((4, 4, SHARE, 768), BF16),
            dma((4, 4)), dma((4, 4)), dma((4, 4)), dma((4, 4)), dma((4, 4)), dma((4, 4)),
        ],
        compiler_params=pltpu.CompilerParams(collective_id=4, has_side_effects=True, vmem_limit_bytes=63 << 20),
        name="ffn",
    )(c01, c2, tokens, cot, vecs, *pieces)


def swap(value, even_bits, odd_bits, n_dp):
    return lax.ppermute(value, "dp", [(d, d ^ (odd_bits if d % 2 else even_bits)) for d in range(n_dp)])


def pick(value, index, axis):
    return lax.dynamic_index_in_dim(value, index, axis, keepdims=False)


def total(a, b):
    return (a.astype(F32) + b.astype(F32)).astype(BF16)


def tie(*values):
    return lax.optimization_barrier(values)


def body(n_dp, tokens, w_query, b_query, w_key, w_value, b_value, w_out, b_out, norm1_gain, norm1_bias, w_up, b_up, w_down,
         b_down, norm2_gain, norm2_bias, key_mask, cluster_order, cotangent):
    dp, mp, core, t = place()
    ring = lambda k: [(z, (z + k) % 4) for z in range(4)]

    order = 2 * jnp.where(core == 1, cluster_order ^ 3072, cluster_order).reshape(3 * L)
    bq, bv, bz = b_query.reshape(3, HD), b_value.reshape(3, HD), jnp.zeros((C,), F32)
    b_heads = jnp.stack([jnp.concatenate([bq[h], bv[h], bz] if h == 1 else [bv[h], bq[h], bz]) for h in range(3)])
    b_heads = jnp.concatenate([b_heads, jnp.zeros((5, 256), F32)])
    extra = jnp.concatenate([b_up.reshape(1, WIDTH), jnp.zeros((PACK - BIAS_ROW - 1, WIDTH), BF16)])

    xs, qkv, w_heads, order, mask, share = collect(
        tokens, w_query.T, w_key.T, w_value.T, b_heads, order, key_mask, w_up, w_down, w_out, extra
    )
    qkv, share = tie(qkv, share)
    shares = [share] + [lax.ppermute(share, "mp", ring(i)) for i in (1, 2, 3)]
    c01, ts01, probs01 = attend(0, order, mask, qkv)
    c01, *shares = tie(c01, *shares)
    near = jnp.stack(shares)
    next_to = swap(near, 2, 4, n_dp)
    c2, ts2, probs2 = attend(2, order, mask, qkv)
    c2, near, next_to = tie(c2, near, next_to)
    far = swap(jnp.stack([near, next_to]), 4, 2, n_dp)
    c01, c2 = spread(c01, c2)

    vecs = jnp.stack([b_out, norm1_gain, norm1_bias, b_down, norm2_gain, norm2_bias, b_out, b_out])
    layer_out, grad_residual, g01, g2, keep, give = ffn(c01, c2, tokens, cotangent, vecs, (near, next_to, far))

    got = swap(give, 2, 4, n_dp)
    g01, g2 = regroup(g01, g2)
    d0 = attend_back(0, order, g01, ts01, probs01)
    d0, keep, got = tie(d0, keep, got)
    keep, give = total(keep[0], got[0]), total(keep[1], got[1])
    got = swap(give, 4, 2, n_dp)
    d1 = attend_back(1, order, g01, ts01, probs01)
    d1, keep, got = tie(d1, keep, got)
    sums = total(keep, got)
    for bit in range(3, n_dp.bit_length() - 1):
        sums = total(sums, swap(sums, 1 << bit, 1 << bit, n_dp))
    parts = [pick(sums, mp, 0)]
    for i in (1, 2, 3):
        parts.append(lax.ppermute(pick(sums, (mp + i) % 4, 0), "mp", ring(i)))
    d2 = attend_back(2, order, g2, ts2, probs2)
    d2, *parts = tie(d2, *parts)
    mine = sum(p.astype(F32) for p in parts).astype(BF16)
    grad_tokens, *sums = settle(d0, d1, d2, xs, w_heads, grad_residual, mine)
    hq, hk, hv, g_up, g_down, g_out, small, spare = (s.astype(F32) for s in sums)
    for bit in range(3, n_dp.bit_length() - 1):
        hq, hk, hv, spare = (s + swap(s, 1 << bit, 1 << bit, n_dp) for s in (hq, hk, hv, spare))
    sums_of = lambda where: jnp.concatenate([spare[h, 0, where[h] : where[h] + HD] for h in range(3)])
    vec = lambda i: small[i]
    return (
        layer_out,
        grad_tokens,
        hq.T,
        sums_of((HD, 0, HD)),
        hk.T,
        hv.T,
        sums_of((0, HD, 0)),
        g_out,
        vec(5),
        vec(1),
        vec(2),
        g_up,
        vec(0),
        g_down,
        vec(6),
        vec(3),
        vec(4),
    )


def solution(mesh):
    return jax.shard_map(
        functools.partial(body, mesh.shape["dp"]),
        mesh=mesh,
        in_specs=(
            P(("dp", "mp"), None), P(None, "mp"), P("mp"), P(None, "mp"), P(None, "mp"), P("mp"), P("mp", None), P(), P(), P(),
            P(None, "mp"), P("mp"), P("mp", None), P(), P(), P(), P("dp", None), P("dp", "mp", None), P(("dp", "mp"), None),
        ),
        out_specs=(
            P(("dp", "mp"), None), P(("dp", "mp"), None), P(None, "mp"), P("mp"), P(None, "mp"), P(None, "mp"), P("mp"),
            P("mp", None), P(), P(), P(), P(None, "mp"), P("mp"), P("mp", None), P(), P(), P(),
        ),
        check_vma=False,
    )
```

```python
import functools
import jax
import jax.numpy as jnp
from jax import lax
from jax.experimental import pallas as pl
from jax.experimental.pallas import tpu as pltpu
from jax.sharding import PartitionSpec as P

L = 4096
C = 128
HD = 64
GROUP = 2
STEP = 1024
GROUPS = STEP // (GROUP * C)
F32 = jnp.float32
BF16 = jnp.bfloat16
VMEM = pltpu.VMEM


def dot(a, b, da, db):
    return lax.dot_general(a, b, (((da,), (db,)), ((), ())), preferred_element_type=F32)


def in_turn(gather, compute, scatter, bufs, outs):
    gather(0, bufs[0])
    for group in range(GROUPS):
        if group + 1 < GROUPS:
            gather(group + 1, bufs[(group + 1) % 2])
        compute(group, bufs[group % 2], outs[group % 2])
        if group:
            scatter(group - 1, outs[(group - 1) % 2])
    scatter(GROUPS - 1, outs[(GROUPS - 1) % 2])


def attend_kernel(first, ord_ref, mask_ref, qkv_ref, c_ref, ts_ref, pr_ref, src, ctx, *slots):
    head, step = pl.program_id(0) + first, pl.program_id(1)
    live = jnp.sum(mask_ref[...].astype(F32), axis=1, keepdims=True).astype(jnp.int32)

    @pl.when(step == 0)
    def _():
        src[pl.ds(0, L, stride=2), :] = qkv_ref[0, :, :C].astype(F32)
        src[pl.ds(1, L, stride=2), :] = qkv_ref[0, :, C:].astype(F32)

    def gather(group, buf):
        for u in range(GROUP * C):
            buf[pl.ds(2 * u, 2), :] = src[pl.ds(pl.multiple_of(ord_ref[group * GROUP * C + u], 2), 2), :]

    def compute(group, buf, out):
        each = range(GROUP)
        rows = [pl.ds((group * GROUP + i) * C, C) for i in each]
        t0 = [buf[pl.ds(2 * i * C, C, stride=2), :].astype(BF16) for i in each]
        t1 = [buf[pl.ds(2 * i * C + 1, C, stride=2), :].astype(BF16) for i in each]
        for i in each:
            ts_ref[0, rows[i], :C] = t0[i]
            ts_ref[0, rows[i], C:] = t1[i]
        slot = [step * STEP + (group * GROUP + i) * C + lax.broadcasted_iota(jnp.int32, (C, C), 0) for i in each]
        scores = [dot(t1[i], t0[i], 1, 1) * 0.125 + jnp.where(slot[i] < live, 0.0, -10000.0) for i in each]
        e = [jnp.exp(scores[i] - jnp.max(scores[i], axis=0, keepdims=True)) for i in each]
        probs = [e[i] * (1.0 / jnp.sum(e[i], axis=0, keepdims=True)) for i in each]
        for i in each:
            pr_ref[0, rows[i], :] = probs[i]
        for i in each:
            out[pl.ds(i * C, C), :] = dot(probs[i].astype(BF16), t0[i], 0, 0)

    def scatter(group, out):
        for u in range(GROUP * C):
            ctx[pl.ds(ord_ref[group * GROUP * C + u], 1), :] = out[pl.ds(u, 1), :]

    in_turn(gather, compute, scatter, slots[:2], slots[2:])

    @pl.when(step == L // STEP - 1)
    def _():
        lane = lax.broadcasted_iota(jnp.int32, (1, C), 1)
        if first == 2:
            for k in range(4):
                low = ctx[pl.ds(k * 2048, 512, stride=2), :]
                high = pltpu.roll(ctx[pl.ds(k * 2048 + 1024, 512, stride=2), :], HD, 1)
                c_ref[pl.ds(k * 512, 512), :] = jnp.where(lane < HD, low, high).astype(BF16)
        else:
            rows = ctx[pl.ds(0, L, stride=2), :].astype(BF16)

            @pl.when(head == 0)
            def _():
                c_ref[...] = rows

            @pl.when(head == 1)
            def _():
                c_ref[...] = jnp.where(lane < HD, c_ref[...], rows)


def attend(first, order, mask, qkv):
    heads = 2 if first == 0 else 1
    whole = lambda shape: pl.BlockSpec(shape, lambda h, i: (0,) * len(shape), pipeline_mode=pl.Buffered(1))
    per_step = lambda width: pl.BlockSpec((1, STEP, width), lambda h, i: (h, i, 0))
    steps = L // STEP
    out_rows = L if first == 0 else L // 2
    return pl.pallas_call(
        functools.partial(attend_kernel, first),
        grid=(heads, steps),
        in_specs=[
            pl.BlockSpec((STEP,), lambda h, i: ((h + first) * steps + i,), memory_space=pltpu.SMEM),
            whole((1, L)),
            pl.BlockSpec((1, L, 2 * C), lambda h, i: (h + first, 0, 0)),
        ],
        out_specs=[whole((out_rows, C)), per_step(2 * C), per_step(C)],
        out_shape=[
            jax.ShapeDtypeStruct((out_rows, C), BF16),
            jax.ShapeDtypeStruct((heads, L, 2 * C), BF16),
            jax.ShapeDtypeStruct((heads, L, C), F32),
        ],
        scratch_shapes=[VMEM((2 * L, C), F32), VMEM((2 * L, C), F32)]
        + [VMEM((2 * GROUP * C, C), F32)] * 2 + [VMEM((GROUP * C, C), F32)] * 2,
        compiler_params=pltpu.CompilerParams(vmem_limit_bytes=60 << 20),
        cost_estimate=pl.CostEstimate(flops=heads * 9 * 10**9, bytes_accessed=10 << 20, transcendentals=0),
        name="attend",
    )(order, mask, qkv)


def attend_back_kernel(head, ord_ref, g_ref, ts_ref, pr_ref, d_ref, gsrc, dst, *slots):
    step = pl.program_id(0)
    lane = lax.broadcasted_iota(jnp.int32, (1, C), 1)

    @pl.when(step == 0)
    def _():
        if head == 2:
            for k in range(4):
                both = g_ref[pl.ds(k * 512, 512), :].astype(F32)
                gsrc[pl.ds(k * 2048, 512, stride=2), :] = both
                gsrc[pl.ds(k * 2048 + 1024, 512, stride=2), :] = pltpu.roll(both, HD, 1)
        else:
            gsrc[pl.ds(0, L, stride=2), :] = g_ref[...].astype(F32)

    keep = (lane >= HD) if head == 1 else (lane < HD)

    def gather(group, buf):
        for u in range(GROUP * C):
            buf[pl.ds(u, 1), :] = gsrc[pl.ds(ord_ref[group * GROUP * C + u], 1), :]

    def compute(group, buf, out):
        each = range(GROUP)
        rows = [pl.ds((group * GROUP + i) * C, C) for i in each]
        t0 = [ts_ref[0, rows[i], :C] for i in each]
        t1 = [ts_ref[0, rows[i], C:] for i in each]
        probs = [pr_ref[0, rows[i], :] for i in each]
        g = [jnp.where(keep, buf[pl.ds(i * C, C), :], 0.0).astype(BF16) for i in each]
        dp = [dot(t0[i], g[i], 1, 1) for i in each]
        ds = [(probs[i] * (dp[i] - jnp.sum(probs[i] * dp[i], axis=0, keepdims=True))).astype(BF16) for i in each]
        for i in each:
            grad = dot(ds[i], t1[i], 0, 0) * 0.125 + jnp.dot(probs[i].astype(BF16), g[i], preferred_element_type=F32)
            out[pl.ds(2 * i * C, C, stride=2), :] = grad
        for i in each:
            out[pl.ds(2 * i * C + 1, C, stride=2), :] = jnp.dot(ds[i], t0[i], preferred_element_type=F32) * 0.125

    def scatter(group, out):
        for u in range(GROUP * C):
            dst[pl.ds(pl.multiple_of(ord_ref[group * GROUP * C + u], 2), 2), :] = out[pl.ds(2 * u, 2), :]

    in_turn(gather, compute, scatter, slots[:2], slots[2:])

    @pl.when(step == L // STEP - 1)
    def _():
        d_ref[:, :C] = dst[pl.ds(0, L, stride=2), :].astype(BF16)
        d_ref[:, C:] = dst[pl.ds(1, L, stride=2), :].astype(BF16)


def attend_back(head, order, g, ts, probs):
    steps = L // STEP
    whole = lambda shape: pl.BlockSpec(shape, lambda i: (0,) * len(shape), pipeline_mode=pl.Buffered(1))
    per_step = lambda width: pl.BlockSpec((1, STEP, width), lambda i: (head % 2, i, 0))
    return pl.pallas_call(
        functools.partial(attend_back_kernel, head),
        grid=(steps,),
        in_specs=[
            pl.BlockSpec((STEP,), lambda i: (head * steps + i,), memory_space=pltpu.SMEM),
            whole(g.shape), per_step(2 * C), per_step(C),
        ],
        out_specs=whole((L, 2 * C)),
        out_shape=jax.ShapeDtypeStruct((L, 2 * C), BF16),
        scratch_shapes=[VMEM((2 * L, C), F32), VMEM((2 * L, C), F32)]
        + [VMEM((GROUP * C, C), F32)] * 2 + [VMEM((2 * GROUP * C, C), F32)] * 2,
        compiler_params=pltpu.CompilerParams(vmem_limit_bytes=60 << 20),
        cost_estimate=pl.CostEstimate(flops=9 * 10**9, bytes_accessed=10 << 20, transcendentals=0),
        name="attend_back",
    )(order, g, ts, probs)


MESH = pl.DeviceIdType.MESH
WIDTH = 768
ROWS = 1024
SUB = 512
SUBS = ROWS // SUB
SHARE = 208
SHARE_ALL = SHARE + 32
QUARTER = 192
DMA = pltpu.SemaphoreType.DMA
ANY = pl.BlockSpec(memory_space=pl.ANY)
VM = pl.BlockSpec(memory_space=pltpu.VMEM)
sds = jax.ShapeDtypeStruct


def place():
    dp, mp = lax.axis_index("dp"), lax.axis_index("mp")
    core = lax.rem(dp, 2)
    return dp, mp, core, jnp.where(core == 0, mp, 3 - mp)


def at(dp, mp):
    return {"dp": dp, "mp": mp}


def signal(barrier, device):
    pl.semaphore_signal(barrier, inc=1, device_id=device, device_id_type=MESH)


def send(src, dst, send_sem, recv_sem, device):
    copy = pltpu.make_async_remote_copy(
        src_ref=src, dst_ref=dst, send_sem=send_sem, recv_sem=recv_sem, device_id=device, device_id_type=MESH
    )
    copy.start()
    return copy


def wait(ref, sem):
    pltpu.make_async_copy(ref, ref, sem).wait()


def mate(dp, rel):
    return dp + 2 * ((lax.rem(dp, 8) // 2 ^ rel) - lax.rem(dp, 8) // 2)


def greet(barrier, both_cores):
    dp, mp, core, t = place()
    step = 1 - 2 * core
    for k in range(4):
        if k:
            signal(barrier, at(dp, lax.rem(mp + k, 4)))
        signal(barrier, at(dp + step, lax.rem(mp + k, 4)))
    for rel in (1, 2, 3):
        signal(barrier, at(mate(dp, rel), mp))
        if both_cores:
            signal(barrier, at(mate(dp, rel) + step, mp))
    pl.semaphore_wait(barrier, 13 if both_cores else 10)


def worker(group, half, dp_base):
    return at(dp_base + group % 2, 2 * half + group // 2)


def chain_device(u, half, dp_base):
    return at(dp_base + half, jnp.where(half == 0, u, 3 - u))


def collect_kernel(x_ref, wq_ref, wk_ref, wv_ref, bsrc_ref, osrc_ref, msrc_ref,
                   xs_ref, qkv_ref, w_ref, ord_ref, mask_ref,
                   xs, qkv, w, wsrc, bias, relay,
                   chain_recv, relay_recv, pair_recv, chain_send, relay_send, pair_send, own_sem,
                   wz_recv, wz_send, wp_recv, wp_send, b_recv, b_send, o_recv, o_send, m_recv, m_send, xs_out, qkv_out, w_out, build_sem):
    dp, mp, core, t = place()
    base, half, spot = dp - core, mp // 2, lax.rem(dp, 8) // 2
    step = 1 - 2 * core
    partner, lower, upper = at(dp + step, mp), at(dp, mp - step), at(dp, mp + step)
    group = lax.rem(mp, 2) * 2 + core
    gives = core == lax.rem(mp, 2)
    order_self = worker(mp, core, base)
    order_here = (order_self["dp"] == dp) & (order_self["mp"] == mp)
    cut = lambda s: pl.ds(s * SUB, SUB)
    home = lambda u, s: xs.at[pl.ds(pl.multiple_of(u * ROWS + s * SUB, SUB), SUB)]
    quarter = lambda q: pl.ds(pl.multiple_of(q * QUARTER, QUARTER), QUARTER)

    own = pltpu.make_async_copy(x_ref, xs.at[pl.ds(pl.multiple_of(jnp.minimum(t, 1) * ROWS, ROWS), ROWS)], own_sem)

    @pl.when(t <= 1)
    def _():
        own.start()

    parts = []
    for h in range(3):
        for n, part in enumerate((wq_ref, wv_ref, wk_ref, None) if h == 1 else (wv_ref, wq_ref, None, wk_ref)):
            rows = pl.ds((4 * h + n) * HD, HD)
            if part is None:
                wsrc[rows, :] = jnp.zeros((HD, WIDTH), BF16)
            else:
                copy = pltpu.make_async_copy(part.at[pl.ds(h * HD, HD)], wsrc.at[rows], build_sem.at[4 * h + n])
                copy.start()
                parts.append(copy)
    for copy in parts:
        copy.wait()

    greet(pltpu.get_barrier_semaphore(), False)

    for far in (0, 1):
        target = mp // 2 + 2 * far

        @pl.when(gives & (target != mp))
        def _():
            send(wsrc.at[quarter(spot)], w.at[quarter(spot)], wz_send.at[far], wz_recv, at(dp, target))
            send(bsrc_ref, bias, b_send.at[far], b_recv, at(dp, target))

        @pl.when(gives & (target == mp))
        def _():
            pltpu.make_async_copy(wsrc.at[quarter(spot)], w.at[quarter(spot)], wz_recv).start()
            pltpu.make_async_copy(bsrc_ref, bias, b_recv).start()

    @pl.when(order_here)
    def _():
        pltpu.make_async_copy(osrc_ref, ord_ref, o_recv).start()
        pltpu.make_async_copy(msrc_ref, mask_ref, m_recv).start()

    @pl.when(jnp.logical_not(order_here))
    def _():
        send(osrc_ref, ord_ref, o_send, o_recv, order_self)
        send(msrc_ref, mask_ref, m_send, m_recv, order_self)

    @pl.when(t == 3)
    def _():
        for s in range(SUBS):
            send(x_ref.at[cut(s)], relay.at[cut(s)], chain_send.at[0, s], relay_recv.at[s], lower)

    @pl.when((t == 1) | (t == 2))
    def _():
        for s in range(SUBS):
            send(x_ref.at[cut(s)], home(t, s), chain_send.at[0, s], chain_recv.at[t, s], lower)

    @pl.when(t == 0)
    def _():
        for s in range(SUBS):
            send(x_ref.at[cut(s)], home(0, s), chain_send.at[0, s], chain_recv.at[0, s], upper)

    wait(w.at[quarter(spot)], wz_recv)
    for rel in (1, 2, 3):
        send(w.at[quarter(spot)], w.at[quarter(spot)], wp_send.at[rel], wp_recv.at[rel], at(mate(dp, rel), mp))

    @pl.when(t <= 1)
    def _():
        own.wait()
        for s in range(SUBS):
            send(home(t, s), home(t, s), pair_send.at[t, s], pair_recv.at[t, s], partner)

    tt = jnp.minimum(t, 3 - t)

    def rows_of(i, s):
        return pl.ds(pl.multiple_of(lax.rem(tt + i, 4) * ROWS + s * SUB, SUB), SUB)

    def receive(i, s):
        u = lax.rem(tt + i, 4)
        if i == 1:
            @pl.when(t == 2)
            def _():
                wait(relay.at[cut(s)], relay_recv.at[s])
                send(relay.at[cut(s)], home(3, s), relay_send.at[s], chain_recv.at[3, s], lower)

        if i > 0:
            @pl.when(t <= 1)
            def _():
                wait(home(u, s), chain_recv.at[u, s])
                if i < 3:
                    @pl.when(t == 1)
                    def _():
                        send(home(u, s), home(u, s), chain_send.at[i, s], chain_recv.at[u, s], lower)
                send(home(u, s), home(u, s), pair_send.at[u, s], pair_recv.at[u, s], partner)

        @pl.when(t >= 2)
        def _():
            wait(home(u, s), pair_recv.at[u, s])

        rows = rows_of(i, s)
        pltpu.make_async_copy(xs.at[rows], xs_ref.at[rows], xs_out.at[i, s]).start()

    def project(i, s):
        rows = rows_of(i, s)
        row = jnp.concatenate([bias[pl.ds(h, 1), :] for h in range(3)], axis=1)
        qkv[rows, :] = (dot(xs[rows, :], w[...], 1, 1) + row).astype(BF16)
        for h in range(3):
            pltpu.make_async_copy(qkv.at[rows, pl.ds(h * 256, 256)], qkv_ref.at[h, rows], qkv_out.at[i, s, h]).start()

    pieces = [(i, s) for i in range(4) for s in range(SUBS)]
    for i, s in pieces[:4]:
        receive(i, s)
    for rel in (1, 2, 3):
        wait(w.at[quarter(spot ^ rel)], wp_recv.at[rel])
    wait(bias, b_recv)
    pltpu.make_async_copy(w, w_ref, w_out).start()
    for i, s in pieces[:3]:
        project(i, s)
    for k in range(4, len(pieces)):
        receive(*pieces[k])
        project(*pieces[k - 1])
    project(*pieces[-1])

    for i in range(4):
        u = lax.rem(tt + i, 4)
        for s in range(SUBS):
            rows = pl.ds(pl.multiple_of(u * ROWS + s * SUB, SUB), SUB)
            wait(xs.at[rows], xs_out.at[i, s])
            for h in range(3):
                wait(qkv_ref.at[h, rows], qkv_out.at[i, s, h])

            @pl.when(t <= 1)
            def _():
                wait(home(u, s), pair_send.at[u, s])
    for s in range(SUBS):
        wait(x_ref.at[cut(s)], chain_send.at[0, s])

        @pl.when(t == 1)
        def _():
            wait(x_ref.at[cut(s)], chain_send.at[1, s])
            wait(x_ref.at[cut(s)], chain_send.at[2, s])

        @pl.when(t == 2)
        def _():
            wait(relay.at[cut(s)], relay_send.at[s])
    for rel in (1, 2, 3):
        wait(w.at[quarter(spot)], wp_send.at[rel])
    for far in (0, 1):
        @pl.when(gives & (mp // 2 + 2 * far != mp))
        def _():
            wait(wsrc.at[quarter(spot)], wz_send.at[far])
            wait(bsrc_ref, b_send.at[far])
    wait(ord_ref, o_recv)
    wait(mask_ref, m_recv)

    @pl.when(jnp.logical_not(order_here))
    def _():
        wait(osrc_ref, o_send)
        wait(msrc_ref, m_send)

    wait(w, w_out)


def collect(x, wq, wk, wv, b, order, mask):
    return pl.pallas_call(
        collect_kernel,
        out_shape=[sds((4 * ROWS, WIDTH), BF16), sds((3, 4 * ROWS, 256), BF16), sds((WIDTH, WIDTH), BF16), sds((3 * L,), jnp.int32),
                   sds((1, L), jnp.int32)],
        in_specs=[ANY] * 7,
        out_specs=[ANY] * 5,
        scratch_shapes=[
            VMEM((4 * ROWS, WIDTH), BF16), VMEM((4 * ROWS, WIDTH), BF16), VMEM((WIDTH, WIDTH), BF16), VMEM((WIDTH, WIDTH), BF16),
            VMEM((8, 256), F32), VMEM((ROWS, WIDTH), BF16),
            DMA((4, SUBS)), DMA((SUBS,)), DMA((4, SUBS)), DMA((3, SUBS)), DMA((SUBS,)), DMA((4, SUBS)), DMA,
            DMA, DMA((2,)), DMA((4,)), DMA((4,)), DMA, DMA((2,)), DMA, DMA, DMA, DMA,
            DMA((4, SUBS)), DMA((4, SUBS, 3)), DMA, DMA((12,)),
        ],
        compiler_params=pltpu.CompilerParams(collective_id=0, has_side_effects=True, vmem_limit_bytes=60 << 20),
        name="collect",
    )(x, wq, wk, wv, b, order, mask)


def greet_exchange(barrier):
    dp, mp, core, t = place()
    half, base = mp // 2, dp - core
    mine = lax.rem(mp, 2) * 2 + core
    for u in range(4):
        @pl.when((half != core) | (t != u))
        def _():
            pl.semaphore_signal(barrier, inc=1, device_id=chain_device(u, half, base), device_id_type=MESH)
    for g in range(4):
        @pl.when((half != core) | (mine != g))
        def _():
            pl.semaphore_signal(barrier, inc=1, device_id=worker(g, core, base), device_id_type=MESH)

    @pl.when(half == core)
    def _():
        pl.semaphore_wait(barrier, 6)

    @pl.when(half != core)
    def _():
        pl.semaphore_wait(barrier, 8)


def spread_kernel(a_ref, b_ref, oa_ref, ob_ref, send_sem, recv_sem, local_sem):
    dp, mp, core, t = place()
    half, base = mp // 2, dp - core
    mine = lax.rem(mp, 2) * 2 + core
    greet_exchange(pltpu.get_barrier_semaphore())
    for u in (3, 2, 1, 0):
        pair = ((a_ref.at[pl.ds(u * 1024, 1024)], oa_ref.at[mine]), (b_ref.at[pl.ds(u * 512, 512)], ob_ref.at[mine]))
        for k, (src, dst) in enumerate(pair):
            @pl.when((half != core) | (t != u))
            def _():
                send(src, dst, send_sem.at[u, k], recv_sem.at[mine, k], chain_device(u, half, base))

            @pl.when((half == core) & (t == u))
            def _():
                pltpu.make_async_copy(src, dst, local_sem.at[k]).start()
    for u in range(4):
        for k, src in enumerate((a_ref.at[pl.ds(u * 1024, 1024)], b_ref.at[pl.ds(u * 512, 512)])):
            @pl.when((half != core) | (t != u))
            def _():
                pltpu.make_async_copy(src, src, send_sem.at[u, k]).wait()
    for g in range(4):
        for k, dst in enumerate((oa_ref.at[g], ob_ref.at[g])):
            @pl.when((half != core) | (mine != g))
            def _():
                pltpu.make_async_copy(dst, dst, recv_sem.at[g, k]).wait()

            @pl.when((half == core) & (mine == g))
            def _():
                pltpu.make_async_copy(dst, dst, local_sem.at[k]).wait()


def spread(a, b):
    return pl.pallas_call(
        spread_kernel,
        out_shape=[jax.ShapeDtypeStruct((4, 1024, C), BF16), jax.ShapeDtypeStruct((4, 512, C), BF16)],
        in_specs=[ANY, ANY],
        out_specs=[ANY, ANY],
        scratch_shapes=[DMA((4, 2)), DMA((4, 2)), DMA((2,))],
        compiler_params=pltpu.CompilerParams(collective_id=1, has_side_effects=True),
        name="spread",
    )(a, b)


def regroup_kernel(a_ref, b_ref, oa_ref, ob_ref, send_sem, recv_sem, local_sem):
    dp, mp, core, t = place()
    half, base = mp // 2, dp - core
    mine = lax.rem(mp, 2) * 2 + core
    greet_exchange(pltpu.get_barrier_semaphore())
    big = lambda u: oa_ref.at[pl.ds(u * 1024, 1024)]
    small = lambda u: ob_ref.at[pl.ds(u * 512, 512)]
    for g in (0, 1, 2, 3):
        for k, (src, dst) in enumerate(((a_ref.at[g], big(t)), (b_ref.at[g], small(t)))):
            @pl.when((half != core) | (mine != g))
            def _():
                send(src, dst, send_sem.at[g, k], recv_sem.at[t, k], worker(g, core, base))

            @pl.when((half == core) & (mine == g))
            def _():
                pltpu.make_async_copy(src, dst, local_sem.at[k]).start()
    for g in range(4):
        for k, src in enumerate((a_ref.at[g], b_ref.at[g])):
            @pl.when((half != core) | (mine != g))
            def _():
                pltpu.make_async_copy(src, src, send_sem.at[g, k]).wait()
    for u in range(4):
        for k, dst in enumerate((big(u), small(u))):
            @pl.when((half != core) | (t != u))
            def _():
                pltpu.make_async_copy(dst, dst, recv_sem.at[u, k]).wait()

            @pl.when((half == core) & (t == u))
            def _():
                pltpu.make_async_copy(dst, dst, local_sem.at[k]).wait()


def regroup(a, b):
    return pl.pallas_call(
        regroup_kernel,
        out_shape=[jax.ShapeDtypeStruct((4096, C), BF16), jax.ShapeDtypeStruct((2048, C), BF16)],
        in_specs=[ANY, ANY],
        out_specs=[ANY, ANY],
        scratch_shapes=[DMA((4, 2)), DMA((4, 2)), DMA((2,))],
        compiler_params=pltpu.CompilerParams(collective_id=2, has_side_effects=True),
        name="regroup",
    )(a, b)


def settle_kernel(d0_ref, d1_ref, d2_ref, xs_ref, w_ref, extra_ref, mine_ref, out_ref, *rest):
    pieces_out, rest = rest[:9], rest[9:]
    (heads_ref, grads_ref, stage, pair_in, chain_in, gw, gwl, h_in, z_in, z_out,
                  pair_recv, pair_send, chain_recv, chain_send, relay_send,
                  s_recv, s_send, c_recv, c_send, h_recv, h_send, z_recv, z_send, q_recv, q_send, out_sem) = rest
    dp, mp, core, t = place()
    base, spot = dp - core, lax.rem(dp, 8) // 2
    step = 1 - 2 * core
    partner, lower, upper = at(dp + step, mp), at(dp, mp - step), at(dp, mp + step)
    group = lax.rem(mp, 2) * 2 + core
    gives = core == lax.rem(mp, 2)
    quarter = lambda q: pl.ds(pl.multiple_of(q * QUARTER, QUARTER), QUARTER)
    share = lambda j, parity: grads_ref.at[2 * j + parity]

    greet(pltpu.get_barrier_semaphore(), True)

    grads_ref[2 * spot + core] = mine_ref[...]
    for rel in (1, 2, 3):
        send(mine_ref, share(spot, core), s_send.at[rel], s_recv.at[rel], at(mate(dp, rel), mp))

    def weight_gradients():
        gw[...] = jnp.zeros_like(gw)

        def part(i, sums):
            rows = pl.ds(pl.multiple_of(i * SUB, SUB), SUB)
            x = xs_ref[rows, :]
            new = []
            for h, d_ref in enumerate((d0_ref, d1_ref, d2_ref)):
                d = d_ref[rows, :]
                gw[pl.ds(h * 256, 256), :] += dot(d, x, 0, 0)
                new.append(sums[h] + jnp.sum(d.astype(F32), axis=0, keepdims=True))
            return tuple(new)

        sums = lax.fori_loop(0, 4 * ROWS // SUB, part, tuple(jnp.zeros((1, 256), F32) for _ in range(3)))
        gwl[...] = gw[...].astype(BF16)
        for h in range(3):
            line = jnp.concatenate([sums[h], jnp.zeros((1, WIDTH - 256), F32)], axis=1)
            spare = h * 256 + (192 if h == 1 else 128)
            gwl[pl.ds(spare, 16), :] = jnp.concatenate([line, jnp.zeros((15, WIDTH), F32)], axis=0).astype(BF16)
        for rel in (1, 2, 3):
            send(gwl.at[quarter(spot ^ rel)], h_in.at[rel], h_send.at[rel], h_recv.at[rel], at(mate(dp, rel), mp))

    def plane_sum():
        for rel in (1, 2, 3):
            wait(h_in.at[rel], h_recv.at[rel])
        half_sum = gwl[quarter(spot), :].astype(F32)
        for rel in (1, 2, 3):
            half_sum += h_in[rel].astype(F32)
        z_out[...] = half_sum.astype(BF16)

        @pl.when(mp != group)
        def _():
            send(z_out, z_in.at[mp // 2], z_send, z_recv.at[mp // 2], at(dp, group))

    tt = jnp.minimum(t, 3 - t)
    for i in range(3):
        u = lax.rem(3 - i + tt, 4)
        for s in range(SUBS):
            rows = pl.ds(pl.multiple_of(u * ROWS + s * SUB, SUB), SUB)
            value = jnp.zeros((SUB, WIDTH), F32)
            for h, d_ref in enumerate((d0_ref, d1_ref, d2_ref)):
                value += jnp.dot(d_ref[rows, :], w_ref[pl.ds(h * 256, 256), :], preferred_element_type=F32)

            @pl.when(t >= 2)
            def _():
                stage[rows, :] = value.astype(BF16)
                send(stage.at[rows], pair_in.at[rows], pair_send.at[i, s], pair_recv.at[i, s], partner)

            @pl.when(t <= 1)
            def _():
                wait(pair_in.at[rows], pair_recv.at[i, s])
                here = value + pair_in[rows, :].astype(F32)
                if i == 0:
                    stage[rows, :] = here.astype(BF16)
                else:
                    @pl.when(t == 1)
                    def _():
                        wait(chain_in.at[rows], chain_recv.at[u, s])
                        stage[rows, :] = (here + chain_in[rows, :].astype(F32)).astype(BF16)

                    @pl.when(t == 0)
                    def _():
                        stage[rows, :] = here.astype(BF16)

                @pl.when((t == 0) | (i > 0))
                def _():
                    send(stage.at[rows], chain_in.at[rows], chain_send.at[i, s], chain_recv.at[u, s], upper)

                if i == 0:
                    @pl.when(t == 1)
                    def _():
                        send(stage.at[rows], chain_in.at[rows], chain_send.at[i, s], chain_recv.at[u, s], lower)

        if i < 2:
            @pl.when(t == 1)
            def _():
                (weight_gradients, plane_sum)[i]()

    @pl.when(t != 1)
    def _():
        weight_gradients()

    for rel in (1, 2, 3):
        wait(share(spot ^ rel, core), s_recv.at[rel])
    for j in range(4):
        send(share(j, core), share(j, core), c_send.at[j], c_recv.at[j], partner)

    @pl.when(t == 2)
    def _():
        for s in range(SUBS):
            rows = pl.ds(3 * ROWS + s * SUB, SUB)
            wait(chain_in.at[rows], chain_recv.at[3, s])
            send(chain_in.at[rows], chain_in.at[rows], relay_send.at[s], chain_recv.at[3, s], upper)
            if s == 0:
                plane_sum()

    @pl.when((t == 0) | (t == 3))
    def _():
        plane_sum()

    for s in range(SUBS):
        rows = pl.ds(pl.multiple_of(tt * ROWS + s * SUB, SUB), SUB)
        cut = pl.ds(s * SUB, SUB)
        value = jnp.zeros((SUB, WIDTH), F32)
        for h, d_ref in enumerate((d0_ref, d1_ref, d2_ref)):
            value += jnp.dot(d_ref[rows, :], w_ref[pl.ds(h * 256, 256), :], preferred_element_type=F32)

        @pl.when(t >= 2)
        def _():
            stage[rows, :] = value.astype(BF16)
            send(stage.at[rows], pair_in.at[rows], pair_send.at[3, s], pair_recv.at[3, s], partner)

        @pl.when(t <= 1)
        def _():
            stage[rows, :] = value.astype(BF16)

    @pl.when(gives)
    def _():
        both = jnp.zeros((QUARTER, WIDTH), F32)
        for far in (0, 1):
            source = mp // 2 + 2 * far

            @pl.when(source == mp)
            def _():
                z_in[far] = z_out[...]

            @pl.when(source != mp)
            def _():
                wait(z_in.at[far], z_recv.at[far])

            both += z_in[far].astype(F32)
        heads_ref[quarter(spot), :] = both.astype(BF16)
        mine = heads_ref.at[quarter(spot)]
        send(mine, mine, q_send.at[0], q_recv.at[spot], partner)
        for rel in (1, 2, 3):
            send(mine, mine, q_send.at[rel], q_recv.at[spot], at(mate(dp, rel), mp))
            send(mine, mine, q_send.at[rel + 3], q_recv.at[spot], at(mate(dp, rel) + step, mp))

    for s in range(SUBS):
        cut = pl.ds(s * SUB, SUB)
        rows = pl.ds(pl.multiple_of(t * ROWS + s * SUB, SUB), SUB)
        wait(chain_in.at[rows], chain_recv.at[t, s])
        value = extra_ref[cut, :] + chain_in[rows, :].astype(F32)

        @pl.when(t <= 1)
        def _():
            wait(pair_in.at[rows], pair_recv.at[3, s])
            out_ref[cut, :] = (value + stage[rows, :].astype(F32) + pair_in[rows, :].astype(F32)).astype(BF16)

        @pl.when(t >= 2)
        def _():
            out_ref[cut, :] = value.astype(BF16)

    for q in range(4):
        @pl.when(jnp.logical_not(gives) | (spot != q))
        def _():
            wait(heads_ref.at[quarter(q)], q_recv.at[q])
    for j in range(4):
        wait(share(j, 1 - core), c_recv.at[j])
    copies = []
    for i in range(8):
        for n, (first, rows) in enumerate(((0, 96), (96, 96), (192, 32), (224, 16))):
            if n == 2 and i >= 6:
                continue
            dst = pieces_out[3 + n].at[pl.ds(i * rows, rows)]
            copies.append(pltpu.make_async_copy(grads_ref.at[i, pl.ds(first, rows)], dst, out_sem.at[20 + 4 * i + n]))
    copies.append(pltpu.make_async_copy(grads_ref.at[6, pl.ds(192, 16)], pieces_out[8], out_sem.at[0]))
    for h in range(3):
        for n, where in enumerate((0, 2, 1) if h == 1 else (1, 3, 0)):
            src = heads_ref.at[pl.ds((4 * h + where) * HD, HD)]
            copies.append(pltpu.make_async_copy(src, pieces_out[n].at[pl.ds(h * HD, HD)], out_sem.at[8 + 3 * h + n]))
        src = heads_ref.at[pl.ds(h * 256 + (192 if h == 1 else 128), 16)]
        copies.append(pltpu.make_async_copy(src, pieces_out[7].at[h], out_sem.at[17 + h]))
    for copy in copies:
        copy.start()

    for s in range(SUBS):
        piece = stage.at[pl.ds(s * SUB, SUB)]

        @pl.when(t >= 2)
        def _():
            for i in range(4):
                wait(piece, pair_send.at[i, s])

        @pl.when(t <= 1)
        def _():
            for i in range(3):
                wait(piece, chain_send.at[i, s])

        @pl.when(t == 2)
        def _():
            wait(piece, relay_send.at[s])
    for rel in (1, 2, 3):
        wait(mine_ref, s_send.at[rel])
        wait(z_out, h_send.at[rel])
    for j in range(4):
        wait(mine_ref, c_send.at[j])

    @pl.when(mp != group)
    def _():
        wait(z_out, z_send)

    @pl.when(gives)
    def _():
        for k in range(7):
            wait(z_out, q_send.at[k])

    for copy in copies:
        copy.wait()


def settle(d0, d1, d2, xs, w, extra, mine):
    return pl.pallas_call(
        settle_kernel,
        out_shape=[sds((ROWS, WIDTH), BF16)] + [sds((rows, WIDTH), BF16) for rows in (192, 192, 192, 768, 768, 192, 128)]
        + [sds((3, 16, WIDTH), BF16), sds((16, WIDTH), BF16)],
        in_specs=[VM] * 7,
        out_specs=[VM] + [ANY] * 9,
        scratch_shapes=[VMEM((WIDTH, WIDTH), BF16), VMEM((8, SHARE_ALL, WIDTH), BF16)] + [VMEM((4 * ROWS, WIDTH), BF16)] * 3 + [
            VMEM((WIDTH, WIDTH), F32), VMEM((WIDTH, WIDTH), BF16), VMEM((4, QUARTER, WIDTH), BF16), VMEM((2, QUARTER, WIDTH), BF16),
            VMEM((QUARTER, WIDTH), BF16),
            DMA((4, SUBS)), DMA((4, SUBS)), DMA((4, SUBS)), DMA((3, SUBS)), DMA((SUBS,)),
            DMA((4,)), DMA((4,)), DMA((4,)), DMA((4,)), DMA((4,)), DMA((4,)), DMA((2,)), DMA, DMA((4,)), DMA((7,)), DMA((52,)),
        ],
        compiler_params=pltpu.CompilerParams(collective_id=3, has_side_effects=True, vmem_limit_bytes=60 << 20),
        name="settle",
    )(d0, d1, d2, xs, w, extra, mine)


EPS = 1e-12
CHUNK = 512
FF_MODEL = 768


def gelu_and_slope(v):
    size = jnp.abs(v)
    u = 1.0 / (1.0 + (0.3275911 * 0.7071067811865476) * size)
    bell = jnp.exp2(v * v * -0.7213475204444817 - 1.3257480647361595)
    poly = u * (0.3193815306 + u * (-0.3565637784 + u * (1.7814779345 + u * (-1.8212559786 + u * 1.3302744294))))
    tail = poly * bell
    cdf = jnp.where(v < 0, tail, 1.0 - tail)
    return v * cdf, cdf + v * bell


def row_mean(v):
    return jnp.sum(v, axis=-1, keepdims=True) * (1.0 / FF_MODEL)


def ffn_kernel(c01_ref, c2_ref, tok_ref, cot_ref, vec_ref, near_ref, a_ref, b_ref,
               out_ref, res_ref, g01_ref, g2_ref, keep_ref, next_ref, give_ref, keep_tail_ref, give_tail_ref,
               w, wout, ctx, x, gf, act, slope, zhat, acc, rstd, cols, recv, recv2, tail, tail_in,
               o_local, o_send, o_recv, f_send, f_recv, w_local, w_send, w_recv, d_send, d_recv,
               g_send, g_recv, m_send, m_recv, t_send, t_recv, out_sem, tail_sem):
    dp, mp, core, t = place()
    step = 1 - 2 * core
    partner = at(dp + step, mp)
    spot = lax.rem(dp, 8) // 2
    one, two = jnp.where(core == 0, 1, 2), jnp.where(core == 0, 2, 1)
    mate_a, mate_b = at(dp + 2 * ((spot ^ one) - spot), mp), at(dp + 2 * ((spot ^ two) - spot), mp)
    shard = lambda k: lax.rem(mp - k + 4, 4)
    barrier = pltpu.get_barrier_semaphore()
    for device in (partner, mate_a, mate_b):
        signal(barrier, device)
    pl.semaphore_wait(barrier, 3)

    def out_rows(m, i):
        first = jnp.where(i < 4, m * C + 32 * i, 4 * C + m * HD + 32 * (i - 4))
        return wout.at[pl.ds(pl.multiple_of(first, 32), 32)]

    sources = ((0, near_ref), (one, a_ref), (two, b_ref))
    far = spot ^ 3
    for k in range(4):
        @pl.when(spot ^ one < 3)
        def _():
            send(a_ref.at[k, pl.ds(SHARE, 32)], out_rows(shard(k), 2 * (spot ^ one) + core), f_send.at[k], f_recv.at[k], mate_b)
    for rel, ref in sources:
        j = spot ^ rel
        for k in range(4):
            src = ref.at[k, pl.ds(SHARE, 32)]

            @pl.when(j < 3)
            def _():
                pltpu.make_async_copy(src, out_rows(shard(k), 2 * j + core), o_local.at[j, k]).start()
                send(src, out_rows(shard(k), 2 * j + core), o_send.at[j, k], o_recv.at[j, k], partner)

    body = pl.ds(0, SHARE)
    for k in range(4):
        send(a_ref.at[k, body], w.at[2 * (spot ^ one) + core, shard(k)], d_send.at[k], d_recv.at[k], mate_b)
    for rel, ref in sources:
        for k in range(4):
            mine = w.at[2 * (spot ^ rel) + core, shard(k)]
            pltpu.make_async_copy(ref.at[k, body], mine, w_local.at[rel, k]).start()
            send(ref.at[k, body], mine, w_send.at[rel, k], w_recv.at[rel, k], partner)

    lane = lax.broadcasted_iota(jnp.int32, (1, C), 1)
    for g in range(4):
        ctx[:, pl.ds(g * C, C)] = c01_ref[g]
    for g in (0, 2):
        a, b = c2_ref[g].astype(F32), c2_ref[g + 1].astype(F32)
        col = pl.ds(4 * C + g * HD, C)
        ctx[pl.ds(0, 512), col] = jnp.where(lane < HD, a, pltpu.roll(b, HD, 1)).astype(BF16)
        ctx[pl.ds(512, 512), col] = jnp.where(lane < HD, pltpu.roll(a, HD, 1), b).astype(BF16)
    cols[...] = jnp.zeros_like(cols)
    b_out, gain1, bias1, b_down, gain2, bias2 = (vec_ref[pl.ds(i, 1), :] for i in range(6))
    row_chunks = [pl.ds(r * CHUNK, CHUNK) for r in range(1024 // CHUNK)]

    part = wout.at[pl.ds(0, 32)]
    for k in range(4):
        @pl.when(far < 3)
        def _():
            mine = out_rows(shard(k), 2 * far + core)
            wait(mine, f_recv.at[k])
            send(mine, mine, o_send.at[far, k], o_recv.at[far, k], partner)
    for j in range(3):
        for k in range(4):
            @pl.when(far != j)
            def _():
                wait(part, o_local.at[j, k])

            wait(part, o_recv.at[j, k])

    for rows in row_chunks:
        h = jnp.dot(ctx[rows, :], wout[...], preferred_element_type=F32) + tok_ref[rows, :].astype(F32) + b_out
        h = h - row_mean(h)
        scale = lax.rsqrt(row_mean(h * h) + EPS)
        rstd[rows, :] = scale
        h = h * scale
        zhat[rows, :] = h
        first = h * gain1 + bias1
        acc[rows, :] = first + b_down
        x[rows, :] = first.astype(BF16)

    whole = w.at[0, 0]
    up_pair = lambda j: w[pl.ds(2 * j, 2), :, pl.ds(0, 96), :].reshape(768, FF_MODEL)
    down_pair = lambda j: w[pl.ds(2 * j, 2), :, pl.ds(96, 96), :].reshape(768, FF_MODEL)

    def up(j, rel, rows):
        bias = [jnp.sum(w[2 * j + f, :, pl.ds(192, 16), :].astype(F32), axis=0)[0:1, :384] for f in range(2)]
        pre = dot(x[rows, :], up_pair(j), 1, 1) + jnp.concatenate(bias, axis=1)
        value, grad = gelu_and_slope(pre)
        act[rel, rows, :] = value.astype(BF16)
        slope[rel, rows, :] = grad.astype(BF16)

    def down(j, rel, rows):
        acc[rows, :] += jnp.dot(act[rel, rows, :], down_pair(j), preferred_element_type=F32)

    for rel in range(4):
        j = spot ^ rel
        if rel == 2:
            for k in range(4):
                mine = w.at[2 * (spot ^ 3) + core, shard(k)]
                wait(mine, d_recv.at[k])
                send(mine, mine, w_send.at[3, k], w_recv.at[3, k], partner)
        for k in range(4):
            if rel < 3:
                wait(whole, w_local.at[rel, k])
            wait(whole, w_recv.at[rel, k])
        before = None
        for rows in row_chunks:
            up(j, rel, rows)
            if before is not None:
                down(j, rel, before)
            before = rows
        down(j, rel, before)

    for rows in row_chunks:
        z = acc[rows, :]
        z = z - row_mean(z)
        scale = lax.rsqrt(row_mean(z * z) + EPS)
        z = z * scale
        out_ref[rows, :] = (z * gain2 + bias2).astype(BF16)
        cot = cot_ref[rows, :].astype(F32)
        dz = cot * gain2
        gs = scale * (dz - row_mean(dz) - z * row_mean(dz * z))
        cols[pl.ds(2, 1), :] += jnp.sum(cot * z, axis=0, keepdims=True)
        cols[pl.ds(3, 1), :] += jnp.sum(cot, axis=0, keepdims=True)
        cols[pl.ds(5, 1), :] += jnp.sum(gs, axis=0, keepdims=True)
        acc[rows, :] = gs
        gf[rows, :] = gs.astype(BF16)

    for rel in range(4):
        for k in range(4):
            wait(whole, w_send.at[rel, k])
    for k in range(4):
        wait(whole, d_send.at[k])

    grads = pl.ds(0, 192)
    order = (3, 1, 2, 0)
    place_of = {rel: q for q, rel in enumerate(order)}

    def add_cores(rel):
        q, i = place_of[rel], 2 * (spot ^ rel) + core
        wait(recv.at[q], g_recv.at[q])
        for m in range(4):
            recv[q, m] = (recv[q, m].astype(F32) + w[i, m, grads, :].astype(F32)).astype(BF16)
        if rel == 3:
            send(recv.at[q], recv2, m_send, m_recv, mate_a)
        elif rel == 0:
            pltpu.make_async_copy(recv.at[q], keep_ref, out_sem.at[0]).start()
        else:
            @pl.when(one == rel)
            def _():
                pltpu.make_async_copy(recv.at[q], next_ref, out_sem.at[1]).start()

    for q, rel in enumerate(order):
        j = spot ^ rel
        for rows in row_chunks:
            ga = dot(gf[rows, :], down_pair(j), 1, 1)
            slope[rel, rows, :] = (ga * slope[rel, rows, :].astype(F32)).astype(BF16)
            acc[rows, :] += jnp.dot(slope[rel, rows, :], up_pair(j), preferred_element_type=F32)
        for f in range(2):
            cut = pl.ds(f * 384, 384)
            gp = slope[rel, :, cut]
            w[2 * j + f, :, pl.ds(0, 96), :] = dot(gp, x[...], 0, 0).astype(BF16).reshape(4, 96, FF_MODEL)
            w[2 * j + f, :, pl.ds(96, 96), :] = dot(act[rel, :, cut], gf[...], 0, 0).astype(BF16).reshape(4, 96, FF_MODEL)
            cols[pl.ds(8 + 2 * j + f, 1), pl.ds(0, 384)] = jnp.sum(gp.astype(F32), axis=0, keepdims=True)
        send(w.at[2 * j + 1 - core, :, grads], recv.at[q], g_send.at[q], g_recv.at[q], partner)
        if q:
            add_cores(order[q - 1])

    ctx_grad = x.at[:, pl.ds(0, 2 * C)]
    for rows in row_chunks:
        grad = acc[rows, :]
        z = zhat[rows, :]
        dz = grad * gain1
        gr = rstd[rows, :] * (dz - row_mean(dz) - z * row_mean(dz * z))
        cols[pl.ds(0, 1), :] += jnp.sum(grad * z, axis=0, keepdims=True)
        cols[pl.ds(1, 1), :] += jnp.sum(grad, axis=0, keepdims=True)
        cols[pl.ds(4, 1), :] += jnp.sum(gr, axis=0, keepdims=True)
        res_ref[rows, :] = gr
        low = gr.astype(BF16)
        gf[rows, :] = low
        gc = dot(low, wout[...], 1, 1).astype(BF16)
        for g in range(4):
            g01_ref[g, rows, :] = gc[:, g * C : g * C + C]
        ctx_grad[rows, :] = gc[:, 4 * C :]
    for g in (0, 2):
        top = ctx_grad[pl.ds(0, 512), pl.ds(g * HD, C)].astype(F32)
        low = ctx_grad[pl.ds(512, 512), pl.ds(g * HD, C)].astype(F32)
        g2_ref[g] = jnp.where(lane < HD, top, pltpu.roll(low, HD, 1)).astype(BF16)
        g2_ref[g + 1] = jnp.where(lane < HD, pltpu.roll(top, HD, 1), low).astype(BF16)

    for n in range(3):
        got = dot(ctx[:, pl.ds(n * 256, 256)], gf[...], 0, 0).astype(BF16)
        for i in range(8):
            piece = got[i * 32 : i * 32 + 32, :]
            m, share = (2 * n + i // 4, i % 4) if n < 2 else (i // 2, 4 + i % 2)
            tail[share % 2, share // 2, m, pl.ds(0, 32), :] = piece
    vectors = jnp.concatenate([cols[pl.ds(0, 6), :], jnp.zeros((26, FF_MODEL), F32)], axis=0).astype(BF16)
    for i in range(8):
        line = jnp.concatenate([cols[pl.ds(8 + i, 1), :], jnp.zeros((15, FF_MODEL), F32)], axis=0).astype(BF16)
        for m in range(4):
            tail[i % 2, i // 2, m, pl.ds(32, 16), :] = line
            if i >= 6:
                tail[i % 2, i // 2, m, pl.ds(0, 32), :] = vectors if i == 6 else jnp.zeros((32, FF_MODEL), BF16)
    send(tail.at[1 - core], tail_in, t_send, t_recv, partner)
    add_cores(0)

    wait(recv2, m_recv)
    for rel in (1, 2):
        @pl.when(two == rel)
        def _():
            for m in range(4):
                recv2[m] = (recv2[m].astype(F32) + recv[place_of[rel], m].astype(F32)).astype(BF16)
    give = pltpu.make_async_copy(recv2, give_ref, out_sem.at[2])
    give.start()
    wait(tail_in, t_recv)
    for rel in range(4):
        j = spot ^ rel
        for m in range(4):
            tail_in[j, m] = (tail_in[j, m].astype(F32) + tail[core, j, m].astype(F32)).astype(BF16)
        along, across = jnp.where(core == 0, rel % 2, rel // 2), jnp.where(core == 0, rel // 2, rel % 2)
        for side, ref in enumerate((keep_tail_ref, give_tail_ref)):
            @pl.when(along == side)
            def _():
                pltpu.make_async_copy(tail_in.at[j], ref.at[across], tail_sem.at[rel]).start()
    give.wait()
    wait(recv2, out_sem.at[0])
    wait(recv2, out_sem.at[1])
    for rel in range(4):
        wait(tail_in.at[0], tail_sem.at[rel])
    for q in range(4):
        wait(recv.at[q], g_send.at[q])
    wait(recv2, m_send)
    wait(tail_in, t_send)
    for k in range(4):
        @pl.when(spot ^ one < 3)
        def _():
            wait(part, f_send.at[k])

        for j in range(3):
            wait(part, o_send.at[j, k])


def ffn(c01, c2, tokens, cot, vecs, near, a, b):
    main, rest = sds((4, 192, WIDTH), BF16), sds((2, 4, 48, WIDTH), BF16)
    rows = lambda dtype: VMEM((1024, WIDTH), dtype)
    four = lambda *shape: VMEM((4,) + shape, BF16)
    return pl.pallas_call(
        ffn_kernel,
        out_shape=[sds((1024, WIDTH), BF16), sds((1024, WIDTH), F32), sds((4, 1024, C), BF16), sds((4, 512, C), BF16), main, main, main, rest, rest],
        in_specs=[VM] * 5 + [ANY] * 3,
        out_specs=[VM] * 4 + [ANY] * 5,
        scratch_shapes=[
            VMEM((8, 4, SHARE, WIDTH), BF16), VMEM((WIDTH, WIDTH), BF16), rows(BF16), rows(BF16), rows(BF16), four(1024, WIDTH), four(1024, WIDTH),
            rows(F32), rows(F32), VMEM((1024, 1), F32), VMEM((16, WIDTH), F32), four(4, 192, WIDTH), four(192, WIDTH),
            VMEM((2, 4, 4, 48, WIDTH), BF16), four(4, 48, WIDTH),
        ] + [DMA((4, 4))] * 3 + [DMA((4,))] * 2 + [DMA((4, 4))] * 3 + [DMA((4,))] * 4 + [DMA] * 4 + [DMA((3,)), DMA((4,))],
        compiler_params=pltpu.CompilerParams(collective_id=4, has_side_effects=True, vmem_limit_bytes=63 << 20),
        name="ffn",
    )(c01, c2, tokens, cot, vecs, near, a, b)


def swap(value, even_bits, odd_bits, n_dp):
    return lax.ppermute(value, "dp", [(d, d ^ (odd_bits if d % 2 else even_bits)) for d in range(n_dp)])


def pick(value, index, axis):
    return lax.dynamic_index_in_dim(value, index, axis, keepdims=False)


def total(a, b):
    return (a.astype(F32) + b.astype(F32)).astype(BF16)


def tie(*values):
    return lax.optimization_barrier(values)


def body(n_dp, tokens, w_query, b_query, w_key, w_value, b_value, w_out, b_out, norm1_gain, norm1_bias, w_up, b_up, w_down,
         b_down, norm2_gain, norm2_bias, key_mask, cluster_order, cotangent):
    dp, mp, core, t = place()
    ring = lambda k: [(z, (z + k) % 4) for z in range(4)]

    order = 2 * jnp.where(core == 1, cluster_order ^ 3072, cluster_order).reshape(3 * L)
    bq, bv, bz = b_query.reshape(3, HD), b_value.reshape(3, HD), jnp.zeros((C,), F32)
    b_heads = jnp.stack([jnp.concatenate([bq[h], bv[h], bz] if h == 1 else [bv[h], bq[h], bz]) for h in range(3)])
    b_heads = jnp.concatenate([b_heads, jnp.zeros((5, 256), F32)])
    i = dp % 8
    bias_row = lax.dynamic_update_slice(jnp.zeros((16, WIDTH), BF16), lax.dynamic_slice(b_up, (96 * i,), (96,)).reshape(1, 96), (0, 96 * mp))
    share = jnp.concatenate([
        lax.dynamic_slice(w_up, (0, 96 * i), (WIDTH, 96)).T,
        lax.dynamic_slice(w_down, (96 * i, 0), (96, WIDTH)),
        bias_row,
        lax.dynamic_slice(w_out, (jnp.minimum(32 * i, 160), 0), (32, WIDTH)),
    ])

    xs, qkv, w_heads, order, mask = collect(tokens, w_query.T, w_key.T, w_value.T, b_heads, order, key_mask)
    qkv, share = tie(qkv, share)
    shares = [share] + [lax.ppermute(share, "mp", ring(i)) for i in (1, 2, 3)]
    c01, ts01, probs01 = attend(0, order, mask, qkv)
    c01, *shares = tie(c01, *shares)
    near = jnp.stack(shares)
    along, across = swap(near, 2, 4, n_dp), swap(near, 4, 2, n_dp)
    c2, ts2, probs2 = attend(2, order, mask, qkv)
    c01, c2 = spread(c01, c2)

    vecs = jnp.stack([b_out, norm1_gain, norm1_bias, b_down, norm2_gain, norm2_bias, b_out, b_out])
    layer_out, grad_residual, g01, g2, keep, nearer, give, keep_tail, give_tail = ffn(
        c01, c2, tokens, cotangent, vecs, near, along, across
    )

    got, got_nearer, got_tail = swap(give, 4, 2, n_dp), swap(nearer, 2, 4, n_dp), swap(give_tail, 2, 4, n_dp)
    g01, g2 = regroup(g01, g2)
    g01, keep, got, got_nearer, keep_tail, got_tail = tie(g01, keep, got, got_nearer, keep_tail, got_tail)
    keep = total(keep, got_nearer)
    keep_tail, give_tail = total(keep_tail[0], got_tail[0]), total(keep_tail[1], got_tail[1])
    got_tail = swap(give_tail, 4, 2, n_dp)
    d0 = attend_back(0, order, g01, ts01, probs01)
    d0, order, keep, got, keep_tail, got_tail = tie(d0, order, keep, got, keep_tail, got_tail)
    sums = jnp.concatenate([total(keep, got), total(keep_tail, got_tail)], axis=1)
    for bit in range(3, n_dp.bit_length() - 1):
        sums = total(sums, swap(sums, 1 << bit, 1 << bit, n_dp))
    parts = [pick(sums, mp, 0)]
    for i in (1, 2, 3):
        parts.append(lax.ppermute(pick(sums, (mp + i) % 4, 0), "mp", ring(i)))
    d1 = attend_back(1, order, g01, ts01, probs01)
    d2 = attend_back(2, order, g2, ts2, probs2)
    d2, *parts = tie(d2, *parts)
    mine = sum(p.astype(F32) for p in parts).astype(BF16)
    grad_tokens, *sums = settle(d0, d1, d2, xs, w_heads, grad_residual, mine)
    hq, hk, hv, g_up, g_down, g_out, units, spare, vectors = (s.astype(F32) for s in sums)
    for bit in range(3, n_dp.bit_length() - 1):
        hq, hk, hv, spare = (s + swap(s, 1 << bit, 1 << bit, n_dp) for s in (hq, hk, hv, spare))
    sums_of = lambda where: jnp.concatenate([spare[h, 0, where[h] : where[h] + HD] for h in range(3)])
    g_b_up = lax.dynamic_slice(units.reshape(8, 16, WIDTH)[:, 0], (0, 96 * mp), (8, 96)).reshape(WIDTH)
    return (
        layer_out,
        grad_tokens,
        hq.T,
        sums_of((HD, 0, HD)),
        hk.T,
        hv.T,
        sums_of((0, HD, 0)),
        g_out,
        vectors[4],
        vectors[0],
        vectors[1],
        g_up.T,
        g_b_up,
        g_down,
        vectors[5],
        vectors[2],
        vectors[3],
    )


def solution(mesh):
    return jax.shard_map(
        functools.partial(body, mesh.shape["dp"]),
        mesh=mesh,
        in_specs=(
            P(("dp", "mp"), None), P(None, "mp"), P("mp"), P(None, "mp"), P(None, "mp"), P("mp"), P("mp", None), P(), P(), P(),
            P(None, "mp"), P("mp"), P("mp", None), P(), P(), P(), P("dp", None), P("dp", "mp", None), P(("dp", "mp"), None),
        ),
        out_specs=(
            P(("dp", "mp"), None), P(("dp", "mp"), None), P(None, "mp"), P("mp"), P(None, "mp"), P(None, "mp"), P("mp"),
            P("mp", None), P(), P(), P(), P(None, "mp"), P("mp"), P("mp", None), P(), P(), P(),
        ),
        check_vma=False,
    )
```

```python
import functools
import jax
import jax.numpy as jnp
from jax import lax
from jax.experimental import pallas as pl
from jax.experimental.pallas import tpu as pltpu
from jax.sharding import PartitionSpec as P

L = 4096
C = 128
HD = 64
GROUP = 2
STEP = 1024
GROUPS = STEP // (GROUP * C)
HALVES = 2
F32 = jnp.float32
BF16 = jnp.bfloat16
VMEM = pltpu.VMEM


def dot(a, b, da, db):
    return lax.dot_general(a, b, (((da,), (db,)), ((), ())), preferred_element_type=F32)


def in_turn(gather, compute, scatter, bufs, outs):
    gather(0, bufs[0])
    for group in range(GROUPS):
        if group + 1 < GROUPS:
            gather(group + 1, bufs[(group + 1) % 2])
        compute(group, bufs[group % 2], outs[group % 2])
        if group:
            scatter(group - 1, outs[(group - 1) % 2])
    scatter(GROUPS - 1, outs[(GROUPS - 1) % 2])


def each_window(ord_ref, windows, sems, first, step, steps, work):
    def fetch(n, at_step):
        start = pl.multiple_of((first + at_step * HALVES + n) * STEP, STEP)
        return pltpu.make_async_copy(ord_ref.at[pl.ds(start, STEP)], windows[n], sems.at[n])

    @pl.when(step == 0)
    def _():
        for n in range(HALVES):
            fetch(n, step).start()

    for n in range(HALVES):
        fetch(n, step).wait()
        work(n, windows[n])

        @pl.when(step + 1 < steps)
        def _():
            fetch(n, step + 1).start()


def attend_kernel(first, ord_ref, mask_ref, qkv_ref, c_ref, ts_ref, pr_ref, src, ctx, *rest):
    slots, windows, sems = rest[:4], rest[4 : 4 + HALVES], rest[4 + HALVES]
    head, step = pl.program_id(0) + first, pl.program_id(1)
    live = jnp.sum(mask_ref[...].astype(F32), axis=1, keepdims=True).astype(jnp.int32)

    @pl.when(step == 0)
    def _():
        src[pl.ds(0, L, stride=2), :] = qkv_ref[0, :, :C].astype(F32)
        src[pl.ds(1, L, stride=2), :] = qkv_ref[0, :, C:].astype(F32)

    def work(n, window):
        def gather(group, buf):
            for u in range(GROUP * C):
                buf[pl.ds(2 * u, 2), :] = src[pl.ds(pl.multiple_of(window[group * GROUP * C + u], 2), 2), :]

        def compute(group, buf, out):
            each = range(GROUP)
            rows = [pl.ds(n * STEP + (group * GROUP + i) * C, C) for i in each]
            t0 = [buf[pl.ds(2 * i * C, C, stride=2), :].astype(BF16) for i in each]
            t1 = [buf[pl.ds(2 * i * C + 1, C, stride=2), :].astype(BF16) for i in each]
            for i in each:
                ts_ref[0, rows[i], :C] = t0[i]
                ts_ref[0, rows[i], C:] = t1[i]
            slot = [(step * HALVES + n) * STEP + (group * GROUP + i) * C + lax.broadcasted_iota(jnp.int32, (C, C), 0) for i in each]
            scores = [dot(t1[i], t0[i], 1, 1) * 0.125 + jnp.where(slot[i] < live, 0.0, -10000.0) for i in each]
            e = [jnp.exp(scores[i] - jnp.max(scores[i], axis=0, keepdims=True)) for i in each]
            probs = [e[i] * (1.0 / jnp.sum(e[i], axis=0, keepdims=True)) for i in each]
            for i in each:
                pr_ref[0, rows[i], :] = probs[i]
            for i in each:
                out[pl.ds(i * C, C), :] = dot(probs[i].astype(BF16), t0[i], 0, 0)

        def scatter(group, out):
            for u in range(GROUP * C):
                ctx[pl.ds(window[group * GROUP * C + u], 1), :] = out[pl.ds(u, 1), :]

        in_turn(gather, compute, scatter, slots[:2], slots[2:])

    each_window(ord_ref, windows, sems, head * (L // STEP), step, L // STEP // HALVES, work)

    @pl.when(step == L // STEP // HALVES - 1)
    def _():
        lane = lax.broadcasted_iota(jnp.int32, (1, C), 1)
        if first == 2:
            for k in range(4):
                low = ctx[pl.ds(k * 2048, 512, stride=2), :]
                high = pltpu.roll(ctx[pl.ds(k * 2048 + 1024, 512, stride=2), :], HD, 1)
                c_ref[pl.ds(k * 512, 512), :] = jnp.where(lane < HD, low, high).astype(BF16)
        else:
            rows = ctx[pl.ds(0, L, stride=2), :].astype(BF16)

            @pl.when(head == 0)
            def _():
                c_ref[...] = rows

            @pl.when(head == 1)
            def _():
                c_ref[...] = jnp.where(lane < HD, c_ref[...], rows)


def attend(first, order, mask, qkv):
    heads = 2 if first == 0 else 1
    whole = lambda shape: pl.BlockSpec(shape, lambda h, i: (0,) * len(shape), pipeline_mode=pl.Buffered(1))
    per_step = lambda width: pl.BlockSpec((1, HALVES * STEP, width), lambda h, i: (h, i, 0))
    out_rows = L if first == 0 else L // 2
    return pl.pallas_call(
        functools.partial(attend_kernel, first),
        grid=(heads, L // STEP // HALVES),
        in_specs=[
            pl.BlockSpec(memory_space=pl.ANY),
            whole((1, L)),
            pl.BlockSpec((1, L, 2 * C), lambda h, i: (h + first, 0, 0)),
        ],
        out_specs=[whole((out_rows, C)), per_step(2 * C), per_step(C)],
        out_shape=[
            jax.ShapeDtypeStruct((out_rows, C), BF16),
            jax.ShapeDtypeStruct((heads, L, 2 * C), BF16),
            jax.ShapeDtypeStruct((heads, L, C), F32),
        ],
        scratch_shapes=[VMEM((2 * L, C), F32), VMEM((2 * L, C), F32)]
        + [VMEM((2 * GROUP * C, C), F32)] * 2 + [VMEM((GROUP * C, C), F32)] * 2
        + [pltpu.SMEM((STEP,), jnp.int32)] * HALVES + [pltpu.SemaphoreType.DMA((HALVES,))],
        compiler_params=pltpu.CompilerParams(vmem_limit_bytes=60 << 20),
        cost_estimate=pl.CostEstimate(flops=heads * 9 * 10**9, bytes_accessed=10 << 20, transcendentals=0),
        name="attend",
    )(order, mask, qkv)


def attend_back_kernel(head, ord_ref, g_ref, ts_ref, pr_ref, d_ref, gsrc, dst, *rest):
    slots, windows, sems = rest[:4], rest[4 : 4 + HALVES], rest[4 + HALVES]
    step = pl.program_id(0)
    lane = lax.broadcasted_iota(jnp.int32, (1, C), 1)

    @pl.when(step == 0)
    def _():
        if head == 2:
            for k in range(4):
                both = g_ref[pl.ds(k * 512, 512), :].astype(F32)
                gsrc[pl.ds(k * 2048, 512, stride=2), :] = both
                gsrc[pl.ds(k * 2048 + 1024, 512, stride=2), :] = pltpu.roll(both, HD, 1)
        else:
            gsrc[pl.ds(0, L, stride=2), :] = g_ref[...].astype(F32)

    keep = (lane >= HD) if head == 1 else (lane < HD)

    def work(n, window):
        def gather(group, buf):
            for u in range(GROUP * C):
                buf[pl.ds(u, 1), :] = gsrc[pl.ds(window[group * GROUP * C + u], 1), :]

        def compute(group, buf, out):
            each = range(GROUP)
            rows = [pl.ds(n * STEP + (group * GROUP + i) * C, C) for i in each]
            t0 = [ts_ref[0, rows[i], :C] for i in each]
            t1 = [ts_ref[0, rows[i], C:] for i in each]
            probs = [pr_ref[0, rows[i], :] for i in each]
            g = [jnp.where(keep, buf[pl.ds(i * C, C), :], 0.0).astype(BF16) for i in each]
            dp = [dot(t0[i], g[i], 1, 1) for i in each]
            ds = [(probs[i] * (dp[i] - jnp.sum(probs[i] * dp[i], axis=0, keepdims=True))).astype(BF16) for i in each]
            for i in each:
                grad = dot(ds[i], t1[i], 0, 0) * 0.125 + jnp.dot(probs[i].astype(BF16), g[i], preferred_element_type=F32)
                out[pl.ds(2 * i * C, C, stride=2), :] = grad
            for i in each:
                out[pl.ds(2 * i * C + 1, C, stride=2), :] = jnp.dot(ds[i], t0[i], preferred_element_type=F32) * 0.125

        def scatter(group, out):
            for u in range(GROUP * C):
                dst[pl.ds(pl.multiple_of(window[group * GROUP * C + u], 2), 2), :] = out[pl.ds(2 * u, 2), :]

        in_turn(gather, compute, scatter, slots[:2], slots[2:])

    each_window(ord_ref, windows, sems, head * (L // STEP), step, L // STEP // HALVES, work)

    @pl.when(step == L // STEP // HALVES - 1)
    def _():
        d_ref[:, :C] = dst[pl.ds(0, L, stride=2), :].astype(BF16)
        d_ref[:, C:] = dst[pl.ds(1, L, stride=2), :].astype(BF16)


def attend_back(head, order, g, ts, probs):
    whole = lambda shape: pl.BlockSpec(shape, lambda i: (0,) * len(shape), pipeline_mode=pl.Buffered(1))
    per_step = lambda width: pl.BlockSpec((1, HALVES * STEP, width), lambda i: (head % 2, i, 0))
    return pl.pallas_call(
        functools.partial(attend_back_kernel, head),
        grid=(L // STEP // HALVES,),
        in_specs=[
            pl.BlockSpec(memory_space=pl.ANY),
            whole(g.shape), per_step(2 * C), per_step(C),
        ],
        out_specs=whole((L, 2 * C)),
        out_shape=jax.ShapeDtypeStruct((L, 2 * C), BF16),
        scratch_shapes=[VMEM((2 * L, C), F32), VMEM((2 * L, C), F32)]
        + [VMEM((GROUP * C, C), F32)] * 2 + [VMEM((2 * GROUP * C, C), F32)] * 2
        + [pltpu.SMEM((STEP,), jnp.int32)] * HALVES + [pltpu.SemaphoreType.DMA((HALVES,))],
        compiler_params=pltpu.CompilerParams(vmem_limit_bytes=60 << 20),
        cost_estimate=pl.CostEstimate(flops=9 * 10**9, bytes_accessed=10 << 20, transcendentals=0),
        name="attend_back",
    )(order, g, ts, probs)


MESH = pl.DeviceIdType.MESH
WIDTH = 768
ROWS = 1024
SUB = 512
SUBS = ROWS // SUB
SHARE = 208
SHARE_ALL = SHARE + 32
QUARTER = 192
DMA = pltpu.SemaphoreType.DMA
ANY = pl.BlockSpec(memory_space=pl.ANY)
VM = pl.BlockSpec(memory_space=pltpu.VMEM)
sds = jax.ShapeDtypeStruct


def place():
    dp, mp = lax.axis_index("dp"), lax.axis_index("mp")
    core = lax.rem(dp, 2)
    return dp, mp, core, jnp.where(core == 0, mp, 3 - mp)


def at(dp, mp):
    return {"dp": dp, "mp": mp}


def signal(barrier, device):
    pl.semaphore_signal(barrier, inc=1, device_id=device, device_id_type=MESH)


def send(src, dst, send_sem, recv_sem, device):
    copy = pltpu.make_async_remote_copy(
        src_ref=src, dst_ref=dst, send_sem=send_sem, recv_sem=recv_sem, device_id=device, device_id_type=MESH
    )
    copy.start()
    return copy


def wait(ref, sem):
    pltpu.make_async_copy(ref, ref, sem).wait()


def mate(dp, rel):
    return dp + 2 * ((lax.rem(dp, 8) // 2 ^ rel) - lax.rem(dp, 8) // 2)


def greet(barrier, both_cores):
    dp, mp, core, t = place()
    step = 1 - 2 * core
    for k in range(4):
        if k:
            signal(barrier, at(dp, lax.rem(mp + k, 4)))
        signal(barrier, at(dp + step, lax.rem(mp + k, 4)))
    for rel in (1, 2, 3):
        signal(barrier, at(mate(dp, rel), mp))
        if both_cores:
            signal(barrier, at(mate(dp, rel) + step, mp))
    pl.semaphore_wait(barrier, 13 if both_cores else 10)


def worker(group, half, dp_base):
    return at(dp_base + group % 2, 2 * half + group // 2)


def chain_device(u, half, dp_base):
    return at(dp_base + half, jnp.where(half == 0, u, 3 - u))


def collect_kernel(x_ref, wq_ref, wk_ref, wv_ref, bsrc_ref, osrc_ref, msrc_ref, up_ref, down_ref, wout_ref, brow_ref,
                   xs_ref, qkv_ref, w_ref, ord_ref, mask_ref, share_ref,
                   xs, qkv, w, wsrc, bias, relay, up, up_t,
                   chain_recv, relay_recv, pair_recv, chain_send, relay_send, pair_send, own_sem,
                   wz_recv, wz_send, wp_recv, wp_send, b_recv, b_send, o_recv, o_send, m_recv, m_send, xs_out, qkv_out, w_out, build_sem, up_sem, share_sem):
    dp, mp, core, t = place()
    base, half, spot = dp - core, mp // 2, lax.rem(dp, 8) // 2
    step = 1 - 2 * core
    partner, lower, upper = at(dp + step, mp), at(dp, mp - step), at(dp, mp + step)
    group = lax.rem(mp, 2) * 2 + core
    gives = core == lax.rem(mp, 2)
    order_self = worker(mp, core, base)
    order_here = (order_self["dp"] == dp) & (order_self["mp"] == mp)
    cut = lambda s: pl.ds(s * SUB, SUB)
    home = lambda u, s: xs.at[pl.ds(pl.multiple_of(u * ROWS + s * SUB, SUB), SUB)]
    quarter = lambda q: pl.ds(pl.multiple_of(q * QUARTER, QUARTER), QUARTER)

    own = pltpu.make_async_copy(x_ref, xs.at[pl.ds(pl.multiple_of(jnp.minimum(t, 1) * ROWS, ROWS), ROWS)], own_sem)

    @pl.when(t <= 1)
    def _():
        own.start()

    parts = []
    for h in range(3):
        for n, part in enumerate((wq_ref, wv_ref, wk_ref, None) if h == 1 else (wv_ref, wq_ref, None, wk_ref)):
            rows = pl.ds((4 * h + n) * HD, HD)
            if part is None:
                wsrc[rows, :] = jnp.zeros((HD, WIDTH), BF16)
            else:
                copy = pltpu.make_async_copy(part.at[pl.ds(h * HD, HD)], wsrc.at[rows], build_sem.at[4 * h + n])
                copy.start()
                parts.append(copy)
    greet(pltpu.get_barrier_semaphore(), False)
    for copy in parts:
        copy.wait()

    for far in (0, 1):
        target = mp // 2 + 2 * far

        @pl.when(gives & (target != mp))
        def _():
            send(wsrc.at[quarter(spot)], w.at[quarter(spot)], wz_send.at[far], wz_recv, at(dp, target))
            send(bsrc_ref, bias, b_send.at[far], b_recv, at(dp, target))

        @pl.when(gives & (target == mp))
        def _():
            pltpu.make_async_copy(wsrc.at[quarter(spot)], w.at[quarter(spot)], wz_recv).start()
            pltpu.make_async_copy(bsrc_ref, bias, b_recv).start()

    @pl.when(order_here)
    def _():
        pltpu.make_async_copy(osrc_ref, ord_ref, o_recv).start()
        pltpu.make_async_copy(msrc_ref, mask_ref, m_recv).start()

    @pl.when(jnp.logical_not(order_here))
    def _():
        send(osrc_ref, ord_ref, o_send, o_recv, order_self)
        send(msrc_ref, mask_ref, m_send, m_recv, order_self)

    @pl.when(t == 3)
    def _():
        for s in range(SUBS):
            send(x_ref.at[cut(s)], relay.at[cut(s)], chain_send.at[0, s], relay_recv.at[s], lower)

    @pl.when((t == 1) | (t == 2))
    def _():
        for s in range(SUBS):
            send(x_ref.at[cut(s)], home(t, s), chain_send.at[0, s], chain_recv.at[t, s], lower)

    @pl.when(t == 0)
    def _():
        for s in range(SUBS):
            send(x_ref.at[cut(s)], home(0, s), chain_send.at[0, s], chain_recv.at[0, s], upper)

    number = lax.rem(dp, 8)
    units = pl.ds(pl.multiple_of(96 * number, 32), 96)
    out_rows = pl.ds(pl.multiple_of(32 * jnp.minimum(number, 5), 32), 32)
    load = pltpu.make_async_copy(up_ref, up, up_sem)
    load.start()
    made = [
        pltpu.make_async_copy(down_ref.at[units], share_ref.at[pl.ds(96, 96)], share_sem.at[0]),
        pltpu.make_async_copy(brow_ref, share_ref.at[pl.ds(192, 16)], share_sem.at[1]),
        pltpu.make_async_copy(wout_ref.at[out_rows], share_ref.at[pl.ds(SHARE, 32)], share_sem.at[2]),
    ]
    for copy in made:
        copy.start()

    wait(w.at[quarter(spot)], wz_recv)
    for rel in (1, 2, 3):
        send(w.at[quarter(spot)], w.at[quarter(spot)], wp_send.at[rel], wp_recv.at[rel], at(mate(dp, rel), mp))

    @pl.when(t <= 1)
    def _():
        own.wait()
        for s in range(SUBS):
            send(home(t, s), home(t, s), pair_send.at[t, s], pair_recv.at[t, s], partner)

    tt = jnp.minimum(t, 3 - t)

    def rows_of(i, s):
        return pl.ds(pl.multiple_of(lax.rem(tt + i, 4) * ROWS + s * SUB, SUB), SUB)

    def receive(i, s):
        u = lax.rem(tt + i, 4)
        if i == 1:
            @pl.when(t == 2)
            def _():
                wait(relay.at[cut(s)], relay_recv.at[s])
                send(relay.at[cut(s)], home(3, s), relay_send.at[s], chain_recv.at[3, s], lower)

        if i > 0:
            @pl.when(t <= 1)
            def _():
                wait(home(u, s), chain_recv.at[u, s])
                if i < 3:
                    @pl.when(t == 1)
                    def _():
                        send(home(u, s), home(u, s), chain_send.at[i, s], chain_recv.at[u, s], lower)
                send(home(u, s), home(u, s), pair_send.at[u, s], pair_recv.at[u, s], partner)

        @pl.when(t >= 2)
        def _():
            wait(home(u, s), pair_recv.at[u, s])

        rows = rows_of(i, s)
        pltpu.make_async_copy(xs.at[rows], xs_ref.at[rows], xs_out.at[i, s]).start()

    def project(i, s):
        rows = rows_of(i, s)
        row = jnp.concatenate([bias[pl.ds(h, 1), :] for h in range(3)], axis=1)
        qkv[rows, :] = (dot(xs[rows, :], w[...], 1, 1) + row).astype(BF16)
        for h in range(3):
            pltpu.make_async_copy(qkv.at[rows, pl.ds(h * 256, 256)], qkv_ref.at[h, rows], qkv_out.at[i, s, h]).start()

    pieces = [(i, s) for i in range(4) for s in range(SUBS)]
    for i, s in pieces[:4]:
        receive(i, s)
    for rel in (1, 2, 3):
        wait(w.at[quarter(spot ^ rel)], wp_recv.at[rel])
    wait(bias, b_recv)
    pltpu.make_async_copy(w, w_ref, w_out).start()
    for i, s in pieces[:3]:
        project(i, s)
    load.wait()
    up_t[...] = up[...].T
    made.append(pltpu.make_async_copy(up_t.at[units], share_ref.at[pl.ds(0, 96)], share_sem.at[3]))
    made[-1].start()
    for k in range(4, len(pieces)):
        receive(*pieces[k])
        project(*pieces[k - 1])
    project(*pieces[-1])

    for i in range(4):
        u = lax.rem(tt + i, 4)
        for s in range(SUBS):
            rows = pl.ds(pl.multiple_of(u * ROWS + s * SUB, SUB), SUB)
            wait(xs.at[rows], xs_out.at[i, s])
            for h in range(3):
                wait(qkv_ref.at[h, rows], qkv_out.at[i, s, h])

            @pl.when(t <= 1)
            def _():
                wait(home(u, s), pair_send.at[u, s])
    for s in range(SUBS):
        wait(x_ref.at[cut(s)], chain_send.at[0, s])

        @pl.when(t == 1)
        def _():
            wait(x_ref.at[cut(s)], chain_send.at[1, s])
            wait(x_ref.at[cut(s)], chain_send.at[2, s])

        @pl.when(t == 2)
        def _():
            wait(relay.at[cut(s)], relay_send.at[s])
    for rel in (1, 2, 3):
        wait(w.at[quarter(spot)], wp_send.at[rel])
    for far in (0, 1):
        @pl.when(gives & (mp // 2 + 2 * far != mp))
        def _():
            wait(wsrc.at[quarter(spot)], wz_send.at[far])
            wait(bsrc_ref, b_send.at[far])
    wait(ord_ref, o_recv)
    wait(mask_ref, m_recv)

    @pl.when(jnp.logical_not(order_here))
    def _():
        wait(osrc_ref, o_send)
        wait(msrc_ref, m_send)

    wait(w, w_out)
    for copy in made:
        copy.wait()


def collect(x, wq, wk, wv, b, order, mask, up, down, out, bias_row):
    return pl.pallas_call(
        collect_kernel,
        out_shape=[sds((4 * ROWS, WIDTH), BF16), sds((3, 4 * ROWS, 256), BF16), sds((WIDTH, WIDTH), BF16), sds((3 * L,), jnp.int32),
                   sds((1, L), jnp.int32), sds((SHARE_ALL, WIDTH), BF16)],
        in_specs=[ANY] * 11,
        out_specs=[ANY] * 6,
        scratch_shapes=[
            VMEM((4 * ROWS, WIDTH), BF16), VMEM((4 * ROWS, WIDTH), BF16), VMEM((WIDTH, WIDTH), BF16), VMEM((WIDTH, WIDTH), BF16),
            VMEM((8, 256), F32), VMEM((ROWS, WIDTH), BF16), VMEM((WIDTH, WIDTH), BF16), VMEM((WIDTH, WIDTH), BF16),
            DMA((4, SUBS)), DMA((SUBS,)), DMA((4, SUBS)), DMA((3, SUBS)), DMA((SUBS,)), DMA((4, SUBS)), DMA,
            DMA, DMA((2,)), DMA((4,)), DMA((4,)), DMA, DMA((2,)), DMA, DMA, DMA, DMA,
            DMA((4, SUBS)), DMA((4, SUBS, 3)), DMA, DMA((12,)), DMA, DMA((4,)),
        ],
        compiler_params=pltpu.CompilerParams(collective_id=0, has_side_effects=True, vmem_limit_bytes=60 << 20),
        name="collect",
    )(x, wq, wk, wv, b, order, mask, up, down, out, bias_row)


def greet_exchange(barrier):
    dp, mp, core, t = place()
    half, base = mp // 2, dp - core
    mine = lax.rem(mp, 2) * 2 + core
    for u in range(4):
        @pl.when((half != core) | (t != u))
        def _():
            pl.semaphore_signal(barrier, inc=1, device_id=chain_device(u, half, base), device_id_type=MESH)
    for g in range(4):
        @pl.when((half != core) | (mine != g))
        def _():
            pl.semaphore_signal(barrier, inc=1, device_id=worker(g, core, base), device_id_type=MESH)

    @pl.when(half == core)
    def _():
        pl.semaphore_wait(barrier, 6)

    @pl.when(half != core)
    def _():
        pl.semaphore_wait(barrier, 8)


def spread_kernel(a_ref, b_ref, oa_ref, ob_ref, send_sem, recv_sem, local_sem):
    dp, mp, core, t = place()
    half, base = mp // 2, dp - core
    mine = lax.rem(mp, 2) * 2 + core
    greet_exchange(pltpu.get_barrier_semaphore())
    for u in (3, 2, 1, 0):
        pair = ((a_ref.at[pl.ds(u * 1024, 1024)], oa_ref.at[mine]), (b_ref.at[pl.ds(u * 512, 512)], ob_ref.at[mine]))
        for k, (src, dst) in enumerate(pair):
            @pl.when((half != core) | (t != u))
            def _():
                send(src, dst, send_sem.at[u, k], recv_sem.at[mine, k], chain_device(u, half, base))

            @pl.when((half == core) & (t == u))
            def _():
                pltpu.make_async_copy(src, dst, local_sem.at[k]).start()
    for u in range(4):
        for k, src in enumerate((a_ref.at[pl.ds(u * 1024, 1024)], b_ref.at[pl.ds(u * 512, 512)])):
            @pl.when((half != core) | (t != u))
            def _():
                pltpu.make_async_copy(src, src, send_sem.at[u, k]).wait()
    for g in range(4):
        for k, dst in enumerate((oa_ref.at[g], ob_ref.at[g])):
            @pl.when((half != core) | (mine != g))
            def _():
                pltpu.make_async_copy(dst, dst, recv_sem.at[g, k]).wait()

            @pl.when((half == core) & (mine == g))
            def _():
                pltpu.make_async_copy(dst, dst, local_sem.at[k]).wait()


def spread(a, b):
    return pl.pallas_call(
        spread_kernel,
        out_shape=[jax.ShapeDtypeStruct((4, 1024, C), BF16), jax.ShapeDtypeStruct((4, 512, C), BF16)],
        in_specs=[ANY, ANY],
        out_specs=[ANY, ANY],
        scratch_shapes=[DMA((4, 2)), DMA((4, 2)), DMA((2,))],
        compiler_params=pltpu.CompilerParams(collective_id=1, has_side_effects=True),
        name="spread",
    )(a, b)


def regroup_kernel(a_ref, b_ref, oa_ref, ob_ref, send_sem, recv_sem, local_sem):
    dp, mp, core, t = place()
    half, base = mp // 2, dp - core
    mine = lax.rem(mp, 2) * 2 + core
    greet_exchange(pltpu.get_barrier_semaphore())
    big = lambda u: oa_ref.at[pl.ds(u * 1024, 1024)]
    small = lambda u: ob_ref.at[pl.ds(u * 512, 512)]
    for n in range(4):
        g = lax.rem(n + 2 * core, 4)
        for k, (src, dst) in enumerate(((a_ref.at[g], big(t)), (b_ref.at[g], small(t)))):
            @pl.when((half != core) | (mine != g))
            def _():
                send(src, dst, send_sem.at[g, k], recv_sem.at[t, k], worker(g, core, base))

            @pl.when((half == core) & (mine == g))
            def _():
                pltpu.make_async_copy(src, dst, local_sem.at[k]).start()
    for g in range(4):
        for k, src in enumerate((a_ref.at[g], b_ref.at[g])):
            @pl.when((half != core) | (mine != g))
            def _():
                pltpu.make_async_copy(src, src, send_sem.at[g, k]).wait()
    for u in range(4):
        for k, dst in enumerate((big(u), small(u))):
            @pl.when((half != core) | (t != u))
            def _():
                pltpu.make_async_copy(dst, dst, recv_sem.at[u, k]).wait()

            @pl.when((half == core) & (t == u))
            def _():
                pltpu.make_async_copy(dst, dst, local_sem.at[k]).wait()


def regroup(a, b):
    return pl.pallas_call(
        regroup_kernel,
        out_shape=[jax.ShapeDtypeStruct((4096, C), BF16), jax.ShapeDtypeStruct((2048, C), BF16)],
        in_specs=[ANY, ANY],
        out_specs=[ANY, ANY],
        scratch_shapes=[DMA((4, 2)), DMA((4, 2)), DMA((2,))],
        compiler_params=pltpu.CompilerParams(collective_id=2, has_side_effects=True),
        name="regroup",
    )(a, b)


def settle_kernel(d0_ref, d1_ref, d2_ref, xs_ref, w_ref, extra_ref, mine_ref, out_ref, *rest):
    pieces_out, rest = rest[:9], rest[9:]
    (heads_ref, grads_ref, stage, pair_in, chain_in, gw, gwl, h_in, z_in, z_out,
                  pair_recv, pair_send, chain_recv, chain_send, relay_send,
                  s_recv, s_send, c_recv, c_send, h_recv, h_send, z_recv, z_send, q_recv, q_send, out_sem) = rest
    dp, mp, core, t = place()
    base, spot = dp - core, lax.rem(dp, 8) // 2
    step = 1 - 2 * core
    partner, lower, upper = at(dp + step, mp), at(dp, mp - step), at(dp, mp + step)
    group = lax.rem(mp, 2) * 2 + core
    gives = core == lax.rem(mp, 2)
    quarter = lambda q: pl.ds(pl.multiple_of(q * QUARTER, QUARTER), QUARTER)
    share = lambda j, parity: grads_ref.at[2 * j + parity]

    greet(pltpu.get_barrier_semaphore(), True)

    grads_ref[2 * spot + core] = mine_ref[...]
    for rel in (1, 2, 3):
        send(mine_ref, share(spot, core), s_send.at[rel], s_recv.at[rel], at(mate(dp, rel), mp))

    def weight_gradients():
        gw[...] = jnp.zeros_like(gw)

        def part(i, sums):
            rows = pl.ds(pl.multiple_of(i * SUB, SUB), SUB)
            x = xs_ref[rows, :]
            new = []
            for h, d_ref in enumerate((d0_ref, d1_ref, d2_ref)):
                d = d_ref[rows, :]
                gw[pl.ds(h * 256, 256), :] += dot(d, x, 0, 0)
                new.append(sums[h] + jnp.sum(d.astype(F32), axis=0, keepdims=True))
            return tuple(new)

        sums = lax.fori_loop(0, 4 * ROWS // SUB, part, tuple(jnp.zeros((1, 256), F32) for _ in range(3)))
        gwl[...] = gw[...].astype(BF16)
        for h in range(3):
            line = jnp.concatenate([sums[h], jnp.zeros((1, WIDTH - 256), F32)], axis=1)
            spare = h * 256 + (192 if h == 1 else 128)
            gwl[pl.ds(spare, 16), :] = jnp.concatenate([line, jnp.zeros((15, WIDTH), F32)], axis=0).astype(BF16)
        for rel in (1, 2, 3):
            send(gwl.at[quarter(spot ^ rel)], h_in.at[rel], h_send.at[rel], h_recv.at[rel], at(mate(dp, rel), mp))

    def plane_sum():
        for rel in (1, 2, 3):
            wait(h_in.at[rel], h_recv.at[rel])
        half_sum = gwl[quarter(spot), :].astype(F32)
        for rel in (1, 2, 3):
            half_sum += h_in[rel].astype(F32)
        z_out[...] = half_sum.astype(BF16)

        @pl.when(mp != group)
        def _():
            send(z_out, z_in.at[mp // 2], z_send, z_recv.at[mp // 2], at(dp, group))

    tt = jnp.minimum(t, 3 - t)
    for i in range(3):
        u = lax.rem(3 - i + tt, 4)
        for s in range(SUBS):
            rows = pl.ds(pl.multiple_of(u * ROWS + s * SUB, SUB), SUB)
            value = jnp.zeros((SUB, WIDTH), F32)
            for h, d_ref in enumerate((d0_ref, d1_ref, d2_ref)):
                value += jnp.dot(d_ref[rows, :], w_ref[pl.ds(h * 256, 256), :], preferred_element_type=F32)

            @pl.when(t >= 2)
            def _():
                stage[rows, :] = value.astype(BF16)
                send(stage.at[rows], pair_in.at[rows], pair_send.at[i, s], pair_recv.at[i, s], partner)

            @pl.when(t <= 1)
            def _():
                wait(pair_in.at[rows], pair_recv.at[i, s])
                here = value + pair_in[rows, :].astype(F32)
                if i == 0:
                    stage[rows, :] = here.astype(BF16)
                else:
                    @pl.when(t == 1)
                    def _():
                        wait(chain_in.at[rows], chain_recv.at[u, s])
                        stage[rows, :] = (here + chain_in[rows, :].astype(F32)).astype(BF16)

                    @pl.when(t == 0)
                    def _():
                        stage[rows, :] = here.astype(BF16)

                @pl.when((t == 0) | (i > 0))
                def _():
                    send(stage.at[rows], chain_in.at[rows], chain_send.at[i, s], chain_recv.at[u, s], upper)

                if i == 0:
                    @pl.when(t == 1)
                    def _():
                        send(stage.at[rows], chain_in.at[rows], chain_send.at[i, s], chain_recv.at[u, s], lower)

        if i < 2:
            @pl.when(t == 1)
            def _():
                (weight_gradients, plane_sum)[i]()

    @pl.when(t != 1)
    def _():
        weight_gradients()

    for rel in (1, 2, 3):
        wait(share(spot ^ rel, core), s_recv.at[rel])
    for j in range(4):
        send(share(j, core), share(j, core), c_send.at[j], c_recv.at[j], partner)

    @pl.when(t == 2)
    def _():
        for s in range(SUBS):
            rows = pl.ds(3 * ROWS + s * SUB, SUB)
            wait(chain_in.at[rows], chain_recv.at[3, s])
            send(chain_in.at[rows], chain_in.at[rows], relay_send.at[s], chain_recv.at[3, s], upper)
            if s == 0:
                plane_sum()

    @pl.when((t == 0) | (t == 3))
    def _():
        plane_sum()

    for s in range(SUBS):
        rows = pl.ds(pl.multiple_of(tt * ROWS + s * SUB, SUB), SUB)
        cut = pl.ds(s * SUB, SUB)
        value = jnp.zeros((SUB, WIDTH), F32)
        for h, d_ref in enumerate((d0_ref, d1_ref, d2_ref)):
            value += jnp.dot(d_ref[rows, :], w_ref[pl.ds(h * 256, 256), :], preferred_element_type=F32)

        @pl.when(t >= 2)
        def _():
            stage[rows, :] = value.astype(BF16)
            send(stage.at[rows], pair_in.at[rows], pair_send.at[3, s], pair_recv.at[3, s], partner)

        @pl.when(t <= 1)
        def _():
            stage[rows, :] = value.astype(BF16)

    @pl.when(gives)
    def _():
        both = jnp.zeros((QUARTER, WIDTH), F32)
        for far in (0, 1):
            source = mp // 2 + 2 * far

            @pl.when(source == mp)
            def _():
                z_in[far] = z_out[...]

            @pl.when(source != mp)
            def _():
                wait(z_in.at[far], z_recv.at[far])

            both += z_in[far].astype(F32)
        heads_ref[quarter(spot), :] = both.astype(BF16)
        mine = heads_ref.at[quarter(spot)]
        send(mine, mine, q_send.at[0], q_recv.at[spot], partner)
        for rel in (1, 2, 3):
            send(mine, mine, q_send.at[rel], q_recv.at[spot], at(mate(dp, rel), mp))
            send(mine, mine, q_send.at[rel + 3], q_recv.at[spot], at(mate(dp, rel) + step, mp))

    for s in range(SUBS):
        cut = pl.ds(s * SUB, SUB)
        rows = pl.ds(pl.multiple_of(t * ROWS + s * SUB, SUB), SUB)
        wait(chain_in.at[rows], chain_recv.at[t, s])
        value = extra_ref[cut, :] + chain_in[rows, :].astype(F32)

        @pl.when(t <= 1)
        def _():
            wait(pair_in.at[rows], pair_recv.at[3, s])
            out_ref[cut, :] = (value + stage[rows, :].astype(F32) + pair_in[rows, :].astype(F32)).astype(BF16)

        @pl.when(t >= 2)
        def _():
            out_ref[cut, :] = value.astype(BF16)

    for q in range(4):
        @pl.when(jnp.logical_not(gives) | (spot != q))
        def _():
            wait(heads_ref.at[quarter(q)], q_recv.at[q])
    for j in range(4):
        wait(share(j, 1 - core), c_recv.at[j])
    copies = []
    for i in range(8):
        for n, (first, rows) in enumerate(((0, 96), (96, 96), (192, 32), (224, 16))):
            if n == 2 and i >= 6:
                continue
            dst = pieces_out[3 + n].at[pl.ds(i * rows, rows)]
            copies.append(pltpu.make_async_copy(grads_ref.at[i, pl.ds(first, rows)], dst, out_sem.at[20 + 4 * i + n]))
    copies.append(pltpu.make_async_copy(grads_ref.at[6, pl.ds(192, 16)], pieces_out[8], out_sem.at[0]))
    for h in range(3):
        for n, where in enumerate((0, 2, 1) if h == 1 else (1, 3, 0)):
            src = heads_ref.at[pl.ds((4 * h + where) * HD, HD)]
            copies.append(pltpu.make_async_copy(src, pieces_out[n].at[pl.ds(h * HD, HD)], out_sem.at[8 + 3 * h + n]))
        src = heads_ref.at[pl.ds(h * 256 + (192 if h == 1 else 128), 16)]
        copies.append(pltpu.make_async_copy(src, pieces_out[7].at[h], out_sem.at[17 + h]))
    for copy in copies:
        copy.start()

    for s in range(SUBS):
        piece = stage.at[pl.ds(s * SUB, SUB)]

        @pl.when(t >= 2)
        def _():
            for i in range(4):
                wait(piece, pair_send.at[i, s])

        @pl.when(t <= 1)
        def _():
            for i in range(3):
                wait(piece, chain_send.at[i, s])

        @pl.when(t == 2)
        def _():
            wait(piece, relay_send.at[s])
    for rel in (1, 2, 3):
        wait(mine_ref, s_send.at[rel])
        wait(z_out, h_send.at[rel])
    for j in range(4):
        wait(mine_ref, c_send.at[j])

    @pl.when(mp != group)
    def _():
        wait(z_out, z_send)

    @pl.when(gives)
    def _():
        for k in range(7):
            wait(z_out, q_send.at[k])

    for copy in copies:
        copy.wait()


def settle(d0, d1, d2, xs, w, extra, mine):
    return pl.pallas_call(
        settle_kernel,
        out_shape=[sds((ROWS, WIDTH), BF16)] + [sds((rows, WIDTH), BF16) for rows in (192, 192, 192, 768, 768, 192, 128)]
        + [sds((3, 16, WIDTH), BF16), sds((16, WIDTH), BF16)],
        in_specs=[VM] * 7,
        out_specs=[VM] + [ANY] * 9,
        scratch_shapes=[VMEM((WIDTH, WIDTH), BF16), VMEM((8, SHARE_ALL, WIDTH), BF16)] + [VMEM((4 * ROWS, WIDTH), BF16)] * 3 + [
            VMEM((WIDTH, WIDTH), F32), VMEM((WIDTH, WIDTH), BF16), VMEM((4, QUARTER, WIDTH), BF16), VMEM((2, QUARTER, WIDTH), BF16),
            VMEM((QUARTER, WIDTH), BF16),
            DMA((4, SUBS)), DMA((4, SUBS)), DMA((4, SUBS)), DMA((3, SUBS)), DMA((SUBS,)),
            DMA((4,)), DMA((4,)), DMA((4,)), DMA((4,)), DMA((4,)), DMA((4,)), DMA((2,)), DMA, DMA((4,)), DMA((7,)), DMA((52,)),
        ],
        compiler_params=pltpu.CompilerParams(collective_id=3, has_side_effects=True, vmem_limit_bytes=60 << 20),
        name="settle",
    )(d0, d1, d2, xs, w, extra, mine)


EPS = 1e-12
CHUNK = 512
FF_MODEL = 768


def gelu_and_slope(v):
    size = jnp.abs(v)
    u = 1.0 / (1.0 + (0.3275911 * 0.7071067811865476) * size)
    bell = jnp.exp2(v * v * -0.7213475204444817 - 1.3257480647361595)
    poly = u * (0.3193815306 + u * (-0.3565637784 + u * (1.7814779345 + u * (-1.8212559786 + u * 1.3302744294))))
    tail = poly * bell
    cdf = jnp.where(v < 0, tail, 1.0 - tail)
    return v * cdf, cdf + v * bell


def row_mean(v):
    return jnp.sum(v, axis=-1, keepdims=True) * (1.0 / FF_MODEL)


def ffn_kernel(c01_ref, c2_ref, tok_ref, cot_ref, vec_ref, near_ref, a_ref, b_ref,
               out_ref, res_ref, g01_ref, g2_ref, keep_ref, next_ref, give_ref, keep_tail_ref, give_tail_ref,
               w, wout, ctx, x, gf, act, slope, zhat, acc, rstd, cols, recv, recv2, tail, tail_in,
               o_local, o_send, o_recv, f_send, f_recv, w_local, w_send, w_recv, d_send, d_recv,
               g_send, g_recv, m_send, m_recv, t_send, t_recv, out_sem, tail_sem):
    dp, mp, core, t = place()
    step = 1 - 2 * core
    partner = at(dp + step, mp)
    spot = lax.rem(dp, 8) // 2
    one, two = jnp.where(core == 0, 1, 2), jnp.where(core == 0, 2, 1)
    mate_a, mate_b = at(dp + 2 * ((spot ^ one) - spot), mp), at(dp + 2 * ((spot ^ two) - spot), mp)
    shard = lambda k: lax.rem(mp - k + 4, 4)
    barrier = pltpu.get_barrier_semaphore()
    for device in (partner, mate_a, mate_b):
        signal(barrier, device)
    pl.semaphore_wait(barrier, 3)

    def out_rows(m, i):
        first = jnp.where(i < 4, m * C + 32 * i, 4 * C + m * HD + 32 * (i - 4))
        return wout.at[pl.ds(pl.multiple_of(first, 32), 32)]

    sources = ((0, near_ref), (one, a_ref), (two, b_ref))
    far = spot ^ 3
    for k in range(4):
        @pl.when(spot ^ one < 3)
        def _():
            send(a_ref.at[k, pl.ds(SHARE, 32)], out_rows(shard(k), 2 * (spot ^ one) + core), f_send.at[k], f_recv.at[k], mate_b)
    for rel, ref in sources:
        j = spot ^ rel
        for k in range(4):
            src = ref.at[k, pl.ds(SHARE, 32)]

            @pl.when(j < 3)
            def _():
                pltpu.make_async_copy(src, out_rows(shard(k), 2 * j + core), o_local.at[j, k]).start()
                send(src, out_rows(shard(k), 2 * j + core), o_send.at[j, k], o_recv.at[j, k], partner)

    body = pl.ds(0, SHARE)
    for k in range(4):
        send(a_ref.at[k, body], w.at[2 * (spot ^ one) + core, shard(k)], d_send.at[k], d_recv.at[k], mate_b)
    for rel, ref in sources:
        for k in range(4):
            mine = w.at[2 * (spot ^ rel) + core, shard(k)]
            pltpu.make_async_copy(ref.at[k, body], mine, w_local.at[rel, k]).start()
            send(ref.at[k, body], mine, w_send.at[rel, k], w_recv.at[rel, k], partner)

    lane = lax.broadcasted_iota(jnp.int32, (1, C), 1)
    for g in range(4):
        ctx[:, pl.ds(g * C, C)] = c01_ref[g]
    for g in (0, 2):
        a, b = c2_ref[g].astype(F32), c2_ref[g + 1].astype(F32)
        col = pl.ds(4 * C + g * HD, C)
        ctx[pl.ds(0, 512), col] = jnp.where(lane < HD, a, pltpu.roll(b, HD, 1)).astype(BF16)
        ctx[pl.ds(512, 512), col] = jnp.where(lane < HD, pltpu.roll(a, HD, 1), b).astype(BF16)
    cols[...] = jnp.zeros_like(cols)
    b_out, gain1, bias1, b_down, gain2, bias2 = (vec_ref[pl.ds(i, 1), :] for i in range(6))
    row_chunks = [pl.ds(r * CHUNK, CHUNK) for r in range(1024 // CHUNK)]

    part = wout.at[pl.ds(0, 32)]
    for k in range(4):
        @pl.when(far < 3)
        def _():
            mine = out_rows(shard(k), 2 * far + core)
            wait(mine, f_recv.at[k])
            send(mine, mine, o_send.at[far, k], o_recv.at[far, k], partner)
    for j in range(3):
        for k in range(4):
            @pl.when(far != j)
            def _():
                wait(part, o_local.at[j, k])

            wait(part, o_recv.at[j, k])

    for rows in row_chunks:
        h = jnp.dot(ctx[rows, :], wout[...], preferred_element_type=F32) + tok_ref[rows, :].astype(F32) + b_out
        h = h - row_mean(h)
        scale = lax.rsqrt(row_mean(h * h) + EPS)
        rstd[rows, :] = scale
        h = h * scale
        zhat[rows, :] = h
        first = h * gain1 + bias1
        acc[rows, :] = first + b_down
        x[rows, :] = first.astype(BF16)

    whole = w.at[0, 0]
    up_pair = lambda j: w[pl.ds(2 * j, 2), :, pl.ds(0, 96), :].reshape(768, FF_MODEL)
    down_pair = lambda j: w[pl.ds(2 * j, 2), :, pl.ds(96, 96), :].reshape(768, FF_MODEL)

    def up(j, rel, rows):
        bias = [jnp.sum(w[2 * j + f, :, pl.ds(192, 16), :].astype(F32), axis=0)[0:1, :384] for f in range(2)]
        pre = dot(x[rows, :], up_pair(j), 1, 1) + jnp.concatenate(bias, axis=1)
        value, grad = gelu_and_slope(pre)
        act[rel, rows, :] = value.astype(BF16)
        slope[rel, rows, :] = grad.astype(BF16)

    def down(j, rel, rows):
        acc[rows, :] += jnp.dot(act[rel, rows, :], down_pair(j), preferred_element_type=F32)

    for rel in range(4):
        j = spot ^ rel
        if rel == 2:
            for k in range(4):
                mine = w.at[2 * (spot ^ 3) + core, shard(k)]
                wait(mine, d_recv.at[k])
                send(mine, mine, w_send.at[3, k], w_recv.at[3, k], partner)
        for k in range(4):
            if rel < 3:
                wait(whole, w_local.at[rel, k])
            wait(whole, w_recv.at[rel, k])
        before = None
        for rows in row_chunks:
            up(j, rel, rows)
            if before is not None:
                down(j, rel, before)
            before = rows
        down(j, rel, before)

    for rows in row_chunks:
        z = acc[rows, :]
        z = z - row_mean(z)
        scale = lax.rsqrt(row_mean(z * z) + EPS)
        z = z * scale
        out_ref[rows, :] = (z * gain2 + bias2).astype(BF16)
        cot = cot_ref[rows, :].astype(F32)
        dz = cot * gain2
        gs = scale * (dz - row_mean(dz) - z * row_mean(dz * z))
        cols[pl.ds(2, 1), :] += jnp.sum(cot * z, axis=0, keepdims=True)
        cols[pl.ds(3, 1), :] += jnp.sum(cot, axis=0, keepdims=True)
        cols[pl.ds(5, 1), :] += jnp.sum(gs, axis=0, keepdims=True)
        acc[rows, :] = gs
        gf[rows, :] = gs.astype(BF16)

    for rel in range(4):
        for k in range(4):
            wait(whole, w_send.at[rel, k])
    for k in range(4):
        wait(whole, d_send.at[k])

    grads = pl.ds(0, 192)
    order = (3, 1, 2, 0)
    place_of = {rel: q for q, rel in enumerate(order)}

    def add_cores(rel):
        q, i = place_of[rel], 2 * (spot ^ rel) + core
        wait(recv.at[q], g_recv.at[q])
        for m in range(4):
            recv[q, m] = (recv[q, m].astype(F32) + w[i, m, grads, :].astype(F32)).astype(BF16)
        if rel == 3:
            send(recv.at[q], recv2, m_send, m_recv, mate_a)
        elif rel == 0:
            pltpu.make_async_copy(recv.at[q], keep_ref, out_sem.at[0]).start()
        else:
            @pl.when(one == rel)
            def _():
                pltpu.make_async_copy(recv.at[q], next_ref, out_sem.at[1]).start()

    for q, rel in enumerate(order):
        j = spot ^ rel
        for rows in row_chunks:
            ga = dot(gf[rows, :], down_pair(j), 1, 1)
            slope[rel, rows, :] = (ga * slope[rel, rows, :].astype(F32)).astype(BF16)
            acc[rows, :] += jnp.dot(slope[rel, rows, :], up_pair(j), preferred_element_type=F32)
        for f in range(2):
            cut = pl.ds(f * 384, 384)
            gp = slope[rel, :, cut]
            w[2 * j + f, :, pl.ds(0, 96), :] = dot(gp, x[...], 0, 0).astype(BF16).reshape(4, 96, FF_MODEL)
            w[2 * j + f, :, pl.ds(96, 96), :] = dot(act[rel, :, cut], gf[...], 0, 0).astype(BF16).reshape(4, 96, FF_MODEL)
            cols[pl.ds(8 + 2 * j + f, 1), pl.ds(0, 384)] = jnp.sum(gp.astype(F32), axis=0, keepdims=True)
        send(w.at[2 * j + 1 - core, :, grads], recv.at[q], g_send.at[q], g_recv.at[q], partner)
        if q:
            add_cores(order[q - 1])

    ctx_grad = x.at[:, pl.ds(0, 2 * C)]
    for rows in row_chunks:
        grad = acc[rows, :]
        z = zhat[rows, :]
        dz = grad * gain1
        gr = rstd[rows, :] * (dz - row_mean(dz) - z * row_mean(dz * z))
        cols[pl.ds(0, 1), :] += jnp.sum(grad * z, axis=0, keepdims=True)
        cols[pl.ds(1, 1), :] += jnp.sum(grad, axis=0, keepdims=True)
        cols[pl.ds(4, 1), :] += jnp.sum(gr, axis=0, keepdims=True)
        res_ref[rows, :] = gr
        low = gr.astype(BF16)
        gf[rows, :] = low
        gc = dot(low, wout[...], 1, 1).astype(BF16)
        for g in range(4):
            g01_ref[g, rows, :] = gc[:, g * C : g * C + C]
        ctx_grad[rows, :] = gc[:, 4 * C :]
    for g in (0, 2):
        top = ctx_grad[pl.ds(0, 512), pl.ds(g * HD, C)].astype(F32)
        low = ctx_grad[pl.ds(512, 512), pl.ds(g * HD, C)].astype(F32)
        g2_ref[g] = jnp.where(lane < HD, top, pltpu.roll(low, HD, 1)).astype(BF16)
        g2_ref[g + 1] = jnp.where(lane < HD, pltpu.roll(top, HD, 1), low).astype(BF16)

    for n in range(3):
        got = dot(ctx[:, pl.ds(n * 256, 256)], gf[...], 0, 0).astype(BF16)
        for i in range(8):
            piece = got[i * 32 : i * 32 + 32, :]
            m, share = (2 * n + i // 4, i % 4) if n < 2 else (i // 2, 4 + i % 2)
            tail[share % 2, share // 2, m, pl.ds(0, 32), :] = piece
    vectors = jnp.concatenate([cols[pl.ds(0, 6), :], jnp.zeros((26, FF_MODEL), F32)], axis=0).astype(BF16)
    for i in range(8):
        line = jnp.concatenate([cols[pl.ds(8 + i, 1), :], jnp.zeros((15, FF_MODEL), F32)], axis=0).astype(BF16)
        for m in range(4):
            tail[i % 2, i // 2, m, pl.ds(32, 16), :] = line
            if i >= 6:
                tail[i % 2, i // 2, m, pl.ds(0, 32), :] = vectors if i == 6 else jnp.zeros((32, FF_MODEL), BF16)
    send(tail.at[1 - core], tail_in, t_send, t_recv, partner)
    add_cores(0)

    wait(recv2, m_recv)
    for rel in (1, 2):
        @pl.when(two == rel)
        def _():
            for m in range(4):
                recv2[m] = (recv2[m].astype(F32) + recv[place_of[rel], m].astype(F32)).astype(BF16)
    give = pltpu.make_async_copy(recv2, give_ref, out_sem.at[2])
    give.start()
    wait(tail_in, t_recv)
    for rel in range(4):
        j = spot ^ rel
        for m in range(4):
            tail_in[j, m] = (tail_in[j, m].astype(F32) + tail[core, j, m].astype(F32)).astype(BF16)
        along, across = jnp.where(core == 0, rel % 2, rel // 2), jnp.where(core == 0, rel // 2, rel % 2)
        for side, ref in enumerate((keep_tail_ref, give_tail_ref)):
            @pl.when(along == side)
            def _():
                pltpu.make_async_copy(tail_in.at[j], ref.at[across], tail_sem.at[rel]).start()
    give.wait()
    wait(recv2, out_sem.at[0])
    wait(recv2, out_sem.at[1])
    for rel in range(4):
        wait(tail_in.at[0], tail_sem.at[rel])
    for q in range(4):
        wait(recv.at[q], g_send.at[q])
    wait(recv2, m_send)
    wait(tail_in, t_send)
    for k in range(4):
        @pl.when(spot ^ one < 3)
        def _():
            wait(part, f_send.at[k])

        for j in range(3):
            wait(part, o_send.at[j, k])


def ffn(c01, c2, tokens, cot, vecs, near, a, b):
    main, rest = sds((4, 192, WIDTH), BF16), sds((2, 4, 48, WIDTH), BF16)
    rows = lambda dtype: VMEM((1024, WIDTH), dtype)
    four = lambda *shape: VMEM((4,) + shape, BF16)
    return pl.pallas_call(
        ffn_kernel,
        out_shape=[sds((1024, WIDTH), BF16), sds((1024, WIDTH), F32), sds((4, 1024, C), BF16), sds((4, 512, C), BF16), main, main, main, rest, rest],
        in_specs=[VM] * 5 + [ANY] * 3,
        out_specs=[VM] * 4 + [ANY] * 5,
        scratch_shapes=[
            VMEM((8, 4, SHARE, WIDTH), BF16), VMEM((WIDTH, WIDTH), BF16), rows(BF16), rows(BF16), rows(BF16), four(1024, WIDTH), four(1024, WIDTH),
            rows(F32), rows(F32), VMEM((1024, 1), F32), VMEM((16, WIDTH), F32), four(4, 192, WIDTH), four(192, WIDTH),
            VMEM((2, 4, 4, 48, WIDTH), BF16), four(4, 48, WIDTH),
        ] + [DMA((4, 4))] * 3 + [DMA((4,))] * 2 + [DMA((4, 4))] * 3 + [DMA((4,))] * 4 + [DMA] * 4 + [DMA((3,)), DMA((4,))],
        compiler_params=pltpu.CompilerParams(collective_id=4, has_side_effects=True, vmem_limit_bytes=63 << 20),
        name="ffn",
    )(c01, c2, tokens, cot, vecs, near, a, b)


def swap(value, even_bits, odd_bits, n_dp):
    return lax.ppermute(value, "dp", [(d, d ^ (odd_bits if d % 2 else even_bits)) for d in range(n_dp)])


def pick(value, index, axis):
    return lax.dynamic_index_in_dim(value, index, axis, keepdims=False)


def total(a, b):
    return (a.astype(F32) + b.astype(F32)).astype(BF16)


def tie(*values):
    return lax.optimization_barrier(values)


def body(n_dp, tokens, w_query, b_query, w_key, w_value, b_value, w_out, b_out, norm1_gain, norm1_bias, w_up, b_up, w_down,
         b_down, norm2_gain, norm2_bias, key_mask, cluster_order, cotangent):
    dp, mp, core, t = place()
    ring = lambda k: [(z, (z + k) % 4) for z in range(4)]

    order = 2 * jnp.where(core == 1, cluster_order ^ 3072, cluster_order).reshape(3 * L)
    bq, bv, bz = b_query.reshape(3, HD), b_value.reshape(3, HD), jnp.zeros((C,), F32)
    b_heads = jnp.stack([jnp.concatenate([bq[h], bv[h], bz] if h == 1 else [bv[h], bq[h], bz]) for h in range(3)])
    b_heads = jnp.concatenate([b_heads, jnp.zeros((5, 256), F32)])
    units = lax.dynamic_slice(b_up, (96 * (dp % 8),), (96,)).reshape(1, 96)
    bias_row = lax.dynamic_update_slice(jnp.zeros((16, WIDTH), BF16), units, (0, 96 * mp))

    xs, qkv, w_heads, order, mask, share = collect(
        tokens, w_query.T, w_key.T, w_value.T, b_heads, order, key_mask, w_up, w_down, w_out, bias_row
    )
    qkv, share = tie(qkv, share)
    shares = [share] + [lax.ppermute(share, "mp", ring(i)) for i in (1, 2, 3)]
    c01, ts01, probs01 = attend(0, order, mask, qkv)
    c01, qkv = tie(c01, qkv)
    c2, ts2, probs2 = attend(2, order, mask, qkv)
    c2, *shares = tie(c2, *shares)
    near = jnp.stack(shares)
    along, across = swap(near, 2, 4, n_dp), swap(near, 4, 2, n_dp)
    c01, c2 = spread(c01, c2)

    vecs = jnp.stack([b_out, norm1_gain, norm1_bias, b_down, norm2_gain, norm2_bias, b_out, b_out])
    layer_out, grad_residual, g01, g2, keep, nearer, give, keep_tail, give_tail = ffn(
        c01, c2, tokens, cotangent, vecs, near, along, across
    )

    got, got_nearer, got_tail = swap(give, 4, 2, n_dp), swap(nearer, 2, 4, n_dp), swap(give_tail, 2, 4, n_dp)
    g01, g2 = regroup(g01, g2)
    g01, keep, got, got_nearer, keep_tail, got_tail = tie(g01, keep, got, got_nearer, keep_tail, got_tail)
    groups = [1 << bit for bit in range(3, n_dp.bit_length() - 1)]

    def shard_sums(sums):
        for bits in groups:
            sums = total(sums, swap(sums, bits, bits, n_dp))
        return [pick(sums, mp, 0)] + [lax.ppermute(pick(sums, (mp + k) % 4, 0), "mp", ring(k)) for k in (1, 2, 3)]

    keep = (keep.astype(F32) + got_nearer.astype(F32) + got.astype(F32)).astype(BF16)
    keep_tail, give_tail = total(keep_tail[0], got_tail[0]), total(keep_tail[1], got_tail[1])
    got_tail = swap(give_tail, 4, 2, n_dp)
    d0 = attend_back(0, order, g01, ts01, probs01)
    d0, order, keep, keep_tail, got_tail = tie(d0, order, keep, keep_tail, got_tail)
    parts = shard_sums(jnp.concatenate([keep, total(keep_tail, got_tail)], axis=1))
    d1 = attend_back(1, order, g01, ts01, probs01)
    d2 = attend_back(2, order, g2, ts2, probs2)
    d2, *parts = tie(d2, *parts)
    mine = sum(p.astype(F32) for p in parts).astype(BF16)
    grad_tokens, *sums = settle(d0, d1, d2, xs, w_heads, grad_residual, mine)
    hq, hk, hv, g_up, g_down, g_out, units, spare, vectors = (s.astype(F32) for s in sums)
    for bits in groups:
        hq, hk, hv, spare = (s + swap(s, bits, bits, n_dp) for s in (hq, hk, hv, spare))
    sums_of = lambda where: jnp.concatenate([spare[h, 0, where[h] : where[h] + HD] for h in range(3)])
    g_b_up = lax.dynamic_slice(units.reshape(8, 16, WIDTH)[:, 0], (0, 96 * mp), (8, 96)).reshape(WIDTH)
    return (
        layer_out,
        grad_tokens,
        hq.T,
        sums_of((HD, 0, HD)),
        hk.T,
        hv.T,
        sums_of((0, HD, 0)),
        g_out,
        vectors[4],
        vectors[0],
        vectors[1],
        g_up.T,
        g_b_up,
        g_down,
        vectors[5],
        vectors[2],
        vectors[3],
    )


def solution(mesh):
    return jax.shard_map(
        functools.partial(body, mesh.shape["dp"]),
        mesh=mesh,
        in_specs=(
            P(("dp", "mp"), None), P(None, "mp"), P("mp"), P(None, "mp"), P(None, "mp"), P("mp"), P("mp", None), P(), P(), P(),
            P(None, "mp"), P("mp"), P("mp", None), P(), P(), P(), P("dp", None), P("dp", "mp", None), P(("dp", "mp"), None),
        ),
        out_specs=(
            P(("dp", "mp"), None), P(("dp", "mp"), None), P(None, "mp"), P("mp"), P(None, "mp"), P(None, "mp"), P("mp"),
            P("mp", None), P(), P(), P(), P(None, "mp"), P("mp"), P("mp", None), P(), P(), P(),
        ),
        check_vma=False,
    )
```

```python
import functools
import jax
import jax.numpy as jnp
from jax import lax
from jax.experimental import pallas as pl
from jax.experimental.pallas import tpu as pltpu
from jax.sharding import PartitionSpec as P

L = 4096
C = 128
HD = 64
GROUP = 2
STEP = 1024
GROUPS = STEP // (GROUP * C)
HALVES = 2
F32 = jnp.float32
BF16 = jnp.bfloat16
VMEM = pltpu.VMEM


def dot(a, b, da, db):
    return lax.dot_general(a, b, (((da,), (db,)), ((), ())), preferred_element_type=F32)


def in_turn(gather, compute, scatter, bufs, outs):
    gather(0, bufs[0])
    for group in range(GROUPS):
        if group + 1 < GROUPS:
            gather(group + 1, bufs[(group + 1) % 2])
        compute(group, bufs[group % 2], outs[group % 2])
        if group:
            scatter(group - 1, outs[(group - 1) % 2])
    scatter(GROUPS - 1, outs[(GROUPS - 1) % 2])


def each_window(ord_ref, windows, sems, first, step, steps, work):
    def fetch(n, at_step):
        start = pl.multiple_of((first + at_step * HALVES + n) * STEP, STEP)
        return pltpu.make_async_copy(ord_ref.at[pl.ds(start, STEP)], windows[n], sems.at[n])

    @pl.when(step == 0)
    def _():
        for n in range(HALVES):
            fetch(n, step).start()

    for n in range(HALVES):
        fetch(n, step).wait()
        work(n, windows[n])

        @pl.when(step + 1 < steps)
        def _():
            fetch(n, step + 1).start()


def attend_kernel(first, ord_ref, mask_ref, qkv_ref, c_ref, ts_ref, pr_ref, src, ctx, *rest):
    slots, windows, sems = rest[:4], rest[4 : 4 + HALVES], rest[4 + HALVES]
    head, step = pl.program_id(0) + first, pl.program_id(1)
    live = jnp.sum(mask_ref[...].astype(F32), axis=1, keepdims=True).astype(jnp.int32)

    @pl.when(step == 0)
    def _():
        src[pl.ds(0, L, stride=2), :] = qkv_ref[0, :, :C].astype(F32)
        src[pl.ds(1, L, stride=2), :] = qkv_ref[0, :, C:].astype(F32)

    def work(n, window):
        def gather(group, buf):
            for u in range(GROUP * C):
                buf[pl.ds(2 * u, 2), :] = src[pl.ds(pl.multiple_of(window[group * GROUP * C + u], 2), 2), :]

        def compute(group, buf, out):
            each = range(GROUP)
            rows = [pl.ds(n * STEP + (group * GROUP + i) * C, C) for i in each]
            t0 = [buf[pl.ds(2 * i * C, C, stride=2), :].astype(BF16) for i in each]
            t1 = [buf[pl.ds(2 * i * C + 1, C, stride=2), :].astype(BF16) for i in each]
            for i in each:
                ts_ref[0, rows[i], :C] = t0[i]
                ts_ref[0, rows[i], C:] = t1[i]
            slot = [(step * HALVES + n) * STEP + (group * GROUP + i) * C + lax.broadcasted_iota(jnp.int32, (C, C), 0) for i in each]
            scores = [dot(t1[i], t0[i], 1, 1) * 0.125 + jnp.where(slot[i] < live, 0.0, -10000.0) for i in each]
            e = [jnp.exp(scores[i] - jnp.max(scores[i], axis=0, keepdims=True)) for i in each]
            probs = [e[i] * (1.0 / jnp.sum(e[i], axis=0, keepdims=True)) for i in each]
            for i in each:
                pr_ref[0, rows[i], :] = probs[i]
            for i in each:
                out[pl.ds(i * C, C), :] = dot(probs[i].astype(BF16), t0[i], 0, 0)

        def scatter(group, out):
            for u in range(GROUP * C):
                ctx[pl.ds(window[group * GROUP * C + u], 1), :] = out[pl.ds(u, 1), :]

        in_turn(gather, compute, scatter, slots[:2], slots[2:])

    each_window(ord_ref, windows, sems, head * (L // STEP), step, L // STEP // HALVES, work)

    @pl.when(step == L // STEP // HALVES - 1)
    def _():
        lane = lax.broadcasted_iota(jnp.int32, (1, C), 1)
        if first == 2:
            for k in range(4):
                low = ctx[pl.ds(k * 2048, 512, stride=2), :]
                high = pltpu.roll(ctx[pl.ds(k * 2048 + 1024, 512, stride=2), :], HD, 1)
                c_ref[pl.ds(k * 512, 512), :] = jnp.where(lane < HD, low, high).astype(BF16)
        else:
            rows = ctx[pl.ds(0, L, stride=2), :].astype(BF16)

            @pl.when(head == 0)
            def _():
                c_ref[...] = rows

            @pl.when(head == 1)
            def _():
                c_ref[...] = jnp.where(lane < HD, c_ref[...], rows)


def attend(first, order, mask, qkv):
    heads = 2 if first == 0 else 1
    whole = lambda shape: pl.BlockSpec(shape, lambda h, i: (0,) * len(shape), pipeline_mode=pl.Buffered(1))
    per_step = lambda width: pl.BlockSpec((1, HALVES * STEP, width), lambda h, i: (h, i, 0))
    out_rows = L if first == 0 else L // 2
    return pl.pallas_call(
        functools.partial(attend_kernel, first),
        grid=(heads, L // STEP // HALVES),
        in_specs=[
            pl.BlockSpec(memory_space=pl.ANY),
            whole((1, L)),
            pl.BlockSpec((1, L, 2 * C), lambda h, i: (h + first, 0, 0)),
        ],
        out_specs=[whole((out_rows, C)), per_step(2 * C), per_step(C)],
        out_shape=[
            jax.ShapeDtypeStruct((out_rows, C), BF16),
            jax.ShapeDtypeStruct((heads, L, 2 * C), BF16),
            jax.ShapeDtypeStruct((heads, L, C), F32),
        ],
        scratch_shapes=[VMEM((2 * L, C), F32), VMEM((2 * L, C), F32)]
        + [VMEM((2 * GROUP * C, C), F32)] * 2 + [VMEM((GROUP * C, C), F32)] * 2
        + [pltpu.SMEM((STEP,), jnp.int32)] * HALVES + [pltpu.SemaphoreType.DMA((HALVES,))],
        compiler_params=pltpu.CompilerParams(vmem_limit_bytes=60 << 20),
        cost_estimate=pl.CostEstimate(flops=heads * 9 * 10**9, bytes_accessed=10 << 20, transcendentals=0),
        name="attend",
    )(order, mask, qkv)


def attend_back_kernel(head, ord_ref, g_ref, ts_ref, pr_ref, d_ref, gsrc, dst, *rest):
    slots, windows, sems = rest[:4], rest[4 : 4 + HALVES], rest[4 + HALVES]
    step = pl.program_id(0)
    lane = lax.broadcasted_iota(jnp.int32, (1, C), 1)

    @pl.when(step == 0)
    def _():
        if head == 2:
            for k in range(4):
                both = g_ref[pl.ds(k * 512, 512), :].astype(F32)
                gsrc[pl.ds(k * 2048, 512, stride=2), :] = both
                gsrc[pl.ds(k * 2048 + 1024, 512, stride=2), :] = pltpu.roll(both, HD, 1)
        else:
            gsrc[pl.ds(0, L, stride=2), :] = g_ref[...].astype(F32)

    keep = (lane >= HD) if head == 1 else (lane < HD)

    def work(n, window):
        def gather(group, buf):
            for u in range(GROUP * C):
                buf[pl.ds(u, 1), :] = gsrc[pl.ds(window[group * GROUP * C + u], 1), :]

        def compute(group, buf, out):
            each = range(GROUP)
            rows = [pl.ds(n * STEP + (group * GROUP + i) * C, C) for i in each]
            t0 = [ts_ref[0, rows[i], :C] for i in each]
            t1 = [ts_ref[0, rows[i], C:] for i in each]
            probs = [pr_ref[0, rows[i], :] for i in each]
            g = [jnp.where(keep, buf[pl.ds(i * C, C), :], 0.0).astype(BF16) for i in each]
            dp = [dot(t0[i], g[i], 1, 1) for i in each]
            ds = [(probs[i] * (dp[i] - jnp.sum(probs[i] * dp[i], axis=0, keepdims=True))).astype(BF16) for i in each]
            for i in each:
                grad = dot(ds[i], t1[i], 0, 0) * 0.125 + jnp.dot(probs[i].astype(BF16), g[i], preferred_element_type=F32)
                out[pl.ds(2 * i * C, C, stride=2), :] = grad
            for i in each:
                out[pl.ds(2 * i * C + 1, C, stride=2), :] = jnp.dot(ds[i], t0[i], preferred_element_type=F32) * 0.125

        def scatter(group, out):
            for u in range(GROUP * C):
                dst[pl.ds(pl.multiple_of(window[group * GROUP * C + u], 2), 2), :] = out[pl.ds(2 * u, 2), :]

        in_turn(gather, compute, scatter, slots[:2], slots[2:])

    each_window(ord_ref, windows, sems, head * (L // STEP), step, L // STEP // HALVES, work)

    @pl.when(step == L // STEP // HALVES - 1)
    def _():
        d_ref[:, :C] = dst[pl.ds(0, L, stride=2), :].astype(BF16)
        d_ref[:, C:] = dst[pl.ds(1, L, stride=2), :].astype(BF16)


def attend_back(head, order, g, ts, probs):
    whole = lambda shape: pl.BlockSpec(shape, lambda i: (0,) * len(shape), pipeline_mode=pl.Buffered(1))
    per_step = lambda width: pl.BlockSpec((1, HALVES * STEP, width), lambda i: (head % 2, i, 0))
    return pl.pallas_call(
        functools.partial(attend_back_kernel, head),
        grid=(L // STEP // HALVES,),
        in_specs=[
            pl.BlockSpec(memory_space=pl.ANY),
            whole(g.shape), per_step(2 * C), per_step(C),
        ],
        out_specs=whole((L, 2 * C)),
        out_shape=jax.ShapeDtypeStruct((L, 2 * C), BF16),
        scratch_shapes=[VMEM((2 * L, C), F32), VMEM((2 * L, C), F32)]
        + [VMEM((GROUP * C, C), F32)] * 2 + [VMEM((2 * GROUP * C, C), F32)] * 2
        + [pltpu.SMEM((STEP,), jnp.int32)] * HALVES + [pltpu.SemaphoreType.DMA((HALVES,))],
        compiler_params=pltpu.CompilerParams(vmem_limit_bytes=60 << 20),
        cost_estimate=pl.CostEstimate(flops=9 * 10**9, bytes_accessed=10 << 20, transcendentals=0),
        name="attend_back",
    )(order, g, ts, probs)


MESH = pl.DeviceIdType.MESH
WIDTH = 768
ROWS = 1024
SUB = 512
SUBS = ROWS // SUB
SHARE = 208
SHARE_ALL = SHARE + 32
QUARTER = 192
DMA = pltpu.SemaphoreType.DMA
ANY = pl.BlockSpec(memory_space=pl.ANY)
VM = pl.BlockSpec(memory_space=pltpu.VMEM)
sds = jax.ShapeDtypeStruct


def place():
    dp, mp = lax.axis_index("dp"), lax.axis_index("mp")
    core = lax.rem(dp, 2)
    return dp, mp, core, jnp.where(core == 0, mp, 3 - mp)


def at(dp, mp):
    return {"dp": dp, "mp": mp}


def signal(barrier, device):
    pl.semaphore_signal(barrier, inc=1, device_id=device, device_id_type=MESH)


def send(src, dst, send_sem, recv_sem, device):
    copy = pltpu.make_async_remote_copy(
        src_ref=src, dst_ref=dst, send_sem=send_sem, recv_sem=recv_sem, device_id=device, device_id_type=MESH
    )
    copy.start()
    return copy


def wait(ref, sem):
    pltpu.make_async_copy(ref, ref, sem).wait()


def mate(dp, rel):
    return dp + 2 * ((lax.rem(dp, 8) // 2 ^ rel) - lax.rem(dp, 8) // 2)


def greet(barrier, both_cores):
    dp, mp, core, t = place()
    step = 1 - 2 * core
    for k in range(4):
        if k:
            signal(barrier, at(dp, lax.rem(mp + k, 4)))
        signal(barrier, at(dp + step, lax.rem(mp + k, 4)))
    for rel in (1, 2, 3):
        signal(barrier, at(mate(dp, rel), mp))
        if both_cores:
            signal(barrier, at(mate(dp, rel) + step, mp))
    pl.semaphore_wait(barrier, 13 if both_cores else 10)


def worker(group, half, dp_base):
    return at(dp_base + group % 2, 2 * half + group // 2)


def chain_device(u, half, dp_base):
    return at(dp_base + half, jnp.where(half == 0, u, 3 - u))


def collect_kernel(x_ref, wq_ref, wk_ref, wv_ref, bsrc_ref, osrc_ref, msrc_ref, up_ref, down_ref, wout_ref, brow_ref,
                   xs_ref, qkv_ref, w_ref, ord_ref, mask_ref, share_ref,
                   xs, qkv, w, wsrc, bias, relay, up, up_t,
                   chain_recv, relay_recv, pair_recv, chain_send, relay_send, pair_send, own_sem,
                   wz_recv, wz_send, wp_recv, wp_send, b_recv, b_send, o_recv, o_send, m_recv, m_send, xs_out, qkv_out, w_out, build_sem, up_sem, share_sem):
    dp, mp, core, t = place()
    base, half, spot = dp - core, mp // 2, lax.rem(dp, 8) // 2
    step = 1 - 2 * core
    partner, lower, upper = at(dp + step, mp), at(dp, mp - step), at(dp, mp + step)
    group = lax.rem(mp, 2) * 2 + core
    gives = core == lax.rem(mp, 2)
    order_self = worker(mp, core, base)
    order_here = (order_self["dp"] == dp) & (order_self["mp"] == mp)
    cut = lambda s: pl.ds(s * SUB, SUB)
    home = lambda u, s: xs.at[pl.ds(pl.multiple_of(u * ROWS + s * SUB, SUB), SUB)]
    quarter = lambda q: pl.ds(pl.multiple_of(q * QUARTER, QUARTER), QUARTER)

    own = pltpu.make_async_copy(x_ref, xs.at[pl.ds(pl.multiple_of(jnp.minimum(t, 1) * ROWS, ROWS), ROWS)], own_sem)

    @pl.when(t <= 1)
    def _():
        own.start()

    parts = []
    for h in range(3):
        for n, part in enumerate((wq_ref, wv_ref, wk_ref, None) if h == 1 else (wv_ref, wq_ref, None, wk_ref)):
            rows = pl.ds((4 * h + n) * HD, HD)
            if part is None:
                wsrc[rows, :] = jnp.zeros((HD, WIDTH), BF16)
            else:
                copy = pltpu.make_async_copy(part.at[pl.ds(h * HD, HD)], wsrc.at[rows], build_sem.at[4 * h + n])
                copy.start()
                parts.append(copy)
    greet(pltpu.get_barrier_semaphore(), False)
    for copy in parts:
        copy.wait()

    for far in (0, 1):
        target = mp // 2 + 2 * far

        @pl.when(gives & (target != mp))
        def _():
            send(wsrc.at[quarter(spot)], w.at[quarter(spot)], wz_send.at[far], wz_recv, at(dp, target))
            send(bsrc_ref, bias, b_send.at[far], b_recv, at(dp, target))

        @pl.when(gives & (target == mp))
        def _():
            pltpu.make_async_copy(wsrc.at[quarter(spot)], w.at[quarter(spot)], wz_recv).start()
            pltpu.make_async_copy(bsrc_ref, bias, b_recv).start()

    @pl.when(order_here)
    def _():
        pltpu.make_async_copy(osrc_ref, ord_ref, o_recv).start()
        pltpu.make_async_copy(msrc_ref, mask_ref, m_recv).start()

    @pl.when(jnp.logical_not(order_here))
    def _():
        send(osrc_ref, ord_ref, o_send, o_recv, order_self)
        send(msrc_ref, mask_ref, m_send, m_recv, order_self)

    @pl.when(t == 3)
    def _():
        for s in range(SUBS):
            send(x_ref.at[cut(s)], relay.at[cut(s)], chain_send.at[0, s], relay_recv.at[s], lower)

    @pl.when((t == 1) | (t == 2))
    def _():
        for s in range(SUBS):
            send(x_ref.at[cut(s)], home(t, s), chain_send.at[0, s], chain_recv.at[t, s], lower)

    @pl.when(t == 0)
    def _():
        for s in range(SUBS):
            send(x_ref.at[cut(s)], home(0, s), chain_send.at[0, s], chain_recv.at[0, s], upper)

    number = lax.rem(dp, 8)
    units = pl.ds(pl.multiple_of(96 * number, 32), 96)
    out_rows = pl.ds(pl.multiple_of(32 * jnp.minimum(number, 5), 32), 32)
    load = pltpu.make_async_copy(up_ref, up, up_sem)
    load.start()
    made = [
        pltpu.make_async_copy(down_ref.at[units], share_ref.at[pl.ds(96, 96)], share_sem.at[0]),
        pltpu.make_async_copy(brow_ref, share_ref.at[pl.ds(192, 16)], share_sem.at[1]),
        pltpu.make_async_copy(wout_ref.at[out_rows], share_ref.at[pl.ds(SHARE, 32)], share_sem.at[2]),
    ]
    for copy in made:
        copy.start()

    wait(w.at[quarter(spot)], wz_recv)
    for rel in (1, 2, 3):
        send(w.at[quarter(spot)], w.at[quarter(spot)], wp_send.at[rel], wp_recv.at[rel], at(mate(dp, rel), mp))

    @pl.when(t <= 1)
    def _():
        own.wait()
        for s in range(SUBS):
            send(home(t, s), home(t, s), pair_send.at[t, s], pair_recv.at[t, s], partner)

    tt = jnp.minimum(t, 3 - t)

    def rows_of(i, s):
        return pl.ds(pl.multiple_of(lax.rem(tt + i, 4) * ROWS + s * SUB, SUB), SUB)

    def receive(i, s):
        u = lax.rem(tt + i, 4)
        if i == 1:
            @pl.when(t == 2)
            def _():
                wait(relay.at[cut(s)], relay_recv.at[s])
                send(relay.at[cut(s)], home(3, s), relay_send.at[s], chain_recv.at[3, s], lower)

        if i > 0:
            @pl.when(t <= 1)
            def _():
                wait(home(u, s), chain_recv.at[u, s])
                if i < 3:
                    @pl.when(t == 1)
                    def _():
                        send(home(u, s), home(u, s), chain_send.at[i, s], chain_recv.at[u, s], lower)
                send(home(u, s), home(u, s), pair_send.at[u, s], pair_recv.at[u, s], partner)

        @pl.when(t >= 2)
        def _():
            wait(home(u, s), pair_recv.at[u, s])

        rows = rows_of(i, s)
        pltpu.make_async_copy(xs.at[rows], xs_ref.at[rows], xs_out.at[i, s]).start()

    def project(i, s):
        rows = rows_of(i, s)
        row = jnp.concatenate([bias[pl.ds(h, 1), :] for h in range(3)], axis=1)
        qkv[rows, :] = (dot(xs[rows, :], w[...], 1, 1) + row).astype(BF16)
        for h in range(3):
            pltpu.make_async_copy(qkv.at[rows, pl.ds(h * 256, 256)], qkv_ref.at[h, rows], qkv_out.at[i, s, h]).start()

    pieces = [(i, s) for i in range(4) for s in range(SUBS)]
    for i, s in pieces[:4]:
        receive(i, s)
    for rel in (1, 2, 3):
        wait(w.at[quarter(spot ^ rel)], wp_recv.at[rel])
    wait(bias, b_recv)
    pltpu.make_async_copy(w, w_ref, w_out).start()
    for i, s in pieces[:3]:
        project(i, s)
    load.wait()
    up_t[...] = up[...].T
    made.append(pltpu.make_async_copy(up_t.at[units], share_ref.at[pl.ds(0, 96)], share_sem.at[3]))
    made[-1].start()
    for k in range(4, len(pieces)):
        receive(*pieces[k])
        project(*pieces[k - 1])
    project(*pieces[-1])

    for i in range(4):
        u = lax.rem(tt + i, 4)
        for s in range(SUBS):
            rows = pl.ds(pl.multiple_of(u * ROWS + s * SUB, SUB), SUB)
            wait(xs.at[rows], xs_out.at[i, s])
            for h in range(3):
                wait(qkv_ref.at[h, rows], qkv_out.at[i, s, h])

            @pl.when(t <= 1)
            def _():
                wait(home(u, s), pair_send.at[u, s])
    for s in range(SUBS):
        wait(x_ref.at[cut(s)], chain_send.at[0, s])

        @pl.when(t == 1)
        def _():
            wait(x_ref.at[cut(s)], chain_send.at[1, s])
            wait(x_ref.at[cut(s)], chain_send.at[2, s])

        @pl.when(t == 2)
        def _():
            wait(relay.at[cut(s)], relay_send.at[s])
    for rel in (1, 2, 3):
        wait(w.at[quarter(spot)], wp_send.at[rel])
    for far in (0, 1):
        @pl.when(gives & (mp // 2 + 2 * far != mp))
        def _():
            wait(wsrc.at[quarter(spot)], wz_send.at[far])
            wait(bsrc_ref, b_send.at[far])
    wait(ord_ref, o_recv)
    wait(mask_ref, m_recv)

    @pl.when(jnp.logical_not(order_here))
    def _():
        wait(osrc_ref, o_send)
        wait(msrc_ref, m_send)

    wait(w, w_out)
    for copy in made:
        copy.wait()


def collect(x, wq, wk, wv, b, order, mask, up, down, out, bias_row):
    return pl.pallas_call(
        collect_kernel,
        out_shape=[sds((4 * ROWS, WIDTH), BF16), sds((3, 4 * ROWS, 256), BF16), sds((WIDTH, WIDTH), BF16), sds((3 * L,), jnp.int32),
                   sds((1, L), jnp.int32), sds((SHARE_ALL, WIDTH), BF16)],
        in_specs=[ANY] * 11,
        out_specs=[ANY] * 6,
        scratch_shapes=[
            VMEM((4 * ROWS, WIDTH), BF16), VMEM((4 * ROWS, WIDTH), BF16), VMEM((WIDTH, WIDTH), BF16), VMEM((WIDTH, WIDTH), BF16),
            VMEM((8, 256), F32), VMEM((ROWS, WIDTH), BF16), VMEM((WIDTH, WIDTH), BF16), VMEM((WIDTH, WIDTH), BF16),
            DMA((4, SUBS)), DMA((SUBS,)), DMA((4, SUBS)), DMA((3, SUBS)), DMA((SUBS,)), DMA((4, SUBS)), DMA,
            DMA, DMA((2,)), DMA((4,)), DMA((4,)), DMA, DMA((2,)), DMA, DMA, DMA, DMA,
            DMA((4, SUBS)), DMA((4, SUBS, 3)), DMA, DMA((12,)), DMA, DMA((4,)),
        ],
        compiler_params=pltpu.CompilerParams(collective_id=0, has_side_effects=True, vmem_limit_bytes=60 << 20),
        name="collect",
    )(x, wq, wk, wv, b, order, mask, up, down, out, bias_row)


def greet_exchange(barrier):
    dp, mp, core, t = place()
    half, base = mp // 2, dp - core
    mine = lax.rem(mp, 2) * 2 + core
    for u in range(4):
        @pl.when((half != core) | (t != u))
        def _():
            pl.semaphore_signal(barrier, inc=1, device_id=chain_device(u, half, base), device_id_type=MESH)
    for g in range(4):
        @pl.when((half != core) | (mine != g))
        def _():
            pl.semaphore_signal(barrier, inc=1, device_id=worker(g, core, base), device_id_type=MESH)

    @pl.when(half == core)
    def _():
        pl.semaphore_wait(barrier, 6)

    @pl.when(half != core)
    def _():
        pl.semaphore_wait(barrier, 8)


def spread_kernel(a_ref, b_ref, oa_ref, ob_ref, send_sem, recv_sem, local_sem):
    dp, mp, core, t = place()
    half, base = mp // 2, dp - core
    mine = lax.rem(mp, 2) * 2 + core
    greet_exchange(pltpu.get_barrier_semaphore())
    for u in (3, 2, 1, 0):
        pair = ((a_ref.at[pl.ds(u * 1024, 1024)], oa_ref.at[mine]), (b_ref.at[pl.ds(u * 512, 512)], ob_ref.at[mine]))
        for k, (src, dst) in enumerate(pair):
            @pl.when((half != core) | (t != u))
            def _():
                send(src, dst, send_sem.at[u, k], recv_sem.at[mine, k], chain_device(u, half, base))

            @pl.when((half == core) & (t == u))
            def _():
                pltpu.make_async_copy(src, dst, local_sem.at[k]).start()
    for u in range(4):
        for k, src in enumerate((a_ref.at[pl.ds(u * 1024, 1024)], b_ref.at[pl.ds(u * 512, 512)])):
            @pl.when((half != core) | (t != u))
            def _():
                pltpu.make_async_copy(src, src, send_sem.at[u, k]).wait()
    for g in range(4):
        for k, dst in enumerate((oa_ref.at[g], ob_ref.at[g])):
            @pl.when((half != core) | (mine != g))
            def _():
                pltpu.make_async_copy(dst, dst, recv_sem.at[g, k]).wait()

            @pl.when((half == core) & (mine == g))
            def _():
                pltpu.make_async_copy(dst, dst, local_sem.at[k]).wait()


def spread(a, b):
    return pl.pallas_call(
        spread_kernel,
        out_shape=[jax.ShapeDtypeStruct((4, 1024, C), BF16), jax.ShapeDtypeStruct((4, 512, C), BF16)],
        in_specs=[ANY, ANY],
        out_specs=[ANY, ANY],
        scratch_shapes=[DMA((4, 2)), DMA((4, 2)), DMA((2,))],
        compiler_params=pltpu.CompilerParams(collective_id=1, has_side_effects=True),
        name="spread",
    )(a, b)


def regroup_kernel(a_ref, b_ref, oa_ref, ob_ref, send_sem, recv_sem, local_sem):
    dp, mp, core, t = place()
    half, base = mp // 2, dp - core
    mine = lax.rem(mp, 2) * 2 + core
    greet_exchange(pltpu.get_barrier_semaphore())
    big = lambda u: oa_ref.at[pl.ds(u * 1024, 1024)]
    small = lambda u: ob_ref.at[pl.ds(u * 512, 512)]
    for n in range(4):
        g = lax.rem(n + 2 * core, 4)
        for k, (src, dst) in enumerate(((a_ref.at[g], big(t)), (b_ref.at[g], small(t)))):
            @pl.when((half != core) | (mine != g))
            def _():
                send(src, dst, send_sem.at[g, k], recv_sem.at[t, k], worker(g, core, base))

            @pl.when((half == core) & (mine == g))
            def _():
                pltpu.make_async_copy(src, dst, local_sem.at[k]).start()
    for g in range(4):
        for k, src in enumerate((a_ref.at[g], b_ref.at[g])):
            @pl.when((half != core) | (mine != g))
            def _():
                pltpu.make_async_copy(src, src, send_sem.at[g, k]).wait()
    for u in range(4):
        for k, dst in enumerate((big(u), small(u))):
            @pl.when((half != core) | (t != u))
            def _():
                pltpu.make_async_copy(dst, dst, recv_sem.at[u, k]).wait()

            @pl.when((half == core) & (t == u))
            def _():
                pltpu.make_async_copy(dst, dst, local_sem.at[k]).wait()


def regroup(a, b):
    return pl.pallas_call(
        regroup_kernel,
        out_shape=[jax.ShapeDtypeStruct((4096, C), BF16), jax.ShapeDtypeStruct((2048, C), BF16)],
        in_specs=[ANY, ANY],
        out_specs=[ANY, ANY],
        scratch_shapes=[DMA((4, 2)), DMA((4, 2)), DMA((2,))],
        compiler_params=pltpu.CompilerParams(collective_id=2, has_side_effects=True),
        name="regroup",
    )(a, b)


def settle_kernel(d0_ref, d1_ref, d2_ref, xs_in, w_ref, extra_in, mine_ref, out_ref, *rest):
    pieces_out, rest = rest[:9], rest[9:]
    (xs_ref, extra_ref, up_t, in_sem, heads_ref, grads_ref, stage, pair_in, chain_in, gw, gwl, h_in, z_in, z_out,
                  pair_recv, pair_send, chain_recv, chain_send, relay_send,
                  s_recv, s_send, c_recv, c_send, h_recv, h_send, z_recv, z_send, q_recv, q_send, out_sem) = rest
    dp, mp, core, t = place()
    base, spot = dp - core, lax.rem(dp, 8) // 2
    step = 1 - 2 * core
    partner, lower, upper = at(dp + step, mp), at(dp, mp - step), at(dp, mp + step)
    group = lax.rem(mp, 2) * 2 + core
    gives = core == lax.rem(mp, 2)
    quarter = lambda q: pl.ds(pl.multiple_of(q * QUARTER, QUARTER), QUARTER)
    share = lambda j, parity: grads_ref.at[2 * j + parity]

    later = [pltpu.make_async_copy(src, dst, in_sem.at[n]) for n, (src, dst) in enumerate(((xs_in, xs_ref), (extra_in, extra_ref)))]
    for copy in later:
        copy.start()
    greet(pltpu.get_barrier_semaphore(), True)

    grads_ref[2 * spot + core] = mine_ref[...]
    for rel in (1, 2, 3):
        send(mine_ref, share(spot, core), s_send.at[rel], s_recv.at[rel], at(mate(dp, rel), mp))

    def weight_gradients():
        later[0].wait()
        gw[...] = jnp.zeros_like(gw)

        def part(i, sums):
            rows = pl.ds(pl.multiple_of(i * SUB, SUB), SUB)
            x = xs_ref[rows, :]
            new = []
            for h, d_ref in enumerate((d0_ref, d1_ref, d2_ref)):
                d = d_ref[rows, :]
                gw[pl.ds(h * 256, 256), :] += dot(d, x, 0, 0)
                new.append(sums[h] + jnp.sum(d.astype(F32), axis=0, keepdims=True))
            return tuple(new)

        sums = lax.fori_loop(0, 4 * ROWS // SUB, part, tuple(jnp.zeros((1, 256), F32) for _ in range(3)))
        gwl[...] = gw[...].astype(BF16)
        for h in range(3):
            line = jnp.concatenate([sums[h], jnp.zeros((1, WIDTH - 256), F32)], axis=1)
            spare = h * 256 + (192 if h == 1 else 128)
            gwl[pl.ds(spare, 16), :] = jnp.concatenate([line, jnp.zeros((15, WIDTH), F32)], axis=0).astype(BF16)
        for rel in (1, 2, 3):
            send(gwl.at[quarter(spot ^ rel)], h_in.at[rel], h_send.at[rel], h_recv.at[rel], at(mate(dp, rel), mp))

    def plane_sum():
        for rel in (1, 2, 3):
            wait(h_in.at[rel], h_recv.at[rel])
        half_sum = gwl[quarter(spot), :].astype(F32)
        for rel in (1, 2, 3):
            half_sum += h_in[rel].astype(F32)
        z_out[...] = half_sum.astype(BF16)

        @pl.when(mp != group)
        def _():
            send(z_out, z_in.at[mp // 2], z_send, z_recv.at[mp // 2], at(dp, group))

    tt = jnp.minimum(t, 3 - t)
    for i in range(3):
        u = lax.rem(3 - i + tt, 4)
        for s in range(SUBS):
            rows = pl.ds(pl.multiple_of(u * ROWS + s * SUB, SUB), SUB)
            value = jnp.zeros((SUB, WIDTH), F32)
            for h, d_ref in enumerate((d0_ref, d1_ref, d2_ref)):
                value += jnp.dot(d_ref[rows, :], w_ref[pl.ds(h * 256, 256), :], preferred_element_type=F32)

            @pl.when(t >= 2)
            def _():
                stage[rows, :] = value.astype(BF16)
                send(stage.at[rows], pair_in.at[rows], pair_send.at[i, s], pair_recv.at[i, s], partner)

            @pl.when(t <= 1)
            def _():
                wait(pair_in.at[rows], pair_recv.at[i, s])
                here = value + pair_in[rows, :].astype(F32)
                if i == 0:
                    stage[rows, :] = here.astype(BF16)
                else:
                    @pl.when(t == 1)
                    def _():
                        wait(chain_in.at[rows], chain_recv.at[u, s])
                        stage[rows, :] = (here + chain_in[rows, :].astype(F32)).astype(BF16)

                    @pl.when(t == 0)
                    def _():
                        stage[rows, :] = here.astype(BF16)

                @pl.when((t == 0) | (i > 0))
                def _():
                    send(stage.at[rows], chain_in.at[rows], chain_send.at[i, s], chain_recv.at[u, s], upper)

                if i == 0:
                    @pl.when(t == 1)
                    def _():
                        send(stage.at[rows], chain_in.at[rows], chain_send.at[i, s], chain_recv.at[u, s], lower)

        if i < 2:
            @pl.when(t == 1)
            def _():
                (weight_gradients, plane_sum)[i]()

    @pl.when(t != 1)
    def _():
        weight_gradients()

    for rel in (1, 2, 3):
        wait(share(spot ^ rel, core), s_recv.at[rel])
    for j in range(4):
        send(share(j, core), share(j, core), c_send.at[j], c_recv.at[j], partner)

    @pl.when(t == 2)
    def _():
        for s in range(SUBS):
            rows = pl.ds(3 * ROWS + s * SUB, SUB)
            wait(chain_in.at[rows], chain_recv.at[3, s])
            send(chain_in.at[rows], chain_in.at[rows], relay_send.at[s], chain_recv.at[3, s], upper)
            if s == 0:
                plane_sum()

    @pl.when((t == 0) | (t == 3))
    def _():
        plane_sum()

    for s in range(SUBS):
        rows = pl.ds(pl.multiple_of(tt * ROWS + s * SUB, SUB), SUB)
        cut = pl.ds(s * SUB, SUB)
        value = jnp.zeros((SUB, WIDTH), F32)
        for h, d_ref in enumerate((d0_ref, d1_ref, d2_ref)):
            value += jnp.dot(d_ref[rows, :], w_ref[pl.ds(h * 256, 256), :], preferred_element_type=F32)

        @pl.when(t >= 2)
        def _():
            stage[rows, :] = value.astype(BF16)
            send(stage.at[rows], pair_in.at[rows], pair_send.at[3, s], pair_recv.at[3, s], partner)

        @pl.when(t <= 1)
        def _():
            stage[rows, :] = value.astype(BF16)

    @pl.when(gives)
    def _():
        both = jnp.zeros((QUARTER, WIDTH), F32)
        for far in (0, 1):
            source = mp // 2 + 2 * far

            @pl.when(source == mp)
            def _():
                z_in[far] = z_out[...]

            @pl.when(source != mp)
            def _():
                wait(z_in.at[far], z_recv.at[far])

            both += z_in[far].astype(F32)
        heads_ref[quarter(spot), :] = both.astype(BF16)
        mine = heads_ref.at[quarter(spot)]
        send(mine, mine, q_send.at[0], q_recv.at[spot], partner)
        for rel in (1, 2, 3):
            send(mine, mine, q_send.at[rel], q_recv.at[spot], at(mate(dp, rel), mp))
            send(mine, mine, q_send.at[rel + 3], q_recv.at[spot], at(mate(dp, rel) + step, mp))

    for j in range(4):
        wait(share(j, 1 - core), c_recv.at[j])
    up_t[...] = grads_ref[:, pl.ds(0, 96), :].reshape(WIDTH, WIDTH).T
    copies = [pltpu.make_async_copy(up_t, pieces_out[3], out_sem.at[1])]
    for i in range(8):
        for n, (first, rows) in enumerate(((0, 96), (96, 96), (192, 32), (224, 16))):
            if n == 0 or (n == 2 and i >= 6):
                continue
            dst = pieces_out[3 + n].at[pl.ds(i * rows, rows)]
            copies.append(pltpu.make_async_copy(grads_ref.at[i, pl.ds(first, rows)], dst, out_sem.at[20 + 4 * i + n]))
    copies.append(pltpu.make_async_copy(grads_ref.at[6, pl.ds(192, 16)], pieces_out[8], out_sem.at[0]))
    early = len(copies)
    for copy in copies:
        copy.start()
    later[1].wait()

    for s in range(SUBS):
        cut = pl.ds(s * SUB, SUB)
        rows = pl.ds(pl.multiple_of(t * ROWS + s * SUB, SUB), SUB)
        wait(chain_in.at[rows], chain_recv.at[t, s])
        value = extra_ref[cut, :] + chain_in[rows, :].astype(F32)

        @pl.when(t <= 1)
        def _():
            wait(pair_in.at[rows], pair_recv.at[3, s])
            out_ref[cut, :] = (value + stage[rows, :].astype(F32) + pair_in[rows, :].astype(F32)).astype(BF16)

        @pl.when(t >= 2)
        def _():
            out_ref[cut, :] = value.astype(BF16)

    for q in range(4):
        @pl.when(jnp.logical_not(gives) | (spot != q))
        def _():
            wait(heads_ref.at[quarter(q)], q_recv.at[q])
    for h in range(3):
        for n, where in enumerate((0, 2, 1) if h == 1 else (1, 3, 0)):
            src = heads_ref.at[pl.ds((4 * h + where) * HD, HD)]
            copies.append(pltpu.make_async_copy(src, pieces_out[n].at[pl.ds(h * HD, HD)], out_sem.at[8 + 3 * h + n]))
        src = heads_ref.at[pl.ds(h * 256 + (192 if h == 1 else 128), 16)]
        copies.append(pltpu.make_async_copy(src, pieces_out[7].at[h], out_sem.at[17 + h]))
    for copy in copies[early:]:
        copy.start()

    for s in range(SUBS):
        piece = stage.at[pl.ds(s * SUB, SUB)]

        @pl.when(t >= 2)
        def _():
            for i in range(4):
                wait(piece, pair_send.at[i, s])

        @pl.when(t <= 1)
        def _():
            for i in range(3):
                wait(piece, chain_send.at[i, s])

        @pl.when(t == 2)
        def _():
            wait(piece, relay_send.at[s])
    for rel in (1, 2, 3):
        wait(mine_ref, s_send.at[rel])
        wait(z_out, h_send.at[rel])
    for j in range(4):
        wait(mine_ref, c_send.at[j])

    @pl.when(mp != group)
    def _():
        wait(z_out, z_send)

    @pl.when(gives)
    def _():
        for k in range(7):
            wait(z_out, q_send.at[k])

    for copy in copies:
        copy.wait()


def settle(d0, d1, d2, xs, w, extra, mine):
    return pl.pallas_call(
        settle_kernel,
        out_shape=[sds((ROWS, WIDTH), BF16)] + [sds((rows, WIDTH), BF16) for rows in (192, 192, 192, 768, 768, 192, 128)]
        + [sds((3, 16, WIDTH), BF16), sds((16, WIDTH), BF16)],
        in_specs=[VM, VM, VM, ANY, VM, ANY, VM],
        out_specs=[VM] + [ANY] * 9,
        scratch_shapes=[VMEM((4 * ROWS, WIDTH), BF16), VMEM((ROWS, WIDTH), F32), VMEM((WIDTH, WIDTH), BF16), DMA((2,)),
                        VMEM((WIDTH, WIDTH), BF16), VMEM((8, SHARE_ALL, WIDTH), BF16)] + [VMEM((4 * ROWS, WIDTH), BF16)] * 3 + [
            VMEM((WIDTH, WIDTH), F32), VMEM((WIDTH, WIDTH), BF16), VMEM((4, QUARTER, WIDTH), BF16), VMEM((2, QUARTER, WIDTH), BF16),
            VMEM((QUARTER, WIDTH), BF16),
            DMA((4, SUBS)), DMA((4, SUBS)), DMA((4, SUBS)), DMA((3, SUBS)), DMA((SUBS,)),
            DMA((4,)), DMA((4,)), DMA((4,)), DMA((4,)), DMA((4,)), DMA((4,)), DMA((2,)), DMA, DMA((4,)), DMA((7,)), DMA((52,)),
        ],
        compiler_params=pltpu.CompilerParams(collective_id=3, has_side_effects=True, vmem_limit_bytes=60 << 20),
        name="settle",
    )(d0, d1, d2, xs, w, extra, mine)


EPS = 1e-12
CHUNK = 512
FF_MODEL = 768


def gelu_and_slope(v):
    size = jnp.abs(v)
    u = 1.0 / (1.0 + (0.3275911 * 0.7071067811865476) * size)
    bell = jnp.exp2(v * v * -0.7213475204444817 - 1.3257480647361595)
    poly = u * (0.3193815306 + u * (-0.3565637784 + u * (1.7814779345 + u * (-1.8212559786 + u * 1.3302744294))))
    tail = poly * bell
    cdf = jnp.where(v < 0, tail, 1.0 - tail)
    return v * cdf, cdf + v * bell


def row_mean(v):
    return jnp.sum(v, axis=-1, keepdims=True) * (1.0 / FF_MODEL)


def ffn_kernel(c01_ref, c2_ref, tok_in, cot_in, vec_ref, near_ref, a_ref, b_ref,
               out_o, res_o, g01_o, g2_o, keep_ref, next_ref, give_ref, keep_tail_ref, give_tail_ref,
               tok_ref, cot_ref, out_ref, res_ref, g01_ref, g2_ref, in_sem, early_sem, w, wout, ctx, x, gf, act, slope, zhat, acc, rstd, cols, recv, recv2, tail, tail_in,
               o_local, o_send, o_recv, f_send, f_recv, w_local, w_send, w_recv, d_send, d_recv,
               g_send, g_recv, m_send, m_recv, t_send, t_recv, out_sem, tail_sem):
    dp, mp, core, t = place()
    step = 1 - 2 * core
    partner = at(dp + step, mp)
    spot = lax.rem(dp, 8) // 2
    one, two = jnp.where(core == 0, 1, 2), jnp.where(core == 0, 2, 1)
    mate_a, mate_b = at(dp + 2 * ((spot ^ one) - spot), mp), at(dp + 2 * ((spot ^ two) - spot), mp)
    shard = lambda k: lax.rem(mp - k + 4, 4)
    later = [pltpu.make_async_copy(src, dst, in_sem.at[n]) for n, (src, dst) in enumerate(((tok_in, tok_ref), (cot_in, cot_ref)))]
    for copy in later:
        copy.start()
    results = [pltpu.make_async_copy(src, dst, early_sem.at[n])
               for n, (src, dst) in enumerate(((out_ref, out_o), (res_ref, res_o), (g01_ref, g01_o), (g2_ref, g2_o)))]
    barrier = pltpu.get_barrier_semaphore()
    for device in (partner, mate_a, mate_b):
        signal(barrier, device)
    pl.semaphore_wait(barrier, 3)

    def out_rows(m, i):
        first = jnp.where(i < 4, m * C + 32 * i, 4 * C + m * HD + 32 * (i - 4))
        return wout.at[pl.ds(pl.multiple_of(first, 32), 32)]

    sources = ((0, near_ref), (one, a_ref), (two, b_ref))
    far = spot ^ 3
    for k in range(4):
        @pl.when(spot ^ one < 3)
        def _():
            send(a_ref.at[k, pl.ds(SHARE, 32)], out_rows(shard(k), 2 * (spot ^ one) + core), f_send.at[k], f_recv.at[k], mate_b)
    for rel, ref in sources:
        j = spot ^ rel
        for k in range(4):
            src = ref.at[k, pl.ds(SHARE, 32)]

            @pl.when(j < 3)
            def _():
                pltpu.make_async_copy(src, out_rows(shard(k), 2 * j + core), o_local.at[j, k]).start()
                send(src, out_rows(shard(k), 2 * j + core), o_send.at[j, k], o_recv.at[j, k], partner)

    body = pl.ds(0, SHARE)
    for k in range(4):
        send(a_ref.at[k, body], w.at[2 * (spot ^ one) + core, shard(k)], d_send.at[k], d_recv.at[k], mate_b)
    for rel, ref in sources:
        for k in range(4):
            mine = w.at[2 * (spot ^ rel) + core, shard(k)]
            pltpu.make_async_copy(ref.at[k, body], mine, w_local.at[rel, k]).start()
            send(ref.at[k, body], mine, w_send.at[rel, k], w_recv.at[rel, k], partner)

    lane = lax.broadcasted_iota(jnp.int32, (1, C), 1)
    for g in range(4):
        ctx[:, pl.ds(g * C, C)] = c01_ref[g]
    for g in (0, 2):
        a, b = c2_ref[g].astype(F32), c2_ref[g + 1].astype(F32)
        col = pl.ds(4 * C + g * HD, C)
        ctx[pl.ds(0, 512), col] = jnp.where(lane < HD, a, pltpu.roll(b, HD, 1)).astype(BF16)
        ctx[pl.ds(512, 512), col] = jnp.where(lane < HD, pltpu.roll(a, HD, 1), b).astype(BF16)
    cols[...] = jnp.zeros_like(cols)
    b_out, gain1, bias1, b_down, gain2, bias2 = (vec_ref[pl.ds(i, 1), :] for i in range(6))
    row_chunks = [pl.ds(r * CHUNK, CHUNK) for r in range(1024 // CHUNK)]

    part = wout.at[pl.ds(0, 32)]
    for k in range(4):
        @pl.when(far < 3)
        def _():
            mine = out_rows(shard(k), 2 * far + core)
            wait(mine, f_recv.at[k])
            send(mine, mine, o_send.at[far, k], o_recv.at[far, k], partner)
    for j in range(3):
        for k in range(4):
            @pl.when(far != j)
            def _():
                wait(part, o_local.at[j, k])

            wait(part, o_recv.at[j, k])

    later[0].wait()
    for rows in row_chunks:
        h = jnp.dot(ctx[rows, :], wout[...], preferred_element_type=F32) + tok_ref[rows, :].astype(F32) + b_out
        h = h - row_mean(h)
        scale = lax.rsqrt(row_mean(h * h) + EPS)
        rstd[rows, :] = scale
        h = h * scale
        zhat[rows, :] = h
        first = h * gain1 + bias1
        acc[rows, :] = first + b_down
        x[rows, :] = first.astype(BF16)

    whole = w.at[0, 0]
    up_pair = lambda j: w[pl.ds(2 * j, 2), :, pl.ds(0, 96), :].reshape(768, FF_MODEL)
    down_pair = lambda j: w[pl.ds(2 * j, 2), :, pl.ds(96, 96), :].reshape(768, FF_MODEL)

    def up(j, rel, rows):
        bias = [jnp.sum(w[2 * j + f, :, pl.ds(192, 16), :].astype(F32), axis=0)[0:1, :384] for f in range(2)]
        pre = dot(x[rows, :], up_pair(j), 1, 1) + jnp.concatenate(bias, axis=1)
        value, grad = gelu_and_slope(pre)
        act[rel, rows, :] = value.astype(BF16)
        slope[rel, rows, :] = grad.astype(BF16)

    def down(j, rel, rows):
        acc[rows, :] += jnp.dot(act[rel, rows, :], down_pair(j), preferred_element_type=F32)

    for rel in range(4):
        j = spot ^ rel
        if rel == 2:
            for k in range(4):
                mine = w.at[2 * (spot ^ 3) + core, shard(k)]
                wait(mine, d_recv.at[k])
                send(mine, mine, w_send.at[3, k], w_recv.at[3, k], partner)
        for k in range(4):
            if rel < 3:
                wait(whole, w_local.at[rel, k])
            wait(whole, w_recv.at[rel, k])
        before = None
        for rows in row_chunks:
            up(j, rel, rows)
            if before is not None:
                down(j, rel, before)
            before = rows
        down(j, rel, before)

    later[1].wait()
    for rows in row_chunks:
        z = acc[rows, :]
        z = z - row_mean(z)
        scale = lax.rsqrt(row_mean(z * z) + EPS)
        z = z * scale
        out_ref[rows, :] = (z * gain2 + bias2).astype(BF16)
        cot = cot_ref[rows, :].astype(F32)
        dz = cot * gain2
        gs = scale * (dz - row_mean(dz) - z * row_mean(dz * z))
        cols[pl.ds(2, 1), :] += jnp.sum(cot * z, axis=0, keepdims=True)
        cols[pl.ds(3, 1), :] += jnp.sum(cot, axis=0, keepdims=True)
        cols[pl.ds(5, 1), :] += jnp.sum(gs, axis=0, keepdims=True)
        acc[rows, :] = gs
        gf[rows, :] = gs.astype(BF16)

    results[0].start()

    for rel in range(4):
        for k in range(4):
            wait(whole, w_send.at[rel, k])
    for k in range(4):
        wait(whole, d_send.at[k])

    grads = pl.ds(0, 192)
    order = (3, 1, 2, 0)
    place_of = {rel: q for q, rel in enumerate(order)}

    def add_cores(rel):
        q, i = place_of[rel], 2 * (spot ^ rel) + core
        wait(recv.at[q], g_recv.at[q])
        for m in range(4):
            recv[q, m] = (recv[q, m].astype(F32) + w[i, m, grads, :].astype(F32)).astype(BF16)
        if rel == 3:
            send(recv.at[q], recv2, m_send, m_recv, mate_a)
        elif rel == 0:
            pltpu.make_async_copy(recv.at[q], keep_ref, out_sem.at[0]).start()
        else:
            @pl.when(one == rel)
            def _():
                pltpu.make_async_copy(recv.at[q], next_ref, out_sem.at[1]).start()

    for q, rel in enumerate(order):
        j = spot ^ rel
        for rows in row_chunks:
            ga = dot(gf[rows, :], down_pair(j), 1, 1)
            slope[rel, rows, :] = (ga * slope[rel, rows, :].astype(F32)).astype(BF16)
            acc[rows, :] += jnp.dot(slope[rel, rows, :], up_pair(j), preferred_element_type=F32)
        for f in range(2):
            cut = pl.ds(f * 384, 384)
            gp = slope[rel, :, cut]
            w[2 * j + f, :, pl.ds(0, 96), :] = dot(gp, x[...], 0, 0).astype(BF16).reshape(4, 96, FF_MODEL)
            w[2 * j + f, :, pl.ds(96, 96), :] = dot(act[rel, :, cut], gf[...], 0, 0).astype(BF16).reshape(4, 96, FF_MODEL)
            cols[pl.ds(8 + 2 * j + f, 1), pl.ds(0, 384)] = jnp.sum(gp.astype(F32), axis=0, keepdims=True)
        send(w.at[2 * j + 1 - core, :, grads], recv.at[q], g_send.at[q], g_recv.at[q], partner)
        if q:
            add_cores(order[q - 1])

    ctx_grad = x.at[:, pl.ds(0, 2 * C)]
    for rows in row_chunks:
        grad = acc[rows, :]
        z = zhat[rows, :]
        dz = grad * gain1
        gr = rstd[rows, :] * (dz - row_mean(dz) - z * row_mean(dz * z))
        cols[pl.ds(0, 1), :] += jnp.sum(grad * z, axis=0, keepdims=True)
        cols[pl.ds(1, 1), :] += jnp.sum(grad, axis=0, keepdims=True)
        cols[pl.ds(4, 1), :] += jnp.sum(gr, axis=0, keepdims=True)
        res_ref[rows, :] = gr
        low = gr.astype(BF16)
        gf[rows, :] = low
        gc = dot(low, wout[...], 1, 1).astype(BF16)
        for g in range(4):
            g01_ref[g, rows, :] = gc[:, g * C : g * C + C]
        ctx_grad[rows, :] = gc[:, 4 * C :]
    for g in (0, 2):
        top = ctx_grad[pl.ds(0, 512), pl.ds(g * HD, C)].astype(F32)
        low = ctx_grad[pl.ds(512, 512), pl.ds(g * HD, C)].astype(F32)
        g2_ref[g] = jnp.where(lane < HD, top, pltpu.roll(low, HD, 1)).astype(BF16)
        g2_ref[g + 1] = jnp.where(lane < HD, pltpu.roll(top, HD, 1), low).astype(BF16)

    for copy in results[1:]:
        copy.start()

    for n in range(3):
        got = dot(ctx[:, pl.ds(n * 256, 256)], gf[...], 0, 0).astype(BF16)
        for i in range(8):
            piece = got[i * 32 : i * 32 + 32, :]
            m, share = (2 * n + i // 4, i % 4) if n < 2 else (i // 2, 4 + i % 2)
            tail[share % 2, share // 2, m, pl.ds(0, 32), :] = piece
    vectors = jnp.concatenate([cols[pl.ds(0, 6), :], jnp.zeros((26, FF_MODEL), F32)], axis=0).astype(BF16)
    for i in range(8):
        line = jnp.concatenate([cols[pl.ds(8 + i, 1), :], jnp.zeros((15, FF_MODEL), F32)], axis=0).astype(BF16)
        for m in range(4):
            tail[i % 2, i // 2, m, pl.ds(32, 16), :] = line
            if i >= 6:
                tail[i % 2, i // 2, m, pl.ds(0, 32), :] = vectors if i == 6 else jnp.zeros((32, FF_MODEL), BF16)
    send(tail.at[1 - core], tail_in, t_send, t_recv, partner)
    add_cores(0)

    wait(recv2, m_recv)
    for rel in (1, 2):
        @pl.when(two == rel)
        def _():
            for m in range(4):
                recv2[m] = (recv2[m].astype(F32) + recv[place_of[rel], m].astype(F32)).astype(BF16)
    give = pltpu.make_async_copy(recv2, give_ref, out_sem.at[2])
    give.start()
    wait(tail_in, t_recv)
    for rel in range(4):
        j = spot ^ rel
        for m in range(4):
            tail_in[j, m] = (tail_in[j, m].astype(F32) + tail[core, j, m].astype(F32)).astype(BF16)
        along, across = jnp.where(core == 0, rel % 2, rel // 2), jnp.where(core == 0, rel // 2, rel % 2)
        for side, ref in enumerate((keep_tail_ref, give_tail_ref)):
            @pl.when(along == side)
            def _():
                pltpu.make_async_copy(tail_in.at[j], ref.at[across], tail_sem.at[rel]).start()
    give.wait()
    for copy in results:
        copy.wait()
    wait(recv2, out_sem.at[0])
    wait(recv2, out_sem.at[1])
    for rel in range(4):
        wait(tail_in.at[0], tail_sem.at[rel])
    for q in range(4):
        wait(recv.at[q], g_send.at[q])
    wait(recv2, m_send)
    wait(tail_in, t_send)
    for k in range(4):
        @pl.when(spot ^ one < 3)
        def _():
            wait(part, f_send.at[k])

        for j in range(3):
            wait(part, o_send.at[j, k])


def ffn(c01, c2, tokens, cot, vecs, near, a, b):
    main, rest = sds((4, 192, WIDTH), BF16), sds((2, 4, 48, WIDTH), BF16)
    rows = lambda dtype: VMEM((1024, WIDTH), dtype)
    four = lambda *shape: VMEM((4,) + shape, BF16)
    return pl.pallas_call(
        ffn_kernel,
        out_shape=[sds((1024, WIDTH), BF16), sds((1024, WIDTH), F32), sds((4, 1024, C), BF16), sds((4, 512, C), BF16), main, main, main, rest, rest],
        in_specs=[VM, VM, ANY, ANY, VM] + [ANY] * 3,
        out_specs=[ANY] * 9,
        scratch_shapes=[
            rows(BF16), rows(BF16), rows(BF16), rows(F32), four(1024, C), four(512, C), DMA((2,)), DMA((4,)),
            VMEM((8, 4, SHARE, WIDTH), BF16), VMEM((WIDTH, WIDTH), BF16), rows(BF16), rows(BF16), rows(BF16), four(1024, WIDTH), four(1024, WIDTH),
            rows(F32), rows(F32), VMEM((1024, 1), F32), VMEM((16, WIDTH), F32), four(4, 192, WIDTH), four(192, WIDTH),
            VMEM((2, 4, 4, 48, WIDTH), BF16), four(4, 48, WIDTH),
        ] + [DMA((4, 4))] * 3 + [DMA((4,))] * 2 + [DMA((4, 4))] * 3 + [DMA((4,))] * 4 + [DMA] * 4 + [DMA((3,)), DMA((4,))],
        compiler_params=pltpu.CompilerParams(collective_id=4, has_side_effects=True, vmem_limit_bytes=63 << 20),
        name="ffn",
    )(c01, c2, tokens, cot, vecs, near, a, b)


def swap(value, even_bits, odd_bits, n_dp):
    return lax.ppermute(value, "dp", [(d, d ^ (odd_bits if d % 2 else even_bits)) for d in range(n_dp)])


def pick(value, index, axis):
    return lax.dynamic_index_in_dim(value, index, axis, keepdims=False)


def total(a, b):
    return (a.astype(F32) + b.astype(F32)).astype(BF16)


def tie(*values):
    return lax.optimization_barrier(values)


def body(n_dp, tokens, w_query, b_query, w_key, w_value, b_value, w_out, b_out, norm1_gain, norm1_bias, w_up, b_up, w_down,
         b_down, norm2_gain, norm2_bias, key_mask, cluster_order, cotangent):
    dp, mp, core, t = place()
    ring = lambda k: [(z, (z + k) % 4) for z in range(4)]

    order = 2 * jnp.where(core == 1, cluster_order ^ 3072, cluster_order).reshape(3 * L)
    bq, bv, bz = b_query.reshape(3, HD), b_value.reshape(3, HD), jnp.zeros((C,), F32)
    b_heads = jnp.stack([jnp.concatenate([bq[h], bv[h], bz] if h == 1 else [bv[h], bq[h], bz]) for h in range(3)])
    b_heads = jnp.concatenate([b_heads, jnp.zeros((5, 256), F32)])
    units = lax.dynamic_slice(b_up, (96 * (dp % 8),), (96,)).reshape(1, 96)
    bias_row = lax.dynamic_update_slice(jnp.zeros((16, WIDTH), BF16), units, (0, 96 * mp))

    xs, qkv, w_heads, order, mask, share = collect(
        tokens, w_query.T, w_key.T, w_value.T, b_heads, order, key_mask, w_up, w_down, w_out, bias_row
    )
    qkv, share = tie(qkv, share)
    shares = [share] + [lax.ppermute(share, "mp", ring(i)) for i in (1, 2, 3)]
    c01, ts01, probs01 = attend(0, order, mask, qkv)
    c01, qkv = tie(c01, qkv)
    c2, ts2, probs2 = attend(2, order, mask, qkv)
    c2, *shares = tie(c2, *shares)
    near = jnp.stack(shares)
    along, across = swap(near, 2, 4, n_dp), swap(near, 4, 2, n_dp)
    c01, c2 = spread(c01, c2)

    vecs = jnp.stack([b_out, norm1_gain, norm1_bias, b_down, norm2_gain, norm2_bias, b_out, b_out])
    layer_out, grad_residual, g01, g2, keep, nearer, give, keep_tail, give_tail = ffn(
        c01, c2, tokens, cotangent, vecs, near, along, across
    )

    got, got_nearer, got_tail = swap(give, 4, 2, n_dp), swap(nearer, 2, 4, n_dp), swap(give_tail, 2, 4, n_dp)
    g01, g2 = regroup(g01, g2)
    g01, keep, got, got_nearer, keep_tail, got_tail = tie(g01, keep, got, got_nearer, keep_tail, got_tail)
    groups = [1 << bit for bit in range(3, n_dp.bit_length() - 1)]

    def shard_sums(sums):
        for bits in groups:
            sums = total(sums, swap(sums, bits, bits, n_dp))
        return [pick(sums, mp, 0)] + [lax.ppermute(pick(sums, (mp + k) % 4, 0), "mp", ring(k)) for k in (1, 2, 3)]

    keep = (keep.astype(F32) + got_nearer.astype(F32) + got.astype(F32)).astype(BF16)
    keep_tail, give_tail = total(keep_tail[0], got_tail[0]), total(keep_tail[1], got_tail[1])
    got_tail = swap(give_tail, 4, 2, n_dp)
    d0 = attend_back(0, order, g01, ts01, probs01)
    d0, order, keep, keep_tail, got_tail = tie(d0, order, keep, keep_tail, got_tail)
    parts = shard_sums(jnp.concatenate([keep, total(keep_tail, got_tail)], axis=1))
    d1 = attend_back(1, order, g01, ts01, probs01)
    d2 = attend_back(2, order, g2, ts2, probs2)
    d2, *parts = tie(d2, *parts)
    mine = sum(p.astype(F32) for p in parts).astype(BF16)
    grad_tokens, *sums = settle(d0, d1, d2, xs, w_heads, grad_residual, mine)
    hq, hk, hv, g_up, g_down, g_out, units, spare, vectors = (s.astype(F32) for s in sums)
    for bits in groups:
        hq, hk, hv, spare = (s + swap(s, bits, bits, n_dp) for s in (hq, hk, hv, spare))
    sums_of = lambda where: jnp.concatenate([spare[h, 0, where[h] : where[h] + HD] for h in range(3)])
    g_b_up = lax.dynamic_slice(units.reshape(8, 16, WIDTH)[:, 0], (0, 96 * mp), (8, 96)).reshape(WIDTH)
    return (
        layer_out,
        grad_tokens,
        hq.T,
        sums_of((HD, 0, HD)),
        hk.T,
        hv.T,
        sums_of((0, HD, 0)),
        g_out,
        vectors[4],
        vectors[0],
        vectors[1],
        g_up,
        g_b_up,
        g_down,
        vectors[5],
        vectors[2],
        vectors[3],
    )


def solution(mesh):
    return jax.shard_map(
        functools.partial(body, mesh.shape["dp"]),
        mesh=mesh,
        in_specs=(
            P(("dp", "mp"), None), P(None, "mp"), P("mp"), P(None, "mp"), P(None, "mp"), P("mp"), P("mp", None), P(), P(), P(),
            P(None, "mp"), P("mp"), P("mp", None), P(), P(), P(), P("dp", None), P("dp", "mp", None), P(("dp", "mp"), None),
        ),
        out_specs=(
            P(("dp", "mp"), None), P(("dp", "mp"), None), P(None, "mp"), P("mp"), P(None, "mp"), P(None, "mp"), P("mp"),
            P("mp", None), P(), P(), P(), P(None, "mp"), P("mp"), P("mp", None), P(), P(), P(),
        ),
        check_vma=False,
    )
```

```python
import functools
import jax
import jax.numpy as jnp
from jax import lax
from jax.experimental import pallas as pl
from jax.experimental.pallas import tpu as pltpu
from jax.sharding import PartitionSpec as P

L = 4096
C = 128
HD = 64
GROUP = 4
STEP = 1024
GROUPS = STEP // (GROUP * C)
HALVES = 2
F32 = jnp.float32
BF16 = jnp.bfloat16
VMEM = pltpu.VMEM


def dot(a, b, da, db):
    return lax.dot_general(a, b, (((da,), (db,)), ((), ())), preferred_element_type=F32)


def in_turn(gather, compute, scatter, bufs, outs):
    gather(0, bufs[0])
    for group in range(GROUPS):
        if group + 1 < GROUPS:
            gather(group + 1, bufs[(group + 1) % 2])
        compute(group, bufs[group % 2], outs[group % 2])
        if group:
            scatter(group - 1, outs[(group - 1) % 2])
    scatter(GROUPS - 1, outs[(GROUPS - 1) % 2])


def each_window(ord_ref, windows, sems, first, step, steps, work):
    def fetch(n, at_step):
        start = pl.multiple_of((first + at_step * HALVES + n) * STEP, STEP)
        return pltpu.make_async_copy(ord_ref.at[pl.ds(start, STEP)], windows[n], sems.at[n])

    @pl.when(step == 0)
    def _():
        for n in range(HALVES):
            fetch(n, step).start()

    for n in range(HALVES):
        fetch(n, step).wait()
        work(n, windows[n])

        @pl.when(step + 1 < steps)
        def _():
            fetch(n, step + 1).start()


def attend_kernel(first, ord_ref, mask_ref, qkv_ref, c_ref, ts_ref, pr_ref, src, ctx, *rest):
    slots, windows, sems = rest[:4], rest[4 : 4 + HALVES], rest[4 + HALVES]
    head, step = pl.program_id(0) + first, pl.program_id(1)
    live = jnp.sum(mask_ref[...].astype(F32), axis=1, keepdims=True).astype(jnp.int32)

    @pl.when(step == 0)
    def _():
        src[pl.ds(0, L, stride=2), :] = qkv_ref[0, :, :C].astype(F32)
        src[pl.ds(1, L, stride=2), :] = qkv_ref[0, :, C:].astype(F32)

    def work(n, window):
        def gather(group, buf):
            for u in range(GROUP * C):
                buf[pl.ds(2 * u, 2), :] = src[pl.ds(pl.multiple_of(window[group * GROUP * C + u], 2), 2), :]

        def compute(group, buf, out):
            each = range(GROUP)
            rows = [pl.ds(n * STEP + (group * GROUP + i) * C, C) for i in each]
            t0 = [buf[pl.ds(2 * i * C, C, stride=2), :].astype(BF16) for i in each]
            t1 = [buf[pl.ds(2 * i * C + 1, C, stride=2), :].astype(BF16) for i in each]
            for i in each:
                ts_ref[0, rows[i], :C] = t0[i]
                ts_ref[0, rows[i], C:] = t1[i]
            slot = [(step * HALVES + n) * STEP + (group * GROUP + i) * C + lax.broadcasted_iota(jnp.int32, (C, C), 0) for i in each]
            scores = [dot(t1[i], t0[i], 1, 1) * 0.125 + jnp.where(slot[i] < live, 0.0, -10000.0) for i in each]
            e = [jnp.exp(scores[i] - jnp.max(scores[i], axis=0, keepdims=True)) for i in each]
            probs = [e[i] * (1.0 / jnp.sum(e[i], axis=0, keepdims=True)) for i in each]
            for i in each:
                pr_ref[0, rows[i], :] = probs[i]
            for i in each:
                out[pl.ds(i * C, C), :] = dot(probs[i].astype(BF16), t0[i], 0, 0)

        def scatter(group, out):
            for u in range(GROUP * C):
                ctx[pl.ds(window[group * GROUP * C + u], 1), :] = out[pl.ds(u, 1), :]

        in_turn(gather, compute, scatter, slots[:2], slots[2:])

    each_window(ord_ref, windows, sems, head * (L // STEP), step, L // STEP // HALVES, work)

    @pl.when(step == L // STEP // HALVES - 1)
    def _():
        lane = lax.broadcasted_iota(jnp.int32, (1, C), 1)
        if first == 2:
            for k in range(4):
                low = ctx[pl.ds(k * 2048, 512, stride=2), :]
                high = pltpu.roll(ctx[pl.ds(k * 2048 + 1024, 512, stride=2), :], HD, 1)
                c_ref[pl.ds(k * 512, 512), :] = jnp.where(lane < HD, low, high).astype(BF16)
        else:
            rows = ctx[pl.ds(0, L, stride=2), :].astype(BF16)

            @pl.when(head == 0)
            def _():
                c_ref[...] = rows

            @pl.when(head == 1)
            def _():
                c_ref[...] = jnp.where(lane < HD, c_ref[...], rows)


def attend(first, order, mask, qkv):
    heads = 2 if first == 0 else 1
    whole = lambda shape: pl.BlockSpec(shape, lambda h, i: (0,) * len(shape), pipeline_mode=pl.Buffered(1))
    per_step = lambda width: pl.BlockSpec((1, HALVES * STEP, width), lambda h, i: (h, i, 0))
    out_rows = L if first == 0 else L // 2
    return pl.pallas_call(
        functools.partial(attend_kernel, first),
        grid=(heads, L // STEP // HALVES),
        in_specs=[
            pl.BlockSpec(memory_space=pl.ANY),
            whole((1, L)),
            pl.BlockSpec((1, L, 2 * C), lambda h, i: (h + first, 0, 0)),
        ],
        out_specs=[whole((out_rows, C)), per_step(2 * C), per_step(C)],
        out_shape=[
            jax.ShapeDtypeStruct((out_rows, C), BF16),
            jax.ShapeDtypeStruct((heads, L, 2 * C), BF16),
            jax.ShapeDtypeStruct((heads, L, C), F32),
        ],
        scratch_shapes=[VMEM((2 * L, C), F32), VMEM((2 * L, C), F32)]
        + [VMEM((2 * GROUP * C, C), F32)] * 2 + [VMEM((GROUP * C, C), F32)] * 2
        + [pltpu.SMEM((STEP,), jnp.int32)] * HALVES + [pltpu.SemaphoreType.DMA((HALVES,))],
        compiler_params=pltpu.CompilerParams(vmem_limit_bytes=60 << 20),
        cost_estimate=pl.CostEstimate(flops=heads * 9 * 10**9, bytes_accessed=10 << 20, transcendentals=0),
        name="attend",
    )(order, mask, qkv)


def attend_back_kernel(head, ord_ref, g_ref, ts_ref, pr_ref, d_ref, gsrc, dst, *rest):
    slots, windows, sems = rest[:4], rest[4 : 4 + HALVES], rest[4 + HALVES]
    step = pl.program_id(0)
    lane = lax.broadcasted_iota(jnp.int32, (1, C), 1)

    @pl.when(step == 0)
    def _():
        if head == 2:
            for k in range(4):
                both = g_ref[pl.ds(k * 512, 512), :].astype(F32)
                gsrc[pl.ds(k * 2048, 512, stride=2), :] = both
                gsrc[pl.ds(k * 2048 + 1024, 512, stride=2), :] = pltpu.roll(both, HD, 1)
        else:
            gsrc[pl.ds(0, L, stride=2), :] = g_ref[...].astype(F32)

    keep = (lane >= HD) if head == 1 else (lane < HD)

    def work(n, window):
        def gather(group, buf):
            for u in range(GROUP * C):
                buf[pl.ds(u, 1), :] = gsrc[pl.ds(window[group * GROUP * C + u], 1), :]

        def compute(group, buf, out):
            each = range(GROUP)
            rows = [pl.ds(n * STEP + (group * GROUP + i) * C, C) for i in each]
            t0 = [ts_ref[0, rows[i], :C] for i in each]
            t1 = [ts_ref[0, rows[i], C:] for i in each]
            probs = [pr_ref[0, rows[i], :] for i in each]
            g = [jnp.where(keep, buf[pl.ds(i * C, C), :], 0.0).astype(BF16) for i in each]
            dp = [dot(t0[i], g[i], 1, 1) for i in each]
            ds = [(probs[i] * (dp[i] - jnp.sum(probs[i] * dp[i], axis=0, keepdims=True))).astype(BF16) for i in each]
            for i in each:
                grad = dot(ds[i], t1[i], 0, 0) * 0.125 + jnp.dot(probs[i].astype(BF16), g[i], preferred_element_type=F32)
                out[pl.ds(2 * i * C, C, stride=2), :] = grad
            for i in each:
                out[pl.ds(2 * i * C + 1, C, stride=2), :] = jnp.dot(ds[i], t0[i], preferred_element_type=F32) * 0.125

        def scatter(group, out):
            for u in range(GROUP * C):
                dst[pl.ds(pl.multiple_of(window[group * GROUP * C + u], 2), 2), :] = out[pl.ds(2 * u, 2), :]

        in_turn(gather, compute, scatter, slots[:2], slots[2:])

    each_window(ord_ref, windows, sems, head * (L // STEP), step, L // STEP // HALVES, work)

    @pl.when(step == L // STEP // HALVES - 1)
    def _():
        d_ref[:, :C] = dst[pl.ds(0, L, stride=2), :].astype(BF16)
        d_ref[:, C:] = dst[pl.ds(1, L, stride=2), :].astype(BF16)


def attend_back(head, order, g, ts, probs):
    whole = lambda shape: pl.BlockSpec(shape, lambda i: (0,) * len(shape), pipeline_mode=pl.Buffered(1))
    per_step = lambda width: pl.BlockSpec((1, HALVES * STEP, width), lambda i: (head % 2, i, 0))
    return pl.pallas_call(
        functools.partial(attend_back_kernel, head),
        grid=(L // STEP // HALVES,),
        in_specs=[
            pl.BlockSpec(memory_space=pl.ANY),
            whole(g.shape), per_step(2 * C), per_step(C),
        ],
        out_specs=whole((L, 2 * C)),
        out_shape=jax.ShapeDtypeStruct((L, 2 * C), BF16),
        scratch_shapes=[VMEM((2 * L, C), F32), VMEM((2 * L, C), F32)]
        + [VMEM((GROUP * C, C), F32)] * 2 + [VMEM((2 * GROUP * C, C), F32)] * 2
        + [pltpu.SMEM((STEP,), jnp.int32)] * HALVES + [pltpu.SemaphoreType.DMA((HALVES,))],
        compiler_params=pltpu.CompilerParams(vmem_limit_bytes=60 << 20),
        cost_estimate=pl.CostEstimate(flops=9 * 10**9, bytes_accessed=10 << 20, transcendentals=0),
        name="attend_back",
    )(order, g, ts, probs)


MESH = pl.DeviceIdType.MESH
WIDTH = 768
ROWS = 1024
SUB = 512
SUBS = ROWS // SUB
SHARE = 208
SHARE_ALL = SHARE + 32
QUARTER = 192
DMA = pltpu.SemaphoreType.DMA
ANY = pl.BlockSpec(memory_space=pl.ANY)
VM = pl.BlockSpec(memory_space=pltpu.VMEM)
sds = jax.ShapeDtypeStruct


def place():
    dp, mp = lax.axis_index("dp"), lax.axis_index("mp")
    core = lax.rem(dp, 2)
    return dp, mp, core, jnp.where(core == 0, mp, 3 - mp)


def at(dp, mp):
    return {"dp": dp, "mp": mp}


def signal(barrier, device):
    pl.semaphore_signal(barrier, inc=1, device_id=device, device_id_type=MESH)


def send(src, dst, send_sem, recv_sem, device):
    copy = pltpu.make_async_remote_copy(
        src_ref=src, dst_ref=dst, send_sem=send_sem, recv_sem=recv_sem, device_id=device, device_id_type=MESH
    )
    copy.start()
    return copy


def wait(ref, sem):
    pltpu.make_async_copy(ref, ref, sem).wait()


def mate(dp, rel):
    return dp + 2 * ((lax.rem(dp, 8) // 2 ^ rel) - lax.rem(dp, 8) // 2)


def greet(barrier, both_cores):
    dp, mp, core, t = place()
    step = 1 - 2 * core
    for k in range(4):
        if k:
            signal(barrier, at(dp, lax.rem(mp + k, 4)))
        signal(barrier, at(dp + step, lax.rem(mp + k, 4)))
    for rel in (1, 2, 3):
        signal(barrier, at(mate(dp, rel), mp))
        if both_cores:
            signal(barrier, at(mate(dp, rel) + step, mp))
    pl.semaphore_wait(barrier, 13 if both_cores else 10)


def worker(group, half, dp_base):
    return at(dp_base + group % 2, 2 * half + group // 2)


def chain_device(u, half, dp_base):
    return at(dp_base + half, jnp.where(half == 0, u, 3 - u))


def collect_kernel(x_ref, wq_ref, wk_ref, wv_ref, bsrc_ref, osrc_ref, msrc_ref, up_ref, down_ref, wout_ref, brow_ref,
                   xs_ref, qkv_ref, w_ref, ord_ref, mask_ref, share_ref,
                   xs, qkv, w, wsrc, bias, relay, up, up_t,
                   chain_recv, relay_recv, pair_recv, chain_send, relay_send, pair_send, own_sem,
                   wz_recv, wz_send, wp_recv, wp_send, b_recv, b_send, o_recv, o_send, m_recv, m_send, xs_out, qkv_out, w_out, build_sem, up_sem, share_sem):
    dp, mp, core, t = place()
    base, half, spot = dp - core, mp // 2, lax.rem(dp, 8) // 2
    step = 1 - 2 * core
    partner, lower, upper = at(dp + step, mp), at(dp, mp - step), at(dp, mp + step)
    group = lax.rem(mp, 2) * 2 + core
    gives = core == lax.rem(mp, 2)
    order_self = worker(mp, core, base)
    order_here = (order_self["dp"] == dp) & (order_self["mp"] == mp)
    cut = lambda s: pl.ds(s * SUB, SUB)
    home = lambda u, s: xs.at[pl.ds(pl.multiple_of(u * ROWS + s * SUB, SUB), SUB)]
    quarter = lambda q: pl.ds(pl.multiple_of(q * QUARTER, QUARTER), QUARTER)

    own = pltpu.make_async_copy(x_ref, xs.at[pl.ds(pl.multiple_of(jnp.minimum(t, 1) * ROWS, ROWS), ROWS)], own_sem)

    @pl.when(t <= 1)
    def _():
        own.start()

    parts = []
    for h in range(3):
        for n, part in enumerate((wq_ref, wv_ref, wk_ref, None) if h == 1 else (wv_ref, wq_ref, None, wk_ref)):
            rows = pl.ds((4 * h + n) * HD, HD)
            if part is None:
                wsrc[rows, :] = jnp.zeros((HD, WIDTH), BF16)
            else:
                copy = pltpu.make_async_copy(part.at[pl.ds(h * HD, HD)], wsrc.at[rows], build_sem.at[4 * h + n])
                copy.start()
                parts.append(copy)
    greet(pltpu.get_barrier_semaphore(), False)
    for copy in parts:
        copy.wait()

    for far in (0, 1):
        target = mp // 2 + 2 * far

        @pl.when(gives & (target != mp))
        def _():
            send(wsrc.at[quarter(spot)], w.at[quarter(spot)], wz_send.at[far], wz_recv, at(dp, target))
            send(bsrc_ref, bias, b_send.at[far], b_recv, at(dp, target))

        @pl.when(gives & (target == mp))
        def _():
            pltpu.make_async_copy(wsrc.at[quarter(spot)], w.at[quarter(spot)], wz_recv).start()
            pltpu.make_async_copy(bsrc_ref, bias, b_recv).start()

    @pl.when(order_here)
    def _():
        pltpu.make_async_copy(osrc_ref, ord_ref, o_recv).start()
        pltpu.make_async_copy(msrc_ref, mask_ref, m_recv).start()

    @pl.when(jnp.logical_not(order_here))
    def _():
        send(osrc_ref, ord_ref, o_send, o_recv, order_self)
        send(msrc_ref, mask_ref, m_send, m_recv, order_self)

    @pl.when(t == 3)
    def _():
        for s in range(SUBS):
            send(x_ref.at[cut(s)], relay.at[cut(s)], chain_send.at[0, s], relay_recv.at[s], lower)

    @pl.when((t == 1) | (t == 2))
    def _():
        for s in range(SUBS):
            send(x_ref.at[cut(s)], home(t, s), chain_send.at[0, s], chain_recv.at[t, s], lower)

    @pl.when(t == 0)
    def _():
        for s in range(SUBS):
            send(x_ref.at[cut(s)], home(0, s), chain_send.at[0, s], chain_recv.at[0, s], upper)

    number = lax.rem(dp, 8)
    units = pl.ds(pl.multiple_of(96 * number, 32), 96)
    out_rows = pl.ds(pl.multiple_of(32 * jnp.minimum(number, 5), 32), 32)
    load = pltpu.make_async_copy(up_ref, up, up_sem)
    load.start()
    made = [
        pltpu.make_async_copy(down_ref.at[units], share_ref.at[pl.ds(96, 96)], share_sem.at[0]),
        pltpu.make_async_copy(brow_ref, share_ref.at[pl.ds(192, 16)], share_sem.at[1]),
        pltpu.make_async_copy(wout_ref.at[out_rows], share_ref.at[pl.ds(SHARE, 32)], share_sem.at[2]),
    ]
    for copy in made:
        copy.start()

    wait(w.at[quarter(spot)], wz_recv)
    for rel in (1, 2, 3):
        send(w.at[quarter(spot)], w.at[quarter(spot)], wp_send.at[rel], wp_recv.at[rel], at(mate(dp, rel), mp))

    @pl.when(t <= 1)
    def _():
        own.wait()
        for s in range(SUBS):
            send(home(t, s), home(t, s), pair_send.at[t, s], pair_recv.at[t, s], partner)

    tt = jnp.minimum(t, 3 - t)

    def rows_of(i, s):
        return pl.ds(pl.multiple_of(lax.rem(tt + i, 4) * ROWS + s * SUB, SUB), SUB)

    def receive(i, s):
        u = lax.rem(tt + i, 4)
        if i == 1:
            @pl.when(t == 2)
            def _():
                wait(relay.at[cut(s)], relay_recv.at[s])
                send(relay.at[cut(s)], home(3, s), relay_send.at[s], chain_recv.at[3, s], lower)

        if i > 0:
            @pl.when(t <= 1)
            def _():
                wait(home(u, s), chain_recv.at[u, s])
                if i < 3:
                    @pl.when(t == 1)
                    def _():
                        send(home(u, s), home(u, s), chain_send.at[i, s], chain_recv.at[u, s], lower)
                send(home(u, s), home(u, s), pair_send.at[u, s], pair_recv.at[u, s], partner)

        @pl.when(t >= 2)
        def _():
            wait(home(u, s), pair_recv.at[u, s])

        rows = rows_of(i, s)
        pltpu.make_async_copy(xs.at[rows], xs_ref.at[rows], xs_out.at[i, s]).start()

    def project(i, s):
        rows = rows_of(i, s)
        row = jnp.concatenate([bias[pl.ds(h, 1), :] for h in range(3)], axis=1)
        qkv[rows, :] = (dot(xs[rows, :], w[...], 1, 1) + row).astype(BF16)
        for h in range(3):
            pltpu.make_async_copy(qkv.at[rows, pl.ds(h * 256, 256)], qkv_ref.at[h, rows], qkv_out.at[i, s, h]).start()

    pieces = [(i, s) for i in range(4) for s in range(SUBS)]
    for i, s in pieces[:4]:
        receive(i, s)
    for rel in (1, 2, 3):
        wait(w.at[quarter(spot ^ rel)], wp_recv.at[rel])
    wait(bias, b_recv)
    pltpu.make_async_copy(w, w_ref, w_out).start()
    for i, s in pieces[:3]:
        project(i, s)
    load.wait()
    up_t[...] = up[...].T
    made.append(pltpu.make_async_copy(up_t.at[units], share_ref.at[pl.ds(0, 96)], share_sem.at[3]))
    made[-1].start()
    for k in range(4, len(pieces)):
        receive(*pieces[k])
        project(*pieces[k - 1])
    project(*pieces[-1])

    for i in range(4):
        u = lax.rem(tt + i, 4)
        for s in range(SUBS):
            rows = pl.ds(pl.multiple_of(u * ROWS + s * SUB, SUB), SUB)
            wait(xs.at[rows], xs_out.at[i, s])
            for h in range(3):
                wait(qkv_ref.at[h, rows], qkv_out.at[i, s, h])

            @pl.when(t <= 1)
            def _():
                wait(home(u, s), pair_send.at[u, s])
    for s in range(SUBS):
        wait(x_ref.at[cut(s)], chain_send.at[0, s])

        @pl.when(t == 1)
        def _():
            wait(x_ref.at[cut(s)], chain_send.at[1, s])
            wait(x_ref.at[cut(s)], chain_send.at[2, s])

        @pl.when(t == 2)
        def _():
            wait(relay.at[cut(s)], relay_send.at[s])
    for rel in (1, 2, 3):
        wait(w.at[quarter(spot)], wp_send.at[rel])
    for far in (0, 1):
        @pl.when(gives & (mp // 2 + 2 * far != mp))
        def _():
            wait(wsrc.at[quarter(spot)], wz_send.at[far])
            wait(bsrc_ref, b_send.at[far])
    wait(ord_ref, o_recv)
    wait(mask_ref, m_recv)

    @pl.when(jnp.logical_not(order_here))
    def _():
        wait(osrc_ref, o_send)
        wait(msrc_ref, m_send)

    wait(w, w_out)
    for copy in made:
        copy.wait()


def collect(x, wq, wk, wv, b, order, mask, up, down, out, bias_row):
    return pl.pallas_call(
        collect_kernel,
        out_shape=[sds((4 * ROWS, WIDTH), BF16), sds((3, 4 * ROWS, 256), BF16), sds((WIDTH, WIDTH), BF16), sds((3 * L,), jnp.int32),
                   sds((1, L), jnp.int32), sds((SHARE_ALL, WIDTH), BF16)],
        in_specs=[ANY] * 11,
        out_specs=[ANY] * 6,
        scratch_shapes=[
            VMEM((4 * ROWS, WIDTH), BF16), VMEM((4 * ROWS, WIDTH), BF16), VMEM((WIDTH, WIDTH), BF16), VMEM((WIDTH, WIDTH), BF16),
            VMEM((8, 256), F32), VMEM((ROWS, WIDTH), BF16), VMEM((WIDTH, WIDTH), BF16), VMEM((WIDTH, WIDTH), BF16),
            DMA((4, SUBS)), DMA((SUBS,)), DMA((4, SUBS)), DMA((3, SUBS)), DMA((SUBS,)), DMA((4, SUBS)), DMA,
            DMA, DMA((2,)), DMA((4,)), DMA((4,)), DMA, DMA((2,)), DMA, DMA, DMA, DMA,
            DMA((4, SUBS)), DMA((4, SUBS, 3)), DMA, DMA((12,)), DMA, DMA((4,)),
        ],
        compiler_params=pltpu.CompilerParams(collective_id=0, has_side_effects=True, vmem_limit_bytes=60 << 20),
        name="collect",
    )(x, wq, wk, wv, b, order, mask, up, down, out, bias_row)


def greet_exchange(barrier):
    dp, mp, core, t = place()
    half, base = mp // 2, dp - core
    mine = lax.rem(mp, 2) * 2 + core
    for u in range(4):
        @pl.when((half != core) | (t != u))
        def _():
            pl.semaphore_signal(barrier, inc=1, device_id=chain_device(u, half, base), device_id_type=MESH)
    for g in range(4):
        @pl.when((half != core) | (mine != g))
        def _():
            pl.semaphore_signal(barrier, inc=1, device_id=worker(g, core, base), device_id_type=MESH)

    @pl.when(half == core)
    def _():
        pl.semaphore_wait(barrier, 6)

    @pl.when(half != core)
    def _():
        pl.semaphore_wait(barrier, 8)


def spread_kernel(a_ref, b_ref, oa_ref, ob_ref, send_sem, recv_sem, local_sem):
    dp, mp, core, t = place()
    half, base = mp // 2, dp - core
    mine = lax.rem(mp, 2) * 2 + core
    greet_exchange(pltpu.get_barrier_semaphore())
    for u in (3, 2, 1, 0):
        pair = ((a_ref.at[pl.ds(u * 1024, 1024)], oa_ref.at[mine]), (b_ref.at[pl.ds(u * 512, 512)], ob_ref.at[mine]))
        for k, (src, dst) in enumerate(pair):
            @pl.when((half != core) | (t != u))
            def _():
                send(src, dst, send_sem.at[u, k], recv_sem.at[mine, k], chain_device(u, half, base))

            @pl.when((half == core) & (t == u))
            def _():
                pltpu.make_async_copy(src, dst, local_sem.at[k]).start()
    for u in range(4):
        for k, src in enumerate((a_ref.at[pl.ds(u * 1024, 1024)], b_ref.at[pl.ds(u * 512, 512)])):
            @pl.when((half != core) | (t != u))
            def _():
                pltpu.make_async_copy(src, src, send_sem.at[u, k]).wait()
    for g in range(4):
        for k, dst in enumerate((oa_ref.at[g], ob_ref.at[g])):
            @pl.when((half != core) | (mine != g))
            def _():
                pltpu.make_async_copy(dst, dst, recv_sem.at[g, k]).wait()

            @pl.when((half == core) & (mine == g))
            def _():
                pltpu.make_async_copy(dst, dst, local_sem.at[k]).wait()


def spread(a, b):
    return pl.pallas_call(
        spread_kernel,
        out_shape=[jax.ShapeDtypeStruct((4, 1024, C), BF16), jax.ShapeDtypeStruct((4, 512, C), BF16)],
        in_specs=[ANY, ANY],
        out_specs=[ANY, ANY],
        scratch_shapes=[DMA((4, 2)), DMA((4, 2)), DMA((2,))],
        compiler_params=pltpu.CompilerParams(collective_id=1, has_side_effects=True),
        name="spread",
    )(a, b)


def regroup_kernel(a_ref, b_ref, oa_ref, ob_ref, send_sem, recv_sem, local_sem):
    dp, mp, core, t = place()
    half, base = mp // 2, dp - core
    mine = lax.rem(mp, 2) * 2 + core
    greet_exchange(pltpu.get_barrier_semaphore())
    big = lambda u: oa_ref.at[pl.ds(u * 1024, 1024)]
    small = lambda u: ob_ref.at[pl.ds(u * 512, 512)]
    for n in range(4):
        g = lax.rem(n + 2 * core, 4)
        for k, (src, dst) in enumerate(((a_ref.at[g], big(t)), (b_ref.at[g], small(t)))):
            @pl.when((half != core) | (mine != g))
            def _():
                send(src, dst, send_sem.at[g, k], recv_sem.at[t, k], worker(g, core, base))

            @pl.when((half == core) & (mine == g))
            def _():
                pltpu.make_async_copy(src, dst, local_sem.at[k]).start()
    for g in range(4):
        for k, src in enumerate((a_ref.at[g], b_ref.at[g])):
            @pl.when((half != core) | (mine != g))
            def _():
                pltpu.make_async_copy(src, src, send_sem.at[g, k]).wait()
    for u in range(4):
        for k, dst in enumerate((big(u), small(u))):
            @pl.when((half != core) | (t != u))
            def _():
                pltpu.make_async_copy(dst, dst, recv_sem.at[u, k]).wait()

            @pl.when((half == core) & (t == u))
            def _():
                pltpu.make_async_copy(dst, dst, local_sem.at[k]).wait()


def regroup(a, b):
    return pl.pallas_call(
        regroup_kernel,
        out_shape=[jax.ShapeDtypeStruct((4096, C), BF16), jax.ShapeDtypeStruct((2048, C), BF16)],
        in_specs=[ANY, ANY],
        out_specs=[ANY, ANY],
        scratch_shapes=[DMA((4, 2)), DMA((4, 2)), DMA((2,))],
        compiler_params=pltpu.CompilerParams(collective_id=2, has_side_effects=True),
        name="regroup",
    )(a, b)


def settle_kernel(d0_ref, d1_ref, d2_ref, xs_in, w_ref, extra_in, mine_ref, out_ref, *rest):
    pieces_out, rest = rest[:9], rest[9:]
    (xs_ref, extra_ref, up_t, in_sem, heads_ref, grads_ref, stage, pair_in, chain_in, gw, gwl, h_in, z_in, z_out,
                  pair_recv, pair_send, chain_recv, chain_send, relay_send,
                  s_recv, s_send, c_recv, c_send, h_recv, h_send, z_recv, z_send, q_recv, q_send, out_sem) = rest
    dp, mp, core, t = place()
    base, spot = dp - core, lax.rem(dp, 8) // 2
    step = 1 - 2 * core
    partner, lower, upper = at(dp + step, mp), at(dp, mp - step), at(dp, mp + step)
    group = lax.rem(mp, 2) * 2 + core
    gives = core == lax.rem(mp, 2)
    quarter = lambda q: pl.ds(pl.multiple_of(q * QUARTER, QUARTER), QUARTER)
    share = lambda j, parity: grads_ref.at[2 * j + parity]

    later = [pltpu.make_async_copy(src, dst, in_sem.at[n]) for n, (src, dst) in enumerate(((xs_in, xs_ref), (extra_in, extra_ref)))]
    for copy in later:
        copy.start()
    greet(pltpu.get_barrier_semaphore(), True)

    grads_ref[2 * spot + core] = mine_ref[...]
    for rel in (1, 2, 3):
        send(mine_ref, share(spot, core), s_send.at[rel], s_recv.at[rel], at(mate(dp, rel), mp))

    def weight_gradients():
        later[0].wait()
        gw[...] = jnp.zeros_like(gw)

        def part(i, sums):
            rows = pl.ds(pl.multiple_of(i * SUB, SUB), SUB)
            x = xs_ref[rows, :]
            new = []
            for h, d_ref in enumerate((d0_ref, d1_ref, d2_ref)):
                d = d_ref[rows, :]
                gw[pl.ds(h * 256, 256), :] += dot(d, x, 0, 0)
                new.append(sums[h] + jnp.sum(d.astype(F32), axis=0, keepdims=True))
            return tuple(new)

        sums = lax.fori_loop(0, 4 * ROWS // SUB, part, tuple(jnp.zeros((1, 256), F32) for _ in range(3)))
        gwl[...] = gw[...].astype(BF16)
        for h in range(3):
            line = jnp.concatenate([sums[h], jnp.zeros((1, WIDTH - 256), F32)], axis=1)
            spare = h * 256 + (192 if h == 1 else 128)
            gwl[pl.ds(spare, 16), :] = jnp.concatenate([line, jnp.zeros((15, WIDTH), F32)], axis=0).astype(BF16)
        for rel in (1, 2, 3):
            send(gwl.at[quarter(spot ^ rel)], h_in.at[rel], h_send.at[rel], h_recv.at[rel], at(mate(dp, rel), mp))

    def plane_sum():
        for rel in (1, 2, 3):
            wait(h_in.at[rel], h_recv.at[rel])
        half_sum = gwl[quarter(spot), :].astype(F32)
        for rel in (1, 2, 3):
            half_sum += h_in[rel].astype(F32)
        z_out[...] = half_sum.astype(BF16)

        @pl.when(mp != group)
        def _():
            send(z_out, z_in.at[mp // 2], z_send, z_recv.at[mp // 2], at(dp, group))

    tt = jnp.minimum(t, 3 - t)
    for i in range(3):
        u = lax.rem(3 - i + tt, 4)
        for s in range(SUBS):
            rows = pl.ds(pl.multiple_of(u * ROWS + s * SUB, SUB), SUB)
            value = jnp.zeros((SUB, WIDTH), F32)
            for h, d_ref in enumerate((d0_ref, d1_ref, d2_ref)):
                value += jnp.dot(d_ref[rows, :], w_ref[pl.ds(h * 256, 256), :], preferred_element_type=F32)

            @pl.when(t >= 2)
            def _():
                stage[rows, :] = value.astype(BF16)
                send(stage.at[rows], pair_in.at[rows], pair_send.at[i, s], pair_recv.at[i, s], partner)

            @pl.when(t <= 1)
            def _():
                wait(pair_in.at[rows], pair_recv.at[i, s])
                here = value + pair_in[rows, :].astype(F32)
                if i == 0:
                    stage[rows, :] = here.astype(BF16)
                else:
                    @pl.when(t == 1)
                    def _():
                        wait(chain_in.at[rows], chain_recv.at[u, s])
                        stage[rows, :] = (here + chain_in[rows, :].astype(F32)).astype(BF16)

                    @pl.when(t == 0)
                    def _():
                        stage[rows, :] = here.astype(BF16)

                @pl.when((t == 0) | (i > 0))
                def _():
                    send(stage.at[rows], chain_in.at[rows], chain_send.at[i, s], chain_recv.at[u, s], upper)

                if i == 0:
                    @pl.when(t == 1)
                    def _():
                        send(stage.at[rows], chain_in.at[rows], chain_send.at[i, s], chain_recv.at[u, s], lower)

        if i < 2:
            @pl.when(t == 1)
            def _():
                (weight_gradients, plane_sum)[i]()

    @pl.when(t != 1)
    def _():
        weight_gradients()

    for rel in (1, 2, 3):
        wait(share(spot ^ rel, core), s_recv.at[rel])
    for j in range(4):
        send(share(j, core), share(j, core), c_send.at[j], c_recv.at[j], partner)

    @pl.when(t == 2)
    def _():
        for s in range(SUBS):
            rows = pl.ds(3 * ROWS + s * SUB, SUB)
            wait(chain_in.at[rows], chain_recv.at[3, s])
            send(chain_in.at[rows], chain_in.at[rows], relay_send.at[s], chain_recv.at[3, s], upper)
            if s == 0:
                plane_sum()

    @pl.when((t == 0) | (t == 3))
    def _():
        plane_sum()

    for s in range(SUBS):
        rows = pl.ds(pl.multiple_of(tt * ROWS + s * SUB, SUB), SUB)
        cut = pl.ds(s * SUB, SUB)
        value = jnp.zeros((SUB, WIDTH), F32)
        for h, d_ref in enumerate((d0_ref, d1_ref, d2_ref)):
            value += jnp.dot(d_ref[rows, :], w_ref[pl.ds(h * 256, 256), :], preferred_element_type=F32)

        @pl.when(t >= 2)
        def _():
            stage[rows, :] = value.astype(BF16)
            send(stage.at[rows], pair_in.at[rows], pair_send.at[3, s], pair_recv.at[3, s], partner)

        @pl.when(t <= 1)
        def _():
            stage[rows, :] = value.astype(BF16)

    @pl.when(gives)
    def _():
        both = jnp.zeros((QUARTER, WIDTH), F32)
        for far in (0, 1):
            source = mp // 2 + 2 * far

            @pl.when(source == mp)
            def _():
                z_in[far] = z_out[...]

            @pl.when(source != mp)
            def _():
                wait(z_in.at[far], z_recv.at[far])

            both += z_in[far].astype(F32)
        heads_ref[quarter(spot), :] = both.astype(BF16)
        mine = heads_ref.at[quarter(spot)]
        send(mine, mine, q_send.at[0], q_recv.at[spot], partner)
        for rel in (1, 2, 3):
            send(mine, mine, q_send.at[rel], q_recv.at[spot], at(mate(dp, rel), mp))
            send(mine, mine, q_send.at[rel + 3], q_recv.at[spot], at(mate(dp, rel) + step, mp))

    for j in range(4):
        wait(share(j, 1 - core), c_recv.at[j])
    up_t[...] = grads_ref[:, pl.ds(0, 96), :].reshape(WIDTH, WIDTH).T
    copies = [pltpu.make_async_copy(up_t, pieces_out[3], out_sem.at[1])]
    for i in range(8):
        for n, (first, rows) in enumerate(((0, 96), (96, 96), (192, 32), (224, 16))):
            if n == 0 or (n == 2 and i >= 6):
                continue
            dst = pieces_out[3 + n].at[pl.ds(i * rows, rows)]
            copies.append(pltpu.make_async_copy(grads_ref.at[i, pl.ds(first, rows)], dst, out_sem.at[20 + 4 * i + n]))
    copies.append(pltpu.make_async_copy(grads_ref.at[6, pl.ds(192, 16)], pieces_out[8], out_sem.at[0]))
    early = len(copies)
    for copy in copies:
        copy.start()
    later[1].wait()

    for s in range(SUBS):
        cut = pl.ds(s * SUB, SUB)
        rows = pl.ds(pl.multiple_of(t * ROWS + s * SUB, SUB), SUB)
        wait(chain_in.at[rows], chain_recv.at[t, s])
        value = extra_ref[cut, :] + chain_in[rows, :].astype(F32)

        @pl.when(t <= 1)
        def _():
            wait(pair_in.at[rows], pair_recv.at[3, s])
            out_ref[cut, :] = (value + stage[rows, :].astype(F32) + pair_in[rows, :].astype(F32)).astype(BF16)

        @pl.when(t >= 2)
        def _():
            out_ref[cut, :] = value.astype(BF16)

    for q in range(4):
        @pl.when(jnp.logical_not(gives) | (spot != q))
        def _():
            wait(heads_ref.at[quarter(q)], q_recv.at[q])
    for h in range(3):
        for n, where in enumerate((0, 2, 1) if h == 1 else (1, 3, 0)):
            src = heads_ref.at[pl.ds((4 * h + where) * HD, HD)]
            copies.append(pltpu.make_async_copy(src, pieces_out[n].at[pl.ds(h * HD, HD)], out_sem.at[8 + 3 * h + n]))
        src = heads_ref.at[pl.ds(h * 256 + (192 if h == 1 else 128), 16)]
        copies.append(pltpu.make_async_copy(src, pieces_out[7].at[h], out_sem.at[17 + h]))
    for copy in copies[early:]:
        copy.start()

    for s in range(SUBS):
        piece = stage.at[pl.ds(s * SUB, SUB)]

        @pl.when(t >= 2)
        def _():
            for i in range(4):
                wait(piece, pair_send.at[i, s])

        @pl.when(t <= 1)
        def _():
            for i in range(3):
                wait(piece, chain_send.at[i, s])

        @pl.when(t == 2)
        def _():
            wait(piece, relay_send.at[s])
    for rel in (1, 2, 3):
        wait(mine_ref, s_send.at[rel])
        wait(z_out, h_send.at[rel])
    for j in range(4):
        wait(mine_ref, c_send.at[j])

    @pl.when(mp != group)
    def _():
        wait(z_out, z_send)

    @pl.when(gives)
    def _():
        for k in range(7):
            wait(z_out, q_send.at[k])

    for copy in copies:
        copy.wait()


def settle(d0, d1, d2, xs, w, extra, mine):
    return pl.pallas_call(
        settle_kernel,
        out_shape=[sds((ROWS, WIDTH), BF16)] + [sds((rows, WIDTH), BF16) for rows in (192, 192, 192, 768, 768, 192, 128)]
        + [sds((3, 16, WIDTH), BF16), sds((16, WIDTH), BF16)],
        in_specs=[VM, VM, VM, ANY, VM, ANY, VM],
        out_specs=[VM] + [ANY] * 9,
        scratch_shapes=[VMEM((4 * ROWS, WIDTH), BF16), VMEM((ROWS, WIDTH), F32), VMEM((WIDTH, WIDTH), BF16), DMA((2,)),
                        VMEM((WIDTH, WIDTH), BF16), VMEM((8, SHARE_ALL, WIDTH), BF16)] + [VMEM((4 * ROWS, WIDTH), BF16)] * 3 + [
            VMEM((WIDTH, WIDTH), F32), VMEM((WIDTH, WIDTH), BF16), VMEM((4, QUARTER, WIDTH), BF16), VMEM((2, QUARTER, WIDTH), BF16),
            VMEM((QUARTER, WIDTH), BF16),
            DMA((4, SUBS)), DMA((4, SUBS)), DMA((4, SUBS)), DMA((3, SUBS)), DMA((SUBS,)),
            DMA((4,)), DMA((4,)), DMA((4,)), DMA((4,)), DMA((4,)), DMA((4,)), DMA((2,)), DMA, DMA((4,)), DMA((7,)), DMA((52,)),
        ],
        compiler_params=pltpu.CompilerParams(collective_id=3, has_side_effects=True, vmem_limit_bytes=60 << 20),
        name="settle",
    )(d0, d1, d2, xs, w, extra, mine)


EPS = 1e-12
CHUNK = 512
FF_MODEL = 768


def gelu_and_slope(v):
    size = jnp.abs(v)
    u = 1.0 / (1.0 + (0.3275911 * 0.7071067811865476) * size)
    bell = jnp.exp2(v * v * -0.7213475204444817 - 1.3257480647361595)
    poly = u * (0.3193815306 + u * (-0.3565637784 + u * (1.7814779345 + u * (-1.8212559786 + u * 1.3302744294))))
    tail = poly * bell
    cdf = jnp.where(v < 0, tail, 1.0 - tail)
    return v * cdf, cdf + v * bell


def row_mean(v):
    return jnp.sum(v, axis=-1, keepdims=True) * (1.0 / FF_MODEL)


def ffn_kernel(c01_ref, c2_ref, tok_in, cot_in, vec_ref, near_ref, a_ref, b_ref,
               out_o, res_o, g01_o, g2_o, keep_ref, next_ref, give_ref, keep_tail_ref, give_tail_ref,
               tok_ref, cot_ref, out_ref, res_ref, g01_ref, g2_ref, in_sem, early_sem, w, wout, ctx, x, gf, act, slope, zhat, acc, rstd, cols, recv, recv2, tail, tail_in,
               o_local, o_send, o_recv, f_send, f_recv, w_local, w_send, w_recv, d_send, d_recv,
               g_send, g_recv, m_send, m_recv, t_send, t_recv, out_sem, tail_sem):
    dp, mp, core, t = place()
    step = 1 - 2 * core
    partner = at(dp + step, mp)
    spot = lax.rem(dp, 8) // 2
    one, two = jnp.where(core == 0, 1, 2), jnp.where(core == 0, 2, 1)
    mate_a, mate_b = at(dp + 2 * ((spot ^ one) - spot), mp), at(dp + 2 * ((spot ^ two) - spot), mp)
    shard = lambda k: lax.rem(mp - k + 4, 4)
    later = [pltpu.make_async_copy(src, dst, in_sem.at[n]) for n, (src, dst) in enumerate(((tok_in, tok_ref), (cot_in, cot_ref)))]
    for copy in later:
        copy.start()
    results = [pltpu.make_async_copy(src, dst, early_sem.at[n])
               for n, (src, dst) in enumerate(((out_ref, out_o), (res_ref, res_o), (g01_ref, g01_o), (g2_ref, g2_o)))]
    barrier = pltpu.get_barrier_semaphore()
    for device in (partner, mate_a, mate_b):
        signal(barrier, device)
    pl.semaphore_wait(barrier, 3)

    def out_rows(m, i):
        first = jnp.where(i < 4, m * C + 32 * i, 4 * C + m * HD + 32 * (i - 4))
        return wout.at[pl.ds(pl.multiple_of(first, 32), 32)]

    sources = ((0, near_ref), (one, a_ref), (two, b_ref))
    far = spot ^ 3
    for k in range(4):
        @pl.when(spot ^ one < 3)
        def _():
            send(a_ref.at[k, pl.ds(SHARE, 32)], out_rows(shard(k), 2 * (spot ^ one) + core), f_send.at[k], f_recv.at[k], mate_b)
    for rel, ref in sources:
        j = spot ^ rel
        for k in range(4):
            src = ref.at[k, pl.ds(SHARE, 32)]

            @pl.when(j < 3)
            def _():
                pltpu.make_async_copy(src, out_rows(shard(k), 2 * j + core), o_local.at[j, k]).start()
                send(src, out_rows(shard(k), 2 * j + core), o_send.at[j, k], o_recv.at[j, k], partner)

    body = pl.ds(0, SHARE)
    for k in range(4):
        send(a_ref.at[k, body], w.at[2 * (spot ^ one) + core, shard(k)], d_send.at[k], d_recv.at[k], mate_b)
    for rel, ref in sources:
        for k in range(4):
            mine = w.at[2 * (spot ^ rel) + core, shard(k)]
            pltpu.make_async_copy(ref.at[k, body], mine, w_local.at[rel, k]).start()
            send(ref.at[k, body], mine, w_send.at[rel, k], w_recv.at[rel, k], partner)

    lane = lax.broadcasted_iota(jnp.int32, (1, C), 1)
    for g in range(4):
        ctx[:, pl.ds(g * C, C)] = c01_ref[g]
    for g in (0, 2):
        a, b = c2_ref[g].astype(F32), c2_ref[g + 1].astype(F32)
        col = pl.ds(4 * C + g * HD, C)
        ctx[pl.ds(0, 512), col] = jnp.where(lane < HD, a, pltpu.roll(b, HD, 1)).astype(BF16)
        ctx[pl.ds(512, 512), col] = jnp.where(lane < HD, pltpu.roll(a, HD, 1), b).astype(BF16)
    cols[...] = jnp.zeros_like(cols)
    b_out, gain1, bias1, b_down, gain2, bias2 = (vec_ref[pl.ds(i, 1), :] for i in range(6))
    row_chunks = [pl.ds(r * CHUNK, CHUNK) for r in range(1024 // CHUNK)]

    part = wout.at[pl.ds(0, 32)]
    for k in range(4):
        @pl.when(far < 3)
        def _():
            mine = out_rows(shard(k), 2 * far + core)
            wait(mine, f_recv.at[k])
            send(mine, mine, o_send.at[far, k], o_recv.at[far, k], partner)
    for j in range(3):
        for k in range(4):
            @pl.when(far != j)
            def _():
                wait(part, o_local.at[j, k])

            wait(part, o_recv.at[j, k])

    later[0].wait()
    for rows in row_chunks:
        h = jnp.dot(ctx[rows, :], wout[...], preferred_element_type=F32) + tok_ref[rows, :].astype(F32) + b_out
        h = h - row_mean(h)
        scale = lax.rsqrt(row_mean(h * h) + EPS)
        rstd[rows, :] = scale
        h = h * scale
        zhat[rows, :] = h
        first = h * gain1 + bias1
        acc[rows, :] = first + b_down
        x[rows, :] = first.astype(BF16)

    whole = w.at[0, 0]
    up_pair = lambda j: w[pl.ds(2 * j, 2), :, pl.ds(0, 96), :].reshape(768, FF_MODEL)
    down_pair = lambda j: w[pl.ds(2 * j, 2), :, pl.ds(96, 96), :].reshape(768, FF_MODEL)

    def up(j, rel, rows):
        bias = [jnp.sum(w[2 * j + f, :, pl.ds(192, 16), :].astype(F32), axis=0)[0:1, :384] for f in range(2)]
        pre = dot(x[rows, :], up_pair(j), 1, 1) + jnp.concatenate(bias, axis=1)
        value, grad = gelu_and_slope(pre)
        act[rel, rows, :] = value.astype(BF16)
        slope[rel, rows, :] = grad.astype(BF16)

    def down(j, rel, rows):
        acc[rows, :] += jnp.dot(act[rel, rows, :], down_pair(j), preferred_element_type=F32)

    for rel in range(4):
        j = spot ^ rel
        if rel == 2:
            for k in range(4):
                mine = w.at[2 * (spot ^ 3) + core, shard(k)]
                wait(mine, d_recv.at[k])
                send(mine, mine, w_send.at[3, k], w_recv.at[3, k], partner)
        for k in range(4):
            if rel < 3:
                wait(whole, w_local.at[rel, k])
            wait(whole, w_recv.at[rel, k])
        before = None
        for rows in row_chunks:
            up(j, rel, rows)
            if before is not None:
                down(j, rel, before)
            before = rows
        down(j, rel, before)

    later[1].wait()
    for rows in row_chunks:
        z = acc[rows, :]
        z = z - row_mean(z)
        scale = lax.rsqrt(row_mean(z * z) + EPS)
        z = z * scale
        out_ref[rows, :] = (z * gain2 + bias2).astype(BF16)
        cot = cot_ref[rows, :].astype(F32)
        dz = cot * gain2
        gs = scale * (dz - row_mean(dz) - z * row_mean(dz * z))
        cols[pl.ds(2, 1), :] += jnp.sum(cot * z, axis=0, keepdims=True)
        cols[pl.ds(3, 1), :] += jnp.sum(cot, axis=0, keepdims=True)
        cols[pl.ds(5, 1), :] += jnp.sum(gs, axis=0, keepdims=True)
        acc[rows, :] = gs
        gf[rows, :] = gs.astype(BF16)

    results[0].start()

    for rel in range(4):
        for k in range(4):
            wait(whole, w_send.at[rel, k])
    for k in range(4):
        wait(whole, d_send.at[k])

    grads = pl.ds(0, 192)
    order = (3, 1, 2, 0)
    place_of = {rel: q for q, rel in enumerate(order)}

    def add_cores(rel):
        q, i = place_of[rel], 2 * (spot ^ rel) + core
        wait(recv.at[q], g_recv.at[q])
        for m in range(4):
            recv[q, m] = (recv[q, m].astype(F32) + w[i, m, grads, :].astype(F32)).astype(BF16)
        if rel == 3:
            send(recv.at[q], recv2, m_send, m_recv, mate_a)
        elif rel == 0:
            pltpu.make_async_copy(recv.at[q], keep_ref, out_sem.at[0]).start()
        else:
            @pl.when(one == rel)
            def _():
                pltpu.make_async_copy(recv.at[q], next_ref, out_sem.at[1]).start()

    for q, rel in enumerate(order):
        j = spot ^ rel
        for rows in row_chunks:
            ga = dot(gf[rows, :], down_pair(j), 1, 1)
            slope[rel, rows, :] = (ga * slope[rel, rows, :].astype(F32)).astype(BF16)
            acc[rows, :] += jnp.dot(slope[rel, rows, :], up_pair(j), preferred_element_type=F32)
        for f in range(2):
            cut = pl.ds(f * 384, 384)
            gp = slope[rel, :, cut]
            w[2 * j + f, :, pl.ds(0, 96), :] = dot(gp, x[...], 0, 0).astype(BF16).reshape(4, 96, FF_MODEL)
            w[2 * j + f, :, pl.ds(96, 96), :] = dot(act[rel, :, cut], gf[...], 0, 0).astype(BF16).reshape(4, 96, FF_MODEL)
            cols[pl.ds(8 + 2 * j + f, 1), pl.ds(0, 384)] = jnp.sum(gp.astype(F32), axis=0, keepdims=True)
        send(w.at[2 * j + 1 - core, :, grads], recv.at[q], g_send.at[q], g_recv.at[q], partner)
        if q:
            add_cores(order[q - 1])

    ctx_grad = x.at[:, pl.ds(0, 2 * C)]
    for rows in row_chunks:
        grad = acc[rows, :]
        z = zhat[rows, :]
        dz = grad * gain1
        gr = rstd[rows, :] * (dz - row_mean(dz) - z * row_mean(dz * z))
        cols[pl.ds(0, 1), :] += jnp.sum(grad * z, axis=0, keepdims=True)
        cols[pl.ds(1, 1), :] += jnp.sum(grad, axis=0, keepdims=True)
        cols[pl.ds(4, 1), :] += jnp.sum(gr, axis=0, keepdims=True)
        res_ref[rows, :] = gr
        low = gr.astype(BF16)
        gf[rows, :] = low
        gc = dot(low, wout[...], 1, 1).astype(BF16)
        for g in range(4):
            g01_ref[g, rows, :] = gc[:, g * C : g * C + C]
        ctx_grad[rows, :] = gc[:, 4 * C :]
    for g in (0, 2):
        top = ctx_grad[pl.ds(0, 512), pl.ds(g * HD, C)].astype(F32)
        low = ctx_grad[pl.ds(512, 512), pl.ds(g * HD, C)].astype(F32)
        g2_ref[g] = jnp.where(lane < HD, top, pltpu.roll(low, HD, 1)).astype(BF16)
        g2_ref[g + 1] = jnp.where(lane < HD, pltpu.roll(top, HD, 1), low).astype(BF16)

    for copy in results[1:]:
        copy.start()

    for n in range(3):
        got = dot(ctx[:, pl.ds(n * 256, 256)], gf[...], 0, 0).astype(BF16)
        for i in range(8):
            piece = got[i * 32 : i * 32 + 32, :]
            m, share = (2 * n + i // 4, i % 4) if n < 2 else (i // 2, 4 + i % 2)
            tail[share % 2, share // 2, m, pl.ds(0, 32), :] = piece
    vectors = jnp.concatenate([cols[pl.ds(0, 6), :], jnp.zeros((26, FF_MODEL), F32)], axis=0).astype(BF16)
    for i in range(8):
        line = jnp.concatenate([cols[pl.ds(8 + i, 1), :], jnp.zeros((15, FF_MODEL), F32)], axis=0).astype(BF16)
        for m in range(4):
            tail[i % 2, i // 2, m, pl.ds(32, 16), :] = line
            if i >= 6:
                tail[i % 2, i // 2, m, pl.ds(0, 32), :] = vectors if i == 6 else jnp.zeros((32, FF_MODEL), BF16)
    send(tail.at[1 - core], tail_in, t_send, t_recv, partner)
    add_cores(0)

    wait(recv2, m_recv)
    for rel in (1, 2):
        @pl.when(two == rel)
        def _():
            for m in range(4):
                recv2[m] = (recv2[m].astype(F32) + recv[place_of[rel], m].astype(F32)).astype(BF16)
    give = pltpu.make_async_copy(recv2, give_ref, out_sem.at[2])
    give.start()
    wait(tail_in, t_recv)
    for rel in range(4):
        j = spot ^ rel
        for m in range(4):
            tail_in[j, m] = (tail_in[j, m].astype(F32) + tail[core, j, m].astype(F32)).astype(BF16)
        along, across = jnp.where(core == 0, rel % 2, rel // 2), jnp.where(core == 0, rel // 2, rel % 2)
        for side, ref in enumerate((keep_tail_ref, give_tail_ref)):
            @pl.when(along == side)
            def _():
                pltpu.make_async_copy(tail_in.at[j], ref.at[across], tail_sem.at[rel]).start()
    give.wait()
    for copy in results:
        copy.wait()
    wait(recv2, out_sem.at[0])
    wait(recv2, out_sem.at[1])
    for rel in range(4):
        wait(tail_in.at[0], tail_sem.at[rel])
    for q in range(4):
        wait(recv.at[q], g_send.at[q])
    wait(recv2, m_send)
    wait(tail_in, t_send)
    for k in range(4):
        @pl.when(spot ^ one < 3)
        def _():
            wait(part, f_send.at[k])

        for j in range(3):
            wait(part, o_send.at[j, k])


def ffn(c01, c2, tokens, cot, vecs, near, a, b):
    main, rest = sds((4, 192, WIDTH), BF16), sds((2, 4, 48, WIDTH), BF16)
    rows = lambda dtype: VMEM((1024, WIDTH), dtype)
    four = lambda *shape: VMEM((4,) + shape, BF16)
    return pl.pallas_call(
        ffn_kernel,
        out_shape=[sds((1024, WIDTH), BF16), sds((1024, WIDTH), F32), sds((4, 1024, C), BF16), sds((4, 512, C), BF16), main, main, main, rest, rest],
        in_specs=[VM, VM, ANY, ANY, VM] + [ANY] * 3,
        out_specs=[ANY] * 9,
        scratch_shapes=[
            rows(BF16), rows(BF16), rows(BF16), rows(F32), four(1024, C), four(512, C), DMA((2,)), DMA((4,)),
            VMEM((8, 4, SHARE, WIDTH), BF16), VMEM((WIDTH, WIDTH), BF16), rows(BF16), rows(BF16), rows(BF16), four(1024, WIDTH), four(1024, WIDTH),
            rows(F32), rows(F32), VMEM((1024, 1), F32), VMEM((16, WIDTH), F32), four(4, 192, WIDTH), four(192, WIDTH),
            VMEM((2, 4, 4, 48, WIDTH), BF16), four(4, 48, WIDTH),
        ] + [DMA((4, 4))] * 3 + [DMA((4,))] * 2 + [DMA((4, 4))] * 3 + [DMA((4,))] * 4 + [DMA] * 4 + [DMA((3,)), DMA((4,))],
        compiler_params=pltpu.CompilerParams(collective_id=4, has_side_effects=True, vmem_limit_bytes=63 << 20),
        name="ffn",
    )(c01, c2, tokens, cot, vecs, near, a, b)


def swap(value, even_bits, odd_bits, n_dp):
    return lax.ppermute(value, "dp", [(d, d ^ (odd_bits if d % 2 else even_bits)) for d in range(n_dp)])


def pick(value, index, axis):
    return lax.dynamic_index_in_dim(value, index, axis, keepdims=False)


def total(a, b):
    return (a.astype(F32) + b.astype(F32)).astype(BF16)


def tie(*values):
    return lax.optimization_barrier(values)


def body(n_dp, tokens, w_query, b_query, w_key, w_value, b_value, w_out, b_out, norm1_gain, norm1_bias, w_up, b_up, w_down,
         b_down, norm2_gain, norm2_bias, key_mask, cluster_order, cotangent):
    dp, mp, core, t = place()
    ring = lambda k: [(z, (z + k) % 4) for z in range(4)]

    order = 2 * jnp.where(core == 1, cluster_order ^ 3072, cluster_order).reshape(3 * L)
    bq, bv, bz = b_query.reshape(3, HD), b_value.reshape(3, HD), jnp.zeros((C,), F32)
    b_heads = jnp.stack([jnp.concatenate([bq[h], bv[h], bz] if h == 1 else [bv[h], bq[h], bz]) for h in range(3)])
    b_heads = jnp.concatenate([b_heads, jnp.zeros((5, 256), F32)])
    units = lax.dynamic_slice(b_up, (96 * (dp % 8),), (96,)).reshape(1, 96)
    bias_row = lax.dynamic_update_slice(jnp.zeros((16, WIDTH), BF16), units, (0, 96 * mp))

    xs, qkv, w_heads, order, mask, share = collect(
        tokens, w_query.T, w_key.T, w_value.T, b_heads, order, key_mask, w_up, w_down, w_out, bias_row
    )
    qkv, share = tie(qkv, share)
    shares = [share] + [lax.ppermute(share, "mp", ring(i)) for i in (1, 2, 3)]
    c01, ts01, probs01 = attend(0, order, mask, qkv)
    c01, qkv = tie(c01, qkv)
    c2, ts2, probs2 = attend(2, order, mask, qkv)
    c2, *shares = tie(c2, *shares)
    near = jnp.stack(shares)
    along, across = swap(near, 2, 4, n_dp), swap(near, 4, 2, n_dp)
    c01, c2 = spread(c01, c2)

    vecs = jnp.stack([b_out, norm1_gain, norm1_bias, b_down, norm2_gain, norm2_bias, b_out, b_out])
    layer_out, grad_residual, g01, g2, keep, nearer, give, keep_tail, give_tail = ffn(
        c01, c2, tokens, cotangent, vecs, near, along, across
    )

    got, got_nearer, got_tail = swap(give, 4, 2, n_dp), swap(nearer, 2, 4, n_dp), swap(give_tail, 2, 4, n_dp)
    g01, g2 = regroup(g01, g2)
    g01, keep, got, got_nearer, keep_tail, got_tail = tie(g01, keep, got, got_nearer, keep_tail, got_tail)
    groups = [1 << bit for bit in range(3, n_dp.bit_length() - 1)]

    def shard_sums(sums):
        for bits in groups:
            sums = total(sums, swap(sums, bits, bits, n_dp))
        return [pick(sums, mp, 0)] + [lax.ppermute(pick(sums, (mp + k) % 4, 0), "mp", ring(k)) for k in (1, 2, 3)]

    keep = (keep.astype(F32) + got_nearer.astype(F32) + got.astype(F32)).astype(BF16)
    keep_tail, give_tail = total(keep_tail[0], got_tail[0]), total(keep_tail[1], got_tail[1])
    got_tail = swap(give_tail, 4, 2, n_dp)
    d0 = attend_back(0, order, g01, ts01, probs01)
    d0, order, keep, keep_tail, got_tail = tie(d0, order, keep, keep_tail, got_tail)
    parts = shard_sums(jnp.concatenate([keep, total(keep_tail, got_tail)], axis=1))
    d1 = attend_back(1, order, g01, ts01, probs01)
    d2 = attend_back(2, order, g2, ts2, probs2)
    d2, *parts = tie(d2, *parts)
    mine = sum(p.astype(F32) for p in parts).astype(BF16)
    grad_tokens, *sums = settle(d0, d1, d2, xs, w_heads, grad_residual, mine)
    hq, hk, hv, g_up, g_down, g_out, units, spare, vectors = (s.astype(F32) for s in sums)
    for bits in groups:
        hq, hk, hv, spare = (s + swap(s, bits, bits, n_dp) for s in (hq, hk, hv, spare))
    sums_of = lambda where: jnp.concatenate([spare[h, 0, where[h] : where[h] + HD] for h in range(3)])
    g_b_up = lax.dynamic_slice(units.reshape(8, 16, WIDTH)[:, 0], (0, 96 * mp), (8, 96)).reshape(WIDTH)
    return (
        layer_out,
        grad_tokens,
        hq.T,
        sums_of((HD, 0, HD)),
        hk.T,
        hv.T,
        sums_of((0, HD, 0)),
        g_out,
        vectors[4],
        vectors[0],
        vectors[1],
        g_up,
        g_b_up,
        g_down,
        vectors[5],
        vectors[2],
        vectors[3],
    )


def solution(mesh):
    return jax.shard_map(
        functools.partial(body, mesh.shape["dp"]),
        mesh=mesh,
        in_specs=(
            P(("dp", "mp"), None), P(None, "mp"), P("mp"), P(None, "mp"), P(None, "mp"), P("mp"), P("mp", None), P(), P(), P(),
            P(None, "mp"), P("mp"), P("mp", None), P(), P(), P(), P("dp", None), P("dp", "mp", None), P(("dp", "mp"), None),
        ),
        out_specs=(
            P(("dp", "mp"), None), P(("dp", "mp"), None), P(None, "mp"), P("mp"), P(None, "mp"), P(None, "mp"), P("mp"),
            P("mp", None), P(), P(), P(), P(None, "mp"), P("mp"), P("mp", None), P(), P(), P(),
        ),
        check_vma=False,
    )
```
